32 devices in a mesh: dp: 16 (over z, y, x), tensor: 2 (over core).
Axes of the slice: x: 2, y: 2, z: 4, core: 2. Of those that a mesh axis runs over, the one named last changes fastest.
Arguments:
- tokens: bfloat16 [16384, 768], P('dp'), may hold values from -6 to 6
- positions: int32 [16384], P('dp'), may hold values from 0 to 1023, as said below
- norm_gain: float32 [2, 2, 768], replicated, may hold values from 0.25 to 1.75
- norm_shift: float32 [2, 2, 768], replicated, may hold values from -1.8 to 1.8
- heads_weight: bfloat16 [2, 3, 768, 768], P(None, None, None, 'tensor'), may hold values from -0.21875 to 0.21875
- offsets: float32 [2, 2, 768], P(None, None, 'tensor'), may hold values from -3 to 3
- merge_weight: bfloat16 [2, 768, 768], P(None, 'tensor'), may hold values from -0.875 to 0.875
- branch_bias: float32 [2, 2, 768], replicated, may hold values from -3 to 3
- expand_weight: bfloat16 [2, 768, 3072], P(None, None, 'tensor'), may hold values from -0.21875 to 0.21875
- hidden_bias: float32 [2, 3072], P(None, 'tensor'), may hold values from -3 to 3
- shrink_weight: bfloat16 [2, 3072, 768], P(None, 'tensor'), may hold values from -0.109375 to 0.109375
- cotangent: bfloat16 [16384, 768], P('dp'), may hold values from -6 to 6
Outputs:
- output: bfloat16 [16384, 768], P('dp')
- grad_tokens: bfloat16 [16384, 768], P('dp')
- grad_gain: float32 [2, 2, 768], replicated
- grad_shift: float32 [2, 2, 768], replicated
- grad_heads: float32 [2, 3, 768, 768], P(None, None, None, 'tensor')
- grad_offsets: float32 [2, 2, 768], P(None, None, 'tensor')
- grad_merge: float32 [2, 768, 768], P(None, 'tensor')
- grad_branch: float32 [2, 2, 768], replicated
- grad_expand: float32 [2, 768, 3072], P(None, None, 'tensor')
- grad_hidden: float32 [2, 3072], P(None, 'tensor')
- grad_shrink: float32 [2, 3072, 768], P(None, 'tensor')
The draws below stay inside these ranges and needn't reach their ends.
Inputs may be any that keep to these rules, and one draw needn't show every extreme that they name: `positions`: each sequence of 1024 tokens is packed documents: a value counts up by one from 0 at each document's first token; sequence 0 is a single document.
All inputs are finite; a program needn't handle non-finite values.
Results may differ from the reference program's by a relative error of at most 0.018.
Values sent between devices are 32-bit elements; how exact they have to be, the bound alone decides.
A program may use at most 256 MiB of HBM per device.

```python
from functools import partial
import jax
import jax.numpy as jnp
from jax import lax

HEADS = 12
HEAD_DIM = 64
FF = 3072
LEN = 1024
LAYERS = 2
D = 768
TOKENS = 16384


def draw_positions(key, part):
    sequences = TOKENS // LEN
    row_index = jnp.arange(LEN, dtype=jnp.int32)
    starts = jax.random.randint(key, (sequences, LEN), 0, LEN // 4) == 0
    starts = starts.at[:, 0].set(True)
    starts = starts.at[0, :].set(row_index == 0)
    latest = lax.cummax(jnp.where(starts, row_index[None, :], 0), axis=1)
    return (row_index[None, :] - latest).reshape(-1).astype(jnp.int32)


def block_levels(own_key, extent, cuts, low, high):
    factor_of = 1.0
    for axis_at, blocks in cuts:
        heights = jax.random.uniform(jax.random.fold_in(jax.random.fold_in(own_key, 6), axis_at), (blocks,), jnp.float32, low / len(cuts), high / len(cuts))
        factor_of = factor_of * jnp.repeat(jnp.exp(heights), extent[axis_at] // blocks).reshape((-1,) + (1,) * (len(extent) - 1 - axis_at))
    return factor_of


def gaussian(key, dims, scale, limit, cuts=(), kind=jnp.bfloat16):
    values = jax.random.normal(key, dims, jnp.float32) * scale
    if len(cuts) > 0:
        values = block_levels(key, dims, cuts, -0.22, 0.18) * values
    return jnp.clip(values, min=-limit, max=limit).astype(kind)


def setup_inputs(seed: int = 0) -> dict:
    key_of = jax.random.split(jax.random.key(seed), 13)
    return {
        "tokens": gaussian(key_of[0], (TOKENS, D), 1.0, 6.0, ((0, 16),)),
        "positions": draw_positions(jax.random.fold_in(key_of[12], 71), 0),
        "norm_gain": jnp.clip(1.0 + 0.15 * jax.random.normal(key_of[2], (LAYERS, 2, D), jnp.float32), 0.25, 1.75),
        "norm_shift": gaussian(key_of[3], (LAYERS, 2, D), 0.3, 1.8, (), jnp.float32),
        "heads_weight": gaussian(key_of[4], (LAYERS, 3, D, D), D ** -0.5, 0.21875, ((3, 2),)),
        "offsets": gaussian(key_of[5], (LAYERS, 2, D), 0.5, 3.0, ((2, 2),), jnp.float32),
        "merge_weight": gaussian(key_of[6], (LAYERS, D, D), (D // 16) ** -0.5, 0.875, ((1, 2),)),
        "branch_bias": gaussian(key_of[7], (LAYERS, 2, D), 0.5, 3.0, (), jnp.float32),
        "expand_weight": gaussian(key_of[8], (LAYERS, D, FF), D ** -0.5, 0.21875, ((2, 2),)),
        "hidden_bias": gaussian(key_of[9], (LAYERS, FF), 0.5, 3.0, ((1, 2),), jnp.float32),
        "shrink_weight": gaussian(key_of[10], (LAYERS, FF, D), FF ** -0.5, 0.109375, ((1, 2),)),
        "cotangent": gaussian(key_of[11], (TOKENS, D), 1.0, 6.0, ((0, 16),)),
    }


@jax.custom_vjp
def low(v):
    return lax.optimization_barrier(v.astype(jnp.bfloat16)).astype(jnp.float32)

@jax.custom_vjp
def low_back(v):
    return v

def low_keep(v):
    return (low(v), None)

def low_pass(kept, grad):
    return (grad,)

def back_keep(v):
    return (v, None)

def back_low(kept, grad):
    return (low(grad),)
low.defvjp(low_keep, low_pass)
low_back.defvjp(back_keep, back_low)
exact_mode = lax.Precision.HIGHEST

def matmul(left, right):
    return jnp.dot(left, right, precision=exact_mode)

def layer_norm(stream, gain_row, shift_row):
    centre = stream - lax.optimization_barrier(jnp.mean(stream, axis=-1, keepdims=True))
    spread = lax.optimization_barrier(jnp.mean(centre * centre, axis=-1, keepdims=True))
    return centre * lax.rsqrt(spread + 1e-05) * gain_row + shift_row

def gelu_tanh(values):
    return 0.5 * values * (1.0 + jnp.tanh(0.7978845608028654 * (values + 0.044715 * values * values * values)))

def attention(query_rows, key_rows, value_rows, offsets_row):
    scores = jnp.einsum('qhd,khd->hqk', query_rows.reshape(LEN, HEADS, HEAD_DIM), key_rows.reshape(LEN, HEADS, HEAD_DIM), precision=exact_mode) * 0.125
    scores = low_back(scores)
    row_index = jnp.arange(LEN, dtype=jnp.int32)
    allowed = (row_index[None, :] <= row_index[:, None]) & (row_index[None, :] >= (row_index - offsets_row)[:, None])
    scores = jnp.where(allowed[None], scores, -1e+30)
    highest = lax.optimization_barrier(jnp.max(scores, axis=-1, keepdims=True))
    weights = jnp.exp(scores - highest)
    chances = weights / lax.optimization_barrier(jnp.sum(weights, axis=-1, keepdims=True))
    blended = jnp.einsum('hqk,khd->qhd', low(chances), value_rows.reshape(LEN, HEADS, HEAD_DIM), precision=exact_mode)
    return blended.reshape(LEN, D)

def residual_block(stream, offsets_row, gain_rows, shift_rows, heads_matrix, heads_offsets, merge_matrix, branch_rows, expand_matrix, hidden_row, shrink_matrix):
    normed = low(layer_norm(stream, gain_rows[0], shift_rows[0]))
    query_rows = low(low_back(matmul(normed, heads_matrix[0]) + heads_offsets[0]))
    key_rows = low(low_back(matmul(normed, heads_matrix[1])))
    value_rows = low(low_back(matmul(normed, heads_matrix[2]) + heads_offsets[1]))
    blended = low(low_back(attention(query_rows, key_rows, value_rows, offsets_row)))
    middle = stream + low_back(matmul(blended, merge_matrix) + branch_rows[0])
    normed_two = low(layer_norm(middle, gain_rows[1], shift_rows[1]))
    hidden = low_back(matmul(normed_two, expand_matrix) + hidden_row)
    active = low(gelu_tanh(hidden))
    return middle + low_back(matmul(active, shrink_matrix) + branch_rows[1])

def forward(stream, params, offsets_row):
    for layer_index in range(LAYERS):
        stream = residual_block(stream, offsets_row, *[weight[layer_index] for weight in params])
    return stream

def reference(tokens, positions, norm_gain, norm_shift, heads_weight, offsets, merge_weight, branch_bias, expand_weight, hidden_bias, shrink_weight, cotangent):
    params = (norm_gain.astype(jnp.float32), norm_shift.astype(jnp.float32), heads_weight.astype(jnp.float32), offsets.astype(jnp.float32), merge_weight.astype(jnp.float32), branch_bias.astype(jnp.float32), expand_weight.astype(jnp.float32), hidden_bias.astype(jnp.float32), shrink_weight.astype(jnp.float32))
    sequences = TOKENS // LEN

    def sequence_step(running, record):
        token_rows, offsets_row, upstream = record
        result, pullback = jax.vjp(partial(forward, offsets_row=offsets_row), token_rows.astype(jnp.float32), params)
        grad_rows, grad_params = pullback(upstream.astype(jnp.float32))
        running = tuple((summed + gradient for summed, gradient in zip(running, grad_params)))
        return (running, (result.astype(jnp.bfloat16), grad_rows.astype(jnp.bfloat16)))
    initial = tuple((jnp.zeros(weight.shape, jnp.float32) for weight in params))
    running, (outputs, gradients) = lax.scan(sequence_step, initial, (tokens.reshape(sequences, LEN, D), positions.reshape(sequences, LEN), cotangent.reshape(sequences, LEN, D)))
    return (outputs.reshape(TOKENS, D), gradients.reshape(TOKENS, D), running[0], running[1], running[2], running[3], running[4], running[5], running[6], running[7], running[8])
```

```python
import jax
import jax.numpy as jnp
from jax import lax
from jax.experimental import pallas as pl
from jax.experimental.pallas import tpu as pltpu
from jax.sharding import PartitionSpec as P
MESH = pl.DeviceIdType.MESH


class Exchange:
    def __init__(self, groups, rows, cols, slots, lags):
        self.groups, self.rows, self.cols, self.slots = groups, rows, cols, slots
        self.half = rows // 2
        self.chunk = self.half // 4
        starts = [0]
        for lag in lags:
            starts.append(starts[-1] + lag)
        self.starts = starts
        self.ticks = groups + starts[-1]
        self.last_slots = starts[9]
        self.gather_slots = max(starts[8] - starts[1], slots)

    def scratch(self):
        groups, slots, half, chunk, cols = self.groups, self.slots, self.half, self.chunk, self.cols
        dma = pltpu.SemaphoreType.DMA
        plain = pltpu.SemaphoreType.REGULAR
        return dict(
            held=pltpu.VMEM((self.held_slots(), 2, half, cols), jnp.float32),
            swap_in=pltpu.VMEM((slots, 2, half, cols), jnp.float32),
            chain_in=pltpu.VMEM((slots, 3, 2, 2, chunk, cols), jnp.float32),
            third_in=pltpu.VMEM((slots, 2, chunk, cols), jnp.float32),
            swap_s=dma((slots,)), swap_r=dma((slots,)),
            chain_s=dma((slots, 3, 2)), chain_r=dma((slots, 3, 2)),
            third_s=dma((slots,)), third_r=dma((slots,)),
            gather_s=dma((slots, 3, 2)), gather_r=dma((self.gather_slots, 3, 2)),
            last_s=dma((slots,)), last_r=dma((self.last_slots,)),
            own_s=dma((slots,)), load_s=dma((slots,)),
            swap_c=plain((2,)), chain_c=plain((3, 2)), third_c=plain((2,)),
        )

    def held_slots(self):
        return self.groups

    def setup(self, refs):
        self.refs = refs
        dp = lax.axis_index("dp")
        core = lax.axis_index("tensor")
        low = lax.rem(dp, 16)
        self.dp, self.core = dp, core
        self.z = lax.div(low, 4)
        self.y = lax.rem(lax.div(low, 2), 2)
        self.x = lax.rem(low, 2)
        self.step_x = 1 - 2 * self.x
        self.step_y = 2 - 4 * self.y
        self.along = ((dp + 4, core), (dp - 4, core))

    def barrier(self, others=()):
        z = self.z
        bar = pltpu.get_barrier_semaphore()

        def greet(device):
            pl.semaphore_signal(bar, inc=1, device_id=device, device_id_type=MESH)

        for device in ((self.dp + self.step_x, self.core), (self.dp + self.step_y, self.core)) + tuple(others):
            greet(device)

        @pl.when(z < 3)
        def _():
            greet(self.along[0])

        @pl.when(z > 0)
        def _():
            greet(self.along[1])

        pl.semaphore_wait(bar, 2 + len(others) + (z < 3).astype(jnp.int32) + (z > 0).astype(jnp.int32))

    def first(self, g):
        return (self.dp + jnp.where(lax.rem(g, 2) == 0, self.step_x, self.step_y), self.core)

    def third(self, g):
        return (self.dp + jnp.where(lax.rem(g, 2) == 0, self.step_y, self.step_x), self.core)

    def side(self, g):
        return jnp.where(lax.rem(g, 2) == 0, self.x, self.y)

    def copy(self, src, dst, send, recv, device):
        return pltpu.make_async_remote_copy(
            src_ref=src, dst_ref=dst, send_sem=send, recv_sem=recv, device_id=device, device_id_type=MESH
        )

    def rows_of(self, j):
        return pl.ds(pl.multiple_of(j * self.chunk, 8), self.chunk)

    def held(self, g):
        return self.refs["held"].at[g]

    def swap(self, g):
        r, k = self.refs, lax.rem(g, self.slots)
        return self.copy(self.sent_half(g), r["swap_in"].at[k], r["swap_s"].at[k], r["swap_r"].at[k], self.first(g))

    def chain_send(self, step, d, g):
        z, r, k = self.z, self.refs, lax.rem(g, self.slots)
        j = 4 - step + z if d == 0 else step - 4 + z
        here = ((z < 3) & (step > z)) if d == 0 else ((z > 0) & (step > 3 - z))
        at = (k, step - 1, d)
        part = self.held(g).at[:, self.rows_of(j)]
        return here, self.copy(part, r["chain_in"].at[at], r["chain_s"].at[at], r["chain_r"].at[at], self.along[d])

    def start_chain(self, step, g):
        for d in range(2):
            here, copy = self.chain_send(step, d, g)

            @pl.when(here)
            def _():
                @pl.when(g >= self.slots)
                def _():
                    pl.semaphore_wait(self.refs["chain_c"].at[step - 1, d], 1)

                copy.start()

    def finish_chain(self, step, g):
        z, r, k = self.z, self.refs, lax.rem(g, self.slots)
        for d in range(2):
            here, copy = self.chain_send(step, d, g)

            @pl.when(here)
            def _():
                copy.wait_send()

        for d in range(2):
            here = ((z >= 1) & (step >= z)) if d == 0 else ((z <= 2) & (step >= 3 - z))
            j = 3 - step + z if d == 0 else step - 3 + z
            at = (k, step - 1, d)

            @pl.when(here)
            def _():
                came = r["chain_in"].at[at]
                self.copy(came, came, r["chain_s"].at[at], r["chain_r"].at[at], self.along[1 - d]).wait_recv()
                part = self.held(g).at[:, self.rows_of(j)]
                part[...] = part[...] + came[...]

                @pl.when(g + self.slots < self.groups)
                def _():
                    pl.semaphore_signal(
                        r["chain_c"].at[step - 1, d], inc=1, device_id=self.along[1 - d], device_id_type=MESH
                    )

    def third_swap(self, g):
        r, k = self.refs, lax.rem(g, self.slots)
        part = self.held(g).at[:, self.rows_of(self.z)]
        return self.copy(part, r["third_in"].at[k], r["third_s"].at[k], r["third_r"].at[k], self.third(g))

    def gather_copy(self, step, d, g, j, source=None):
        r, k = self.refs, lax.rem(g, self.slots)
        part = self.result(g, self.side(g) * self.half + j * self.chunk, self.chunk)
        return self.copy(
            part if source is None else source,
            part,
            r["gather_s"].at[k, step - 1, d],
            r["gather_r"].at[lax.rem(g, self.gather_slots), step - 1, d],
            self.along[d],
        )

    def gather_send(self, step, d, g):
        z = self.z
        j = z - (step - 1) if d == 0 else z + step - 1
        here = ((z < 3) & (step - 1 <= z)) if d == 0 else ((z > 0) & (z + step - 1 <= 3))
        source = self.held(g).at[:, self.rows_of(z)] if step == 1 else None
        return here, self.gather_copy(step, d, g, j, source)

    def start_gather(self, step, g):
        for d in range(2):
            here, copy = self.gather_send(step, d, g)

            @pl.when(here)
            def _():
                copy.start()

    def finish_gather(self, step, g):
        z = self.z
        for d in range(2):
            here, copy = self.gather_send(step, d, g)

            @pl.when(here)
            def _():
                copy.wait_send()

        for d in range(2):
            here = (z >= step) if d == 0 else (z + step <= 3)
            j = z - step if d == 0 else z + step

            @pl.when(here)
            def _():
                self.gather_copy(step, d, g, j).wait_recv()

    def own_copy(self, g):
        k = lax.rem(g, self.slots)
        part = self.held(g).at[:, self.rows_of(self.z)]
        return pltpu.make_async_copy(
            part, self.result(g, self.side(g) * self.half + self.z * self.chunk, self.chunk), self.refs["own_s"].at[k]
        )

    def last(self, g):
        r, k = self.refs, lax.rem(g, self.slots)
        part = self.result(g, self.side(g) * self.half, self.half)
        return self.copy(part, part, r["last_s"].at[k], r["last_r"].at[lax.rem(g, self.last_slots)], self.first(g))

    def stage(self, e, g):
        r, slots, groups = self.refs, self.slots, self.groups
        k = lax.rem(g, slots)
        if e == 0:
            self.prepare(g)

            @pl.when(g >= slots)
            def _():
                pl.semaphore_wait(r["swap_c"].at[lax.rem(g, 2)], 1)

            self.swap(g).start()
        elif e == 1:
            self.settle(g)
            copy = self.swap(g)
            copy.wait_send()
            copy.wait_recv()
            mine = self.held(g)
            mine[...] = mine[...] + r["swap_in"][k]

            @pl.when(g + slots < groups)
            def _():
                pl.semaphore_signal(
                    r["swap_c"].at[lax.rem(g, 2)], inc=1, device_id=self.first(g), device_id_type=MESH
                )

            self.start_chain(1, g)
        elif e in (2, 3):
            self.finish_chain(e - 1, g)
            self.start_chain(e, g)
        elif e == 4:
            self.finish_chain(3, g)

            @pl.when(g >= slots)
            def _():
                pl.semaphore_wait(r["third_c"].at[lax.rem(g, 2)], 1)

            self.third_swap(g).start()
        elif e == 5:
            copy = self.third_swap(g)
            copy.wait_send()
            copy.wait_recv()
            part = self.held(g).at[:, self.rows_of(self.z)]
            part[...] = part[...] + r["third_in"][k]

            @pl.when(g + slots < groups)
            def _():
                pl.semaphore_signal(
                    r["third_c"].at[lax.rem(g, 2)], inc=1, device_id=self.third(g), device_id_type=MESH
                )

            self.start_gather(1, g)
            self.own_copy(g).start()
        elif e in (6, 7):
            self.finish_gather(e - 5, g)
            self.start_gather(e - 4, g)
        elif e == 8:
            self.finish_gather(3, g)
            self.own_copy(g).wait()
            self.last(g).start()
        else:
            copy = self.last(g)
            copy.wait_send()
            copy.wait_recv()

    def tick(self, t):
        for e in reversed(range(10)):
            g = t - self.starts[e]

            @pl.when((g >= 0) & (g < self.groups))
            def _():
                self.stage(e, g)


class FlatExchange(Exchange):
    def sent_half(self, g):
        return self.source.at[g, :, pl.ds(pl.multiple_of((1 - self.side(g)) * self.half, 8), self.half)]

    def load(self, g):
        k = lax.rem(g, self.slots)
        own = self.source.at[g, :, pl.ds(pl.multiple_of(self.side(g) * self.half, 8), self.half)]
        return pltpu.make_async_copy(own, self.held(g), self.refs["load_s"].at[k])

    def prepare(self, g):
        self.load(g).start()

    def settle(self, g):
        self.load(g).wait()

    def result(self, g, start, size):
        return self.target.at[g, :, pl.ds(pl.multiple_of(start, 8), size)]


def all_reduce(flat, slots=4, lags=(2, 1, 1, 1, 1, 1, 1, 1, 2)):
    groups, _, rows, cols = flat.shape
    plan = FlatExchange(groups, rows, cols, slots, lags)
    scratch = plan.scratch()
    names = list(scratch)

    def kernel(source, target, *refs):
        plan.source, plan.target = source, target
        plan.setup(dict(zip(names, refs)))
        plan.barrier()

        def step(t, carry):
            plan.tick(t)
            return carry

        lax.fori_loop(0, plan.ticks, step, 0)

    return pl.pallas_call(
        kernel,
        out_shape=jax.ShapeDtypeStruct(flat.shape, jnp.float32),
        in_specs=[pl.BlockSpec(memory_space=pl.ANY)],
        out_specs=pl.BlockSpec(memory_space=pl.ANY),
        scratch_shapes=[scratch[n] for n in names],
        compiler_params=pltpu.CompilerParams(collective_id=0, has_side_effects=True, vmem_limit_bytes=60 * 2**20),
    )(flat)


HEAD_DIM = 64
LEN = 1024
LAYERS = 2
UNIT = 384


def layer_norm(stream, gain_row, shift_row):
    centre = stream - jnp.mean(stream, axis=-1, keepdims=True)
    spread = jnp.mean(centre * centre, axis=-1, keepdims=True)
    return centre * lax.rsqrt(spread + 1e-05) * gain_row + shift_row


def gelu_tanh(values):
    return (
        0.5
        * values
        * (1.0 + jnp.tanh(0.7978845608028654 * (values + 0.044715 * values * values * values)))
    )


def block_mask(first_row, amount, offset_part, length):
    query_index = first_row + jnp.arange(amount, dtype=jnp.int32)
    key_index = jnp.arange(length, dtype=jnp.int32)
    return (key_index[None, :] <= query_index[:, None]) & (
        key_index[None, :] >= (query_index - offset_part)[:, None]
    )


def attend_sequence(query_rows, key_rows, value_rows, offsets_row):
    length = query_rows.shape[0]
    local_heads = query_rows.shape[1]
    stride = min(512, length)
    pieces = length // stride

    def one_block(record):
        position, query_part, offset_part = record
        scores = (
            jnp.einsum("qhd,khd->hqk", query_part, key_rows, preferred_element_type=jnp.float32)
            * 0.125
        )
        allowed = block_mask(position * stride, stride, offset_part, length)
        scores = jnp.where(allowed[None], scores, -1e30)
        highest = jnp.max(scores, axis=-1, keepdims=True)
        weights = jnp.exp(scores - highest)
        totals = jnp.sum(weights, axis=-1, keepdims=True)
        chances = (weights / totals).astype(jnp.bfloat16)
        blended = jnp.einsum(
            "hqk,khd->qhd", chances, value_rows, preferred_element_type=jnp.float32
        )
        return (blended.astype(jnp.bfloat16), (highest + jnp.log(totals))[:, :, 0])

    blended, logsum = lax.map(
        one_block,
        (
            jnp.arange(pieces, dtype=jnp.int32),
            query_rows.reshape(pieces, stride, local_heads, HEAD_DIM),
            offsets_row.reshape(pieces, stride),
        ),
    )
    return (blended.reshape(length, local_heads, HEAD_DIM), logsum)


def attend_back(query_rows, key_rows, value_rows, offsets_row, logsum, grad_blended):
    length = query_rows.shape[0]
    local_heads = query_rows.shape[1]
    stride = min(512, length)
    pieces = length // stride

    def one_block(running, record):
        grad_keys, grad_values = running
        position, query_part, offset_part, logsum_part, grad_part = record
        scores = (
            jnp.einsum("qhd,khd->hqk", query_part, key_rows, preferred_element_type=jnp.float32)
            * 0.125
        )
        allowed = block_mask(position * stride, stride, offset_part, length)
        chances = jnp.where(allowed[None], jnp.exp(scores - logsum_part[:, :, None]), 0.0)
        grad_chances = jnp.einsum(
            "qhd,khd->hqk", grad_part, value_rows, preferred_element_type=jnp.float32
        )
        centre = jnp.sum(chances * grad_chances, axis=-1, keepdims=True)
        grad_scores = (chances * (grad_chances - centre)).astype(jnp.bfloat16)
        grad_query = (
            jnp.einsum("hqk,khd->qhd", grad_scores, key_rows, preferred_element_type=jnp.float32)
            * 0.125
        )
        grad_keys = (
            grad_keys
            + jnp.einsum(
                "hqk,qhd->khd", grad_scores, query_part, preferred_element_type=jnp.float32
            )
            * 0.125
        )
        grad_values = grad_values + jnp.einsum(
            "hqk,qhd->khd",
            chances.astype(jnp.bfloat16),
            grad_part,
            preferred_element_type=jnp.float32,
        )
        return ((grad_keys, grad_values), grad_query.astype(jnp.bfloat16))

    empty = jnp.zeros((length, local_heads, HEAD_DIM), jnp.float32)
    (grad_keys, grad_values), grad_query = lax.scan(
        one_block,
        (empty, empty),
        (
            jnp.arange(pieces, dtype=jnp.int32),
            query_rows.reshape(pieces, stride, local_heads, HEAD_DIM),
            offsets_row.reshape(pieces, stride),
            logsum,
            grad_blended.reshape(pieces, stride, local_heads, HEAD_DIM),
        ),
    )
    return (
        grad_query.reshape(length, local_heads, HEAD_DIM),
        grad_keys.astype(jnp.bfloat16),
        grad_values.astype(jnp.bfloat16),
    )


def add_branch(stream, partial_sum, bias_row):
    return stream + (lax.psum(partial_sum, "tensor") + bias_row)


def reduce_inputs(partial_sum):
    return lax.psum(partial_sum, "tensor")


BLOCK = 16


def columns_to_units(matrix):
    rows, width = matrix.shape
    return matrix.reshape(rows, width // UNIT, UNIT).transpose(1, 0, 2)


def units_to_columns(units):
    count, rows, width = units.shape
    return units.transpose(1, 0, 2).reshape(rows, count * width)


def reduce_grads(layers):
    ranks = lax.axis_size("dp")
    small = jnp.stack([jnp.concatenate([layer[m].reshape(-1) for m in (0, 1, 3, 5, 7)]) for layer in layers])
    pieces = []
    for layer in reversed(layers):
        heads, merge, expand, shrink = layer[2], layer[4], layer[6], layer[8]
        depth = expand.shape[0]
        pieces.append(columns_to_units(shrink).reshape(shrink.shape[1] // UNIT, -1, UNIT, UNIT).transpose(1, 0, 2, 3).reshape(-1, UNIT, UNIT))
        pieces.append(columns_to_units(expand).reshape(-1, UNIT, UNIT))
        pieces.append(columns_to_units(merge))
        pieces.append(heads.reshape(-1, UNIT, UNIT))
    flat = jnp.concatenate(pieces)
    flat = flat.reshape(flat.shape[0] // 2, 2, UNIT, UNIT)
    if ranks % BLOCK:
        flat = lax.psum(flat, "dp")
    else:
        flat = all_reduce(flat)
        if ranks > BLOCK:
            groups = [[j * BLOCK + i for j in range(ranks // BLOCK)] for i in range(BLOCK)]
            flat = lax.psum(flat, "dp", axis_index_groups=groups)
    small = lax.psum(small, "dp")
    flat = flat.reshape(-1, UNIT, UNIT)
    out = []
    at = 0
    for layer in reversed(layers):
        heads, merge, expand, shrink = layer[2], layer[4], layer[6], layer[8]
        def take(like):
            nonlocal at
            n = like.size // (UNIT * UNIT)
            at += n
            return flat[at - n : at]
        shrink_sum = take(shrink).reshape(-1, shrink.shape[1] // UNIT, UNIT, UNIT).transpose(0, 2, 1, 3).reshape(shrink.shape)
        expand_sum = units_to_columns(take(expand).reshape(-1, expand.shape[0], UNIT))
        merge_sum = units_to_columns(take(merge))
        heads_sum = take(heads).reshape(heads.shape)
        out.append((heads_sum, merge_sum, expand_sum, shrink_sum))
    out = [jnp.stack(group) for group in zip(*reversed(out))]
    smalls = []
    at = 0
    for m in (0, 1, 3, 5, 7):
        like = layers[0][m]
        smalls.append(small[:, at : at + like.size].reshape((len(layers),) + like.shape))
        at += like.size
    return (smalls[0], smalls[1], out[0], smalls[2], out[1], smalls[3], out[2], smalls[4], out[3])


def to_heads(matrix, sequences, local_heads):
    return matrix.reshape(sequences, LEN, local_heads, HEAD_DIM)


def on_device(
    tokens,
    positions,
    norm_gain,
    norm_shift,
    heads_weight,
    offsets,
    merge_weight,
    branch_bias,
    expand_weight,
    hidden_bias,
    shrink_weight,
    cotangent,
):
    row_count = tokens.shape[0]
    local_width = heads_weight.shape[3]
    local_heads = local_width // HEAD_DIM
    sequences = row_count // LEN
    offsets_rows = positions.reshape(sequences, LEN)
    stream = tokens.astype(jnp.float32)
    kept_values = []
    for layer_index in range(LAYERS):
        normed = layer_norm(stream, norm_gain[layer_index, 0], norm_shift[layer_index, 0]).astype(
            jnp.bfloat16
        )
        projected = jnp.einsum(
            "td,cde->cte", normed, heads_weight[layer_index], preferred_element_type=jnp.float32
        )
        query_rows = (projected[0] + offsets[layer_index, 0]).astype(jnp.bfloat16)
        key_rows = projected[1].astype(jnp.bfloat16)
        value_rows = (projected[2] + offsets[layer_index, 1]).astype(jnp.bfloat16)
        blended, logsum = lax.map(
            lambda record: attend_sequence(record[0], record[1], record[2], record[3]),
            (
                to_heads(query_rows, sequences, local_heads),
                to_heads(key_rows, sequences, local_heads),
                to_heads(value_rows, sequences, local_heads),
                offsets_rows,
            ),
        )
        blended_rows = blended.reshape(row_count, local_width)
        partial_sum = jnp.dot(
            blended_rows, merge_weight[layer_index], preferred_element_type=jnp.float32
        )
        middle = add_branch(stream, partial_sum, branch_bias[layer_index, 0])
        normed_two = layer_norm(
            middle, norm_gain[layer_index, 1], norm_shift[layer_index, 1]
        ).astype(jnp.bfloat16)
        hidden = (
            jnp.dot(normed_two, expand_weight[layer_index], preferred_element_type=jnp.float32)
            + hidden_bias[layer_index]
        )
        active = gelu_tanh(hidden).astype(jnp.bfloat16)
        partial_sum = jnp.dot(
            active, shrink_weight[layer_index], preferred_element_type=jnp.float32
        )
        kept_values.append(
            (
                stream,
                normed,
                query_rows,
                key_rows,
                value_rows,
                logsum,
                blended_rows,
                middle,
                normed_two,
                hidden,
                active,
            )
        )
        stream = add_branch(middle, partial_sum, branch_bias[layer_index, 1])
    output = stream.astype(jnp.bfloat16)
    upstream = cotangent.astype(jnp.float32)
    layer_grads = [None] * LAYERS
    for layer_index in reversed(range(LAYERS)):
        (
            stream_in,
            normed,
            query_rows,
            key_rows,
            value_rows,
            logsum,
            blended_rows,
            middle,
            normed_two,
            hidden,
            active,
        ) = kept_values[layer_index]
        grad_second = upstream.astype(jnp.bfloat16)
        bias_second = jnp.sum(grad_second, axis=0, dtype=jnp.float32)
        shrink_grad = jnp.einsum(
            "tf,td->fd", active, grad_second, preferred_element_type=jnp.float32
        )
        grad_active = jnp.einsum(
            "td,fd->tf", grad_second, shrink_weight[layer_index], preferred_element_type=jnp.float32
        )
        _, gelu_pullback = jax.vjp(gelu_tanh, hidden)
        grad_pre = gelu_pullback(grad_active)[0].astype(jnp.bfloat16)
        hidden_grad = jnp.sum(grad_pre, axis=0, dtype=jnp.float32)
        expand_grad = jnp.einsum(
            "td,tf->df", normed_two, grad_pre, preferred_element_type=jnp.float32
        )
        grad_normed_two = reduce_inputs(
            jnp.einsum(
                "tf,df->td",
                grad_pre,
                expand_weight[layer_index],
                preferred_element_type=jnp.float32,
            )
        )
        _, norm_pullback = jax.vjp(
            layer_norm, middle, norm_gain[layer_index, 1], norm_shift[layer_index, 1]
        )
        grad_middle, gain_second, shift_second = norm_pullback(grad_normed_two)
        grad_middle = grad_middle + upstream
        grad_first = grad_middle.astype(jnp.bfloat16)
        bias_first = jnp.sum(grad_first, axis=0, dtype=jnp.float32)
        merge_grad = jnp.einsum(
            "te,td->ed", blended_rows, grad_first, preferred_element_type=jnp.float32
        )
        grad_blended = jnp.einsum(
            "td,ed->te", grad_first, merge_weight[layer_index], preferred_element_type=jnp.float32
        ).astype(jnp.bfloat16)
        grad_query, grad_keys, grad_values = lax.map(
            lambda record: attend_back(
                record[0], record[1], record[2], record[3], record[4], record[5]
            ),
            (
                to_heads(query_rows, sequences, local_heads),
                to_heads(key_rows, sequences, local_heads),
                to_heads(value_rows, sequences, local_heads),
                offsets_rows,
                logsum,
                to_heads(grad_blended, sequences, local_heads),
            ),
        )
        grad_stack = jnp.stack(
            [
                grad_query.reshape(row_count, local_width),
                grad_keys.reshape(row_count, local_width),
                grad_values.reshape(row_count, local_width),
            ]
        )
        heads_grad = jnp.einsum(
            "td,cte->cde", normed, grad_stack, preferred_element_type=jnp.float32
        )
        offsets_grad = jnp.stack(
            [
                jnp.sum(grad_stack[0], axis=0, dtype=jnp.float32),
                jnp.sum(grad_stack[2], axis=0, dtype=jnp.float32),
            ]
        )
        grad_normed = reduce_inputs(
            jnp.einsum(
                "cte,cde->td",
                grad_stack,
                heads_weight[layer_index],
                preferred_element_type=jnp.float32,
            )
        )
        _, norm_pullback = jax.vjp(
            layer_norm, stream_in, norm_gain[layer_index, 0], norm_shift[layer_index, 0]
        )
        grad_stream, gain_first, shift_first = norm_pullback(grad_normed)
        upstream = grad_stream + grad_middle
        gradients = (
            jnp.stack([gain_first, gain_second]),
            jnp.stack([shift_first, shift_second]),
            heads_grad,
            offsets_grad,
            merge_grad,
            jnp.stack([bias_first, bias_second]),
            expand_grad,
            hidden_grad,
            shrink_grad,
        )
        layer_grads[layer_index] = gradients
    stacked = reduce_grads(layer_grads)
    return (
        output,
        upstream.astype(jnp.bfloat16),
        stacked[0],
        stacked[1],
        stacked[2],
        stacked[3],
        stacked[4],
        stacked[5],
        stacked[6],
        stacked[7],
        stacked[8],
    )


def solution(mesh):
    placed = (
        P("dp", None),
        P("dp"),
        P(),
        P(),
        P(None, None, None, "tensor"),
        P(None, None, "tensor"),
        P(None, "tensor", None),
        P(),
        P(None, None, "tensor"),
        P(None, "tensor"),
        P(None, "tensor", None),
        P("dp", None),
    )
    return jax.shard_map(
        on_device,
        mesh=mesh,
        in_specs=placed,
        out_specs=(
            P("dp", None),
            P("dp", None),
            P(),
            P(),
            P(None, None, None, "tensor"),
            P(None, None, "tensor"),
            P(None, "tensor", None),
            P(),
            P(None, None, "tensor"),
            P(None, "tensor"),
            P(None, "tensor", None),
        ),
        check_vma=False,
    )
```

```python
import jax
import jax.numpy as jnp
from jax import lax
from jax.experimental import pallas as pl
from jax.experimental.pallas import tpu as pltpu
from jax.sharding import PartitionSpec as P

HEAD_DIM = 64
LEN = 1024
LAYERS = 2
UNIT = 384
BLOCK = 16
MESH = pl.DeviceIdType.MESH


class Exchange:
    def __init__(self, groups, rows, cols, slots, lags):
        self.groups, self.rows, self.cols, self.slots = groups, rows, cols, slots
        self.half = rows // 2
        self.chunk = self.half // 4
        starts = [0]
        for lag in lags:
            starts.append(starts[-1] + lag)
        self.starts = starts
        self.ticks = groups + starts[-1]
        self.last_slots = starts[9]
        self.gather_slots = max(starts[8] - starts[1], slots)

    def scratch(self):
        groups, slots, half, chunk, cols = self.groups, self.slots, self.half, self.chunk, self.cols
        dma = pltpu.SemaphoreType.DMA
        plain = pltpu.SemaphoreType.REGULAR
        return dict(
            held=pltpu.VMEM((self.held_slots(), 2, half, cols), jnp.float32),
            swap_in=pltpu.VMEM((slots, 2, half, cols), jnp.float32),
            chain_in=pltpu.VMEM((slots, 3, 2, 2, chunk, cols), jnp.float32),
            third_in=pltpu.VMEM((slots, 2, chunk, cols), jnp.float32),
            swap_s=dma((slots,)), swap_r=dma((slots,)),
            chain_s=dma((slots, 3, 2)), chain_r=dma((slots, 3, 2)),
            third_s=dma((slots,)), third_r=dma((slots,)),
            gather_s=dma((slots, 3, 2)), gather_r=dma((self.gather_slots, 3, 2)),
            last_s=dma((slots,)), last_r=dma((self.last_slots,)),
            own_s=dma((slots,)), load_s=dma((slots,)),
            swap_c=plain((2,)), chain_c=plain((3, 2)), third_c=plain((2,)),
        )

    def held_slots(self):
        return self.groups

    def setup(self, refs):
        self.refs = refs
        dp = lax.axis_index("dp")
        core = lax.axis_index("tensor")
        low = lax.rem(dp, 16)
        self.dp, self.core = dp, core
        self.z = lax.div(low, 4)
        self.y = lax.rem(lax.div(low, 2), 2)
        self.x = lax.rem(low, 2)
        self.step_x = 1 - 2 * self.x
        self.step_y = 2 - 4 * self.y
        self.along = ((dp + 4, core), (dp - 4, core))

    def barrier(self, others=()):
        z = self.z
        bar = pltpu.get_barrier_semaphore()

        def greet(device):
            pl.semaphore_signal(bar, inc=1, device_id=device, device_id_type=MESH)

        for device in ((self.dp + self.step_x, self.core), (self.dp + self.step_y, self.core)) + tuple(others):
            greet(device)

        @pl.when(z < 3)
        def _():
            greet(self.along[0])

        @pl.when(z > 0)
        def _():
            greet(self.along[1])

        pl.semaphore_wait(bar, 2 + len(others) + (z < 3).astype(jnp.int32) + (z > 0).astype(jnp.int32))

    def first(self, g):
        return (self.dp + jnp.where(lax.rem(g, 2) == 0, self.step_x, self.step_y), self.core)

    def third(self, g):
        return (self.dp + jnp.where(lax.rem(g, 2) == 0, self.step_y, self.step_x), self.core)

    def side(self, g):
        return jnp.where(lax.rem(g, 2) == 0, self.x, self.y)

    def copy(self, src, dst, send, recv, device):
        return pltpu.make_async_remote_copy(
            src_ref=src, dst_ref=dst, send_sem=send, recv_sem=recv, device_id=device, device_id_type=MESH
        )

    def rows_of(self, j):
        return pl.ds(pl.multiple_of(j * self.chunk, 8), self.chunk)

    def held(self, g):
        return self.refs["held"].at[g]

    def swap(self, g):
        r, k = self.refs, lax.rem(g, self.slots)
        return self.copy(self.sent_half(g), r["swap_in"].at[k], r["swap_s"].at[k], r["swap_r"].at[k], self.first(g))

    def chain_send(self, step, d, g):
        z, r, k = self.z, self.refs, lax.rem(g, self.slots)
        j = 4 - step + z if d == 0 else step - 4 + z
        here = ((z < 3) & (step > z)) if d == 0 else ((z > 0) & (step > 3 - z))
        at = (k, step - 1, d)
        part = self.held(g).at[:, self.rows_of(j)]
        return here, self.copy(part, r["chain_in"].at[at], r["chain_s"].at[at], r["chain_r"].at[at], self.along[d])

    def start_chain(self, step, g):
        for d in range(2):
            here, copy = self.chain_send(step, d, g)

            @pl.when(here)
            def _():
                @pl.when(g >= self.slots)
                def _():
                    pl.semaphore_wait(self.refs["chain_c"].at[step - 1, d], 1)

                copy.start()

    def finish_chain(self, step, g):
        z, r, k = self.z, self.refs, lax.rem(g, self.slots)
        for d in range(2):
            here, copy = self.chain_send(step, d, g)

            @pl.when(here)
            def _():
                copy.wait_send()

        for d in range(2):
            here = ((z >= 1) & (step >= z)) if d == 0 else ((z <= 2) & (step >= 3 - z))
            j = 3 - step + z if d == 0 else step - 3 + z
            at = (k, step - 1, d)

            @pl.when(here)
            def _():
                came = r["chain_in"].at[at]
                self.copy(came, came, r["chain_s"].at[at], r["chain_r"].at[at], self.along[1 - d]).wait_recv()
                part = self.held(g).at[:, self.rows_of(j)]
                part[...] = part[...] + came[...]

                @pl.when(g + self.slots < self.groups)
                def _():
                    pl.semaphore_signal(
                        r["chain_c"].at[step - 1, d], inc=1, device_id=self.along[1 - d], device_id_type=MESH
                    )

    def third_swap(self, g):
        r, k = self.refs, lax.rem(g, self.slots)
        part = self.held(g).at[:, self.rows_of(self.z)]
        return self.copy(part, r["third_in"].at[k], r["third_s"].at[k], r["third_r"].at[k], self.third(g))

    def gather_copy(self, step, d, g, j, source=None):
        r, k = self.refs, lax.rem(g, self.slots)
        part = self.result(g, self.side(g) * self.half + j * self.chunk, self.chunk)
        return self.copy(
            part if source is None else source,
            part,
            r["gather_s"].at[k, step - 1, d],
            r["gather_r"].at[lax.rem(g, self.gather_slots), step - 1, d],
            self.along[d],
        )

    def gather_send(self, step, d, g):
        z = self.z
        j = z - (step - 1) if d == 0 else z + step - 1
        here = ((z < 3) & (step - 1 <= z)) if d == 0 else ((z > 0) & (z + step - 1 <= 3))
        source = self.held(g).at[:, self.rows_of(z)] if step == 1 else None
        return here, self.gather_copy(step, d, g, j, source)

    def start_gather(self, step, g):
        for d in range(2):
            here, copy = self.gather_send(step, d, g)

            @pl.when(here)
            def _():
                copy.start()

    def finish_gather(self, step, g):
        z = self.z
        for d in range(2):
            here, copy = self.gather_send(step, d, g)

            @pl.when(here)
            def _():
                copy.wait_send()

        for d in range(2):
            here = (z >= step) if d == 0 else (z + step <= 3)
            j = z - step if d == 0 else z + step

            @pl.when(here)
            def _():
                self.gather_copy(step, d, g, j).wait_recv()

    def own_copy(self, g):
        k = lax.rem(g, self.slots)
        part = self.held(g).at[:, self.rows_of(self.z)]
        return pltpu.make_async_copy(
            part, self.result(g, self.side(g) * self.half + self.z * self.chunk, self.chunk), self.refs["own_s"].at[k]
        )

    def last(self, g):
        r, k = self.refs, lax.rem(g, self.slots)
        part = self.result(g, self.side(g) * self.half, self.half)
        return self.copy(part, part, r["last_s"].at[k], r["last_r"].at[lax.rem(g, self.last_slots)], self.first(g))

    def stage(self, e, g):
        r, slots, groups = self.refs, self.slots, self.groups
        k = lax.rem(g, slots)
        if e == 0:
            self.prepare(g)

            @pl.when(g >= slots)
            def _():
                pl.semaphore_wait(r["swap_c"].at[lax.rem(g, 2)], 1)

            self.swap(g).start()
        elif e == 1:
            self.settle(g)
            copy = self.swap(g)
            copy.wait_send()
            copy.wait_recv()
            mine = self.held(g)
            mine[...] = mine[...] + r["swap_in"][k]

            @pl.when(g + slots < groups)
            def _():
                pl.semaphore_signal(
                    r["swap_c"].at[lax.rem(g, 2)], inc=1, device_id=self.first(g), device_id_type=MESH
                )

            self.start_chain(1, g)
        elif e in (2, 3):
            self.finish_chain(e - 1, g)
            self.start_chain(e, g)
        elif e == 4:
            self.finish_chain(3, g)

            @pl.when(g >= slots)
            def _():
                pl.semaphore_wait(r["third_c"].at[lax.rem(g, 2)], 1)

            self.third_swap(g).start()
        elif e == 5:
            copy = self.third_swap(g)
            copy.wait_send()
            copy.wait_recv()
            part = self.held(g).at[:, self.rows_of(self.z)]
            part[...] = part[...] + r["third_in"][k]

            @pl.when(g + slots < groups)
            def _():
                pl.semaphore_signal(
                    r["third_c"].at[lax.rem(g, 2)], inc=1, device_id=self.third(g), device_id_type=MESH
                )

            self.start_gather(1, g)
            self.own_copy(g).start()
        elif e in (6, 7):
            self.finish_gather(e - 5, g)
            if e == 6:
                self.own_copy(g).wait()
            self.start_gather(e - 4, g)
        elif e == 8:
            self.finish_gather(3, g)
            self.last(g).start()
        else:
            copy = self.last(g)
            copy.wait_send()
            copy.wait_recv()

    def tick(self, t):
        for e in reversed(range(10)):
            g = t - self.starts[e]

            @pl.when((g >= 0) & (g < self.groups))
            def _():
                self.stage(e, g)


class FlatExchange(Exchange):
    def sent_half(self, g):
        return self.source.at[g, :, pl.ds(pl.multiple_of((1 - self.side(g)) * self.half, 8), self.half)]

    def load(self, g):
        k = lax.rem(g, self.slots)
        own = self.source.at[g, :, pl.ds(pl.multiple_of(self.side(g) * self.half, 8), self.half)]
        return pltpu.make_async_copy(own, self.held(g), self.refs["load_s"].at[k])

    def prepare(self, g):
        self.load(g).start()

    def settle(self, g):
        self.load(g).wait()

    def result(self, g, start, size):
        return self.target.at[g, :, pl.ds(pl.multiple_of(start, 8), size)]


ROWS = 256


def dot(a, b, dims):
    return lax.dot_general(a, b, (dims, ((), ())), preferred_element_type=jnp.float32)


NN = ((1,), (0,))
NT = ((1,), (1,))
TN = ((0,), (0,))


def gelu_slope(x):
    t = jnp.tanh(0.7978845608028654 * (x + 0.044715 * x * x * x))
    return 0.5 * (1.0 + t) + 0.5 * x * (1.0 - t * t) * (
        0.7978845608028654 * (1.0 + 3.0 * 0.044715 * x * x)
    )


def norm_parts(h):
    centre = h - jnp.mean(h, axis=-1, keepdims=True)
    r = lax.rsqrt(jnp.mean(centre * centre, axis=-1, keepdims=True) + 1e-05)
    return centre * r, r


GAIN, SHIFT, BRANCH, HIDDEN, OFFSETS, SMALL = 0, 2, 4, 6, 8, 16
PIECES = 9
PER_LAYER = 12


class Backward(FlatExchange):
    LOADS = ("act", "pre", "norm", "h", "att", "q", "k", "v", "w_shrink", "w_expand", "w_merge", "w_heads")

    def more_scratch(self):
        T, D, W, F = self.T, self.D, self.W, self.F
        low, full = jnp.bfloat16, jnp.float32
        dma = pltpu.SemaphoreType.DMA
        return dict(
            act=pltpu.VMEM((T, F), low), pre=pltpu.VMEM((T, F), full), norm=pltpu.VMEM((T, D), low),
            h=pltpu.VMEM((T, D), full), att=pltpu.VMEM((T, W), low), q=pltpu.VMEM((T, W), low),
            k=pltpu.VMEM((T, W), low), v=pltpu.VMEM((T, W), low), w_shrink=pltpu.VMEM((F, D), low),
            w_expand=pltpu.VMEM((D, F), low), w_merge=pltpu.VMEM((W, D), low), w_heads=pltpu.VMEM((3, D, W), low),
            g=pltpu.VMEM((T, D), full), low=pltpu.VMEM((T, D), low), came=pltpu.VMEM((T, D), full),
            datt=pltpu.VMEM((T, W), low), dqkv=pltpu.VMEM((3, T, W), low),
            staged=pltpu.VMEM((2, 2, 384, 384), full), dk=pltpu.VMEM((T, 128), full), dv=pltpu.VMEM((T, 128), full),
            small=pltpu.VMEM((2 * SMALL, D), full), small_in=pltpu.VMEM((4, 2 * SMALL, D), full),
            input_s=dma((len(self.LOADS),)), cot_s=dma, staged_s=dma((2,)), tokens_s=dma,
            core_s=dma((T // ROWS,)), core_r=dma((T // ROWS,)), core_c=pltpu.SemaphoreType.REGULAR,
            small_s=dma((4,)), small_r=dma((4,)),
        )

    def held_slots(self):
        return self.starts[6]

    def held(self, g):
        return self.refs["held"].at[lax.rem(g, self.held_slots())]

    def fetch(self, name, layer, second=False):
        source = self.inputs[name][layer]
        if name in ("norm", "h"):
            source = source[1 if second else 0]
        pltpu.make_async_copy(source, self.refs[name], self.refs["input_s"].at[self.LOADS.index(name)]).start()

    def arrive(self, name):
        source = self.inputs[name][0]
        if name in ("norm", "h"):
            source = source[0]
        pltpu.make_async_copy(source, self.refs[name], self.refs["input_s"].at[self.LOADS.index(name)]).wait()

    def fetch_next(self, l, *names, second=False):
        @pl.when(l == 1)
        def _():
            for name in names:
                self.fetch(name, 0, second)

    def stage_copy(self, at, g):
        return pltpu.make_async_copy(self.refs["staged"].at[at], self.source.at[g], self.refs["staged_s"].at[at])

    def put(self, at, g, top, bottom):
        self.refs["staged"][at, 0] = top
        self.refs["staged"][at, 1] = bottom
        self.stage_copy(at, g).start()

    def outer(self, left, left_cols, right, right_cols, at, g):
        for u in range(2):
            a = left[:, pl.ds(pl.multiple_of(left_cols + u * 384, 128), 384)]
            self.refs["staged"][at, u] = dot(a, right[:, right_cols], TN)
        self.stage_copy(at, g).start()

    def core_copy(self, i):
        r = self.refs
        rows = pl.ds(pl.multiple_of(i * ROWS, ROWS), ROWS)
        return self.copy(
            r["pre"].at[rows, pl.ds(0, self.D)], r["came"].at[rows], r["core_s"].at[i], r["core_r"].at[i],
            (self.dp, 1 - self.core),
        )

    def partial(self, make, wait):
        @pl.when(wait)
        def _():
            pl.semaphore_wait(self.refs["core_c"], 1)

        def block(i, carry):
            rows = pl.ds(pl.multiple_of(i * ROWS, ROWS), ROWS)
            self.refs["pre"][rows, 0 : self.D] = make(rows)
            self.core_copy(i).start()
            return carry

        lax.fori_loop(0, self.T // ROWS, block, 0)

    def norm_back(self, l, which, more, after):
        r, D = self.refs, self.D
        gain = self.gain[l, which]
        n = 128
        blocks = ROWS // n

        def block(i, carry):
            @pl.when(lax.rem(i, blocks) == 0)
            def _():
                copy = self.core_copy(lax.div(i, blocks))
                copy.wait_send()
                copy.wait_recv()

            rows = pl.ds(pl.multiple_of(i * n, n), n)
            xhat, rstd = norm_parts(r["h"][rows])
            d = r["pre"][rows, 0:D] + r["came"][rows]
            e = d * gain
            spread = xhat * jnp.mean(e * xhat, axis=-1, keepdims=True)
            new = r["g"][rows] + rstd * (e - jnp.mean(e, axis=-1, keepdims=True) - spread)
            r["g"][rows] = new
            rounded = new.astype(jnp.bfloat16)
            r["low"][rows] = rounded
            return (
                carry[0] + jnp.sum(d * xhat, axis=0, keepdims=True),
                carry[1] + jnp.sum(d, axis=0, keepdims=True),
                carry[2] + jnp.sum(rounded.astype(jnp.float32), axis=0, keepdims=True),
            )

        zero = jnp.zeros((1, D), jnp.float32)
        sums = lax.fori_loop(0, self.T // n, block, (zero, zero, zero))
        self.row(l, GAIN + which)[...] = sums[0]
        self.row(l, SHIFT + which)[...] = sums[1]
        after(sums[2])

        @pl.when(more)
        def _():
            pl.semaphore_signal(
                r["core_c"], inc=1, device_id=(self.dp, 1 - self.core), device_id_type=MESH
            )

    def row(self, l, at, start=0, size=None):
        size = self.D if size is None else size
        return self.refs["small"].at[pl.ds(l * SMALL + at, 1), start : start + size]

    def piece(self, p, l):
        r = self.refs
        T, D, W, F = self.T, self.D, self.W, self.F
        base = (1 - l) * PER_LAYER
        if p == 0:
            @pl.when(l == 1)
            def _():
                pltpu.make_async_copy(self.cotangent, r["low"], r["cot_s"]).wait()

                def widen(i, carry):
                    rows = pl.ds(pl.multiple_of(i * ROWS, ROWS), ROWS)
                    wide = r["low"][rows].astype(jnp.float32)
                    r["g"][rows] = wide
                    return carry + jnp.sum(wide, axis=0, keepdims=True)

                self.row(l, BRANCH + 1)[...] = lax.fori_loop(0, T // ROWS, widen, jnp.zeros((1, D), jnp.float32))

            self.arrive("act")

            def one(i, carry):
                at = lax.rem(i, 2)

                @pl.when(i >= 2)
                def _():
                    self.stage_copy(at, base + i - 2).wait()

                self.outer(r["act"], lax.div(i, 2) * 768, r["low"], pl.ds(pl.multiple_of(at * 384, 128), 384), at, base + i)
                return carry

            lax.fori_loop(0, 4, one, 0)
            for i in (2, 3):
                self.stage_copy(i % 2, base + i).wait()
        elif p == 1:
            self.arrive("w_shrink")
            self.arrive("pre")

            def one(i, carry):
                rows = pl.ds(pl.multiple_of(i * ROWS, ROWS), ROWS)
                sums = []
                for c in range(0, F, 512):
                    d_act = dot(r["low"][rows], r["w_shrink"][c : c + 512], NT)
                    d_pre = (d_act * gelu_slope(r["pre"][rows, c : c + 512])).astype(jnp.bfloat16)
                    r["act"][rows, c : c + 512] = d_pre
                    sums.append(carry[c // 512] + jnp.sum(d_pre.astype(jnp.float32), axis=0, keepdims=True))
                return tuple(sums)

            sums = lax.fori_loop(0, T // ROWS, one, (jnp.zeros((1, 512), jnp.float32),) * (F // 512))
            for i, part in enumerate(sums):
                for j in range(2):
                    at = i * 512 + j * 256
                    self.row(l, HIDDEN + at // D, at % D, 256)[...] = part[:, j * 256 : (j + 1) * 256]
            self.fetch_next(l, "w_shrink")
        elif p == 2:
            self.arrive("w_expand")
            self.partial(lambda rows: dot(r["act"][rows], r["w_expand"][...], NT), l == 0)
            self.arrive("norm")

            def one(i, carry):
                at = lax.rem(i, 2)

                @pl.when(i >= 2)
                def _():
                    self.stage_copy(at, base + 4 + i - 2).wait()

                self.outer(r["norm"], 0, r["act"], pl.ds(pl.multiple_of(i * 384, 128), 384), at, base + 4 + i)
                return carry

            lax.fori_loop(0, 4, one, 0)
            for i in (2, 3):
                self.stage_copy(i % 2, base + 4 + i).wait()
            self.fetch_next(l, "w_expand", "act")
            for layer in range(2):
                @pl.when(l == layer)
                def _():
                    self.fetch("norm", layer)
        elif p == 3:
            self.arrive("h")

            def after(total):
                self.row(l, BRANCH)[...] = total

            self.norm_back(l, 1, jnp.bool_(True), after)
            for layer in range(2):
                @pl.when(l == layer)
                def _():
                    self.fetch("h", layer)

            self.arrive("w_merge")
            self.arrive("att")

            def one(i, carry):
                rows = pl.ds(pl.multiple_of(i * ROWS, ROWS), ROWS)
                r["datt"][rows] = dot(r["low"][rows], r["w_merge"][...], NT).astype(jnp.bfloat16)
                return carry

            lax.fori_loop(0, T // ROWS, one, 0)
            for u in range(2):
                r["staged"][0, u] = dot(r["att"][...], r["low"][:, u * 384 : (u + 1) * 384], TN)
            self.stage_copy(0, base + 8).start()
            self.stage_copy(0, base + 8).wait()
            self.fetch_next(l, "w_merge", "att")
            self.arrive("q")
            self.arrive("k")
            self.arrive("v")
        elif p in (4, 5, 6):
            self.attend_back(p - 4, l)
            if p == 6:
                self.fetch_next(l, "q", "k", "v")
        elif p == 7:
            self.arrive("w_heads")

            def make(rows):
                total = dot(r["dqkv"][0, rows], r["w_heads"][0], NT)
                for c in (1, 2):
                    total = total + dot(r["dqkv"][c, rows], r["w_heads"][c], NT)
                return total

            self.partial(make, jnp.bool_(True))
            self.arrive("norm")
            for c in range(3):
                at = c % 2
                if c == 2:
                    self.stage_copy(at, base + 9).wait()
                for u in range(2):
                    r["staged"][at, u] = dot(r["norm"][:, u * 384 : (u + 1) * 384], r["dqkv"][c], TN)
                self.stage_copy(at, base + 9 + c).start()
            for c in (1, 2):
                self.stage_copy(c % 2, base + 9 + c).wait()
            for i, c in enumerate((0, 2)):
                self.row(l, OFFSETS, i * W, W)[...] = jnp.sum(r["dqkv"][c].astype(jnp.float32), axis=0, keepdims=True)
            self.fetch_next(l, "w_heads")
            self.fetch_next(l, "norm", second=True)
        else:
            self.arrive("h")

            def after(total):
                @pl.when(l == 1)
                def _():
                    self.row(0, BRANCH + 1)[...] = total

            self.norm_back(l, 0, l == 1, after)
            self.fetch_next(l, "pre")
            self.fetch_next(l, "h", second=True)

            @pl.when(l == 0)
            def _():
                pltpu.make_async_copy(r["low"], self.grad_tokens, r["tokens_s"]).start()

    def attend_back(self, pair, l):
        r = self.refs
        T = self.T
        lanes = pl.ds(pl.multiple_of(pair * 128, 128), 128)
        r["dk"][...] = jnp.zeros((T, 128), jnp.float32)
        r["dv"][...] = jnp.zeros((T, 128), jnp.float32)
        lane = lax.broadcasted_iota(jnp.int32, (1, 128), 1)
        for b in range(T // ROWS):
            rows, end = slice(b * ROWS, (b + 1) * ROWS), (b + 1) * ROWS
            query = b * ROWS + lax.broadcasted_iota(jnp.int32, (1, ROWS), 1)
            lowest = query - self.positions[:, rows]
            key = lax.broadcasted_iota(jnp.int32, (end, ROWS), 0)
            allowed = (key <= query) & (key >= lowest)
            q, d = r["q"][rows, lanes], r["datt"][rows, lanes]
            k, v = r["k"][0:end, lanes], r["v"][0:end, lanes]
            dq = jnp.zeros((ROWS, 128), jnp.float32)
            for side in range(2):
                mine = (lax.div(lane, 64) == side).astype(jnp.float32).astype(jnp.bfloat16)
                q_own, d_own = q * mine, d * mine
                scores = dot(k, q_own, NT) * 0.125
                lse = self.lse[l, pl.ds(pair * 2 + side, 1), rows]
                probs = jnp.where(allowed, jnp.exp(scores - lse), 0.0)
                dprob = dot(v, d_own, NT)
                centre = jnp.sum(probs * dprob, axis=0, keepdims=True)
                dscore = (probs * (dprob - centre)).astype(jnp.bfloat16)
                r["dv"][0:end] = r["dv"][0:end] + dot(probs.astype(jnp.bfloat16), d_own, NN)
                r["dk"][0:end] = r["dk"][0:end] + dot(dscore, q_own, NN)
                dq = dq + dot(dscore, k * mine, TN)
            r["dqkv"][0, rows, lanes] = (dq * 0.125).astype(jnp.bfloat16)
        r["dqkv"][1, :, lanes] = (r["dk"][...] * 0.125).astype(jnp.bfloat16)
        r["dqkv"][2, :, lanes] = r["dv"][...].astype(jnp.bfloat16)

    def small_swap(self, step):
        r = self.refs
        z = self.z
        to = (
            self.dp + self.step_x,
            self.dp + self.step_y,
            self.dp + 4 - 8 * lax.rem(z, 2),
            self.dp + 8 - 16 * lax.div(z, 2),
        )[step]
        return self.copy(
            r["small"], r["small_in"].at[step], r["small_s"].at[step], r["small_r"].at[step], (to, self.core)
        )

    def small_stage(self, step):
        if step > 0:
            copy = self.small_swap(step - 1)
            copy.wait_send()
            copy.wait_recv()
            self.refs["small"][...] = self.refs["small"][...] + self.refs["small_in"][step - 1]
        if step < 4:
            self.small_swap(step).start()

    def run(self):
        r = self.refs
        pltpu.make_async_copy(self.cotangent, r["low"], r["cot_s"]).start()
        for name in self.LOADS:
            self.fetch(name, 1, second=True)
        r["small"][...] = jnp.zeros(r["small"].shape, jnp.float32)
        far = (self.dp + 8 - 16 * lax.div(self.z, 2), self.core)
        self.barrier(((self.dp, 1 - self.core), far))

        def step(t, carry):
            l = 1 - lax.div(t, PIECES)
            for p in range(PIECES):
                @pl.when((lax.rem(t, PIECES) == p) & (t < 2 * PIECES))
                def _():
                    self.piece(p, l)

            for s in range(5):
                @pl.when(t == 2 * PIECES + s)
                def _():
                    self.small_stage(s)

            self.tick(t)
            return carry

        lax.fori_loop(0, self.ticks, step, 0)
        pltpu.make_async_copy(r["low"], self.grad_tokens, r["tokens_s"]).wait()
        self.small_out[...] = r["small"][...]


def backward(layers, weights, gain, lse, positions, cotangent, slots=4, lags=(2, 1, 1, 1, 1, 1, 1, 1, 2)):
    T, F = layers[0]["act"].shape
    D, W = cotangent.shape[1], layers[0]["q"].shape[1]
    groups = 2 * PER_LAYER
    plan = Backward(groups, 384, 384, slots, lags)
    plan.T, plan.D, plan.W, plan.F = T, D, W, F
    scratch = plan.scratch() | plan.more_scratch()
    names = list(scratch)
    tree = dict(layers=layers, weights=weights, cotangent=cotangent)
    flat_inputs, shape = jax.tree.flatten(tree)
    n = len(flat_inputs)

    def kernel(*refs):
        held = jax.tree.unflatten(shape, refs[:n])
        plan.gain, plan.lse, plan.positions = refs[n : n + 3]
        plan.target, plan.source, plan.grad_tokens, plan.small_out = refs[n + 3 : n + 7]
        plan.setup(dict(zip(names, refs[n + 7 :])))
        plan.cotangent = held["cotangent"]
        plan.inputs = {name: [held["layers"][i][name] for i in range(2)] for name in ("act", "pre", "norm", "h", "att", "q", "k", "v")}
        for name in ("shrink", "expand", "merge", "heads"):
            plan.inputs["w_" + name] = [held["weights"][name].at[i] for i in range(2)]
        plan.run()

    hbm = pl.BlockSpec(memory_space=pl.ANY)
    vmem = pl.BlockSpec(memory_space=pltpu.VMEM)
    flat = jax.ShapeDtypeStruct((groups, 2, 384, 384), jnp.float32)
    target, _, grad_tokens, small = pl.pallas_call(
        kernel,
        out_shape=(
            flat,
            flat,
            jax.ShapeDtypeStruct((T, D), jnp.bfloat16),
            jax.ShapeDtypeStruct((2 * SMALL, D), jnp.float32),
        ),
        in_specs=[hbm] * n + [vmem] * 3,
        out_specs=(hbm, hbm, hbm, vmem),
        scratch_shapes=[scratch[name] for name in names],
        compiler_params=pltpu.CompilerParams(
            collective_id=0, has_side_effects=True, vmem_limit_bytes=61 * 2**20
        ),
    )(*flat_inputs, gain, lse, positions)
    return target, grad_tokens, small


def layer_norm(stream, gain_row, shift_row):
    centre = stream - jnp.mean(stream, axis=-1, keepdims=True)
    spread = jnp.mean(centre * centre, axis=-1, keepdims=True)
    return centre * lax.rsqrt(spread + 1e-05) * gain_row + shift_row


def gelu_tanh(values):
    return (
        0.5
        * values
        * (1.0 + jnp.tanh(0.7978845608028654 * (values + 0.044715 * values * values * values)))
    )


def block_mask(first_row, amount, offset_part, length):
    query_index = first_row + jnp.arange(amount, dtype=jnp.int32)
    key_index = jnp.arange(length, dtype=jnp.int32)
    return (key_index[None, :] <= query_index[:, None]) & (
        key_index[None, :] >= (query_index - offset_part)[:, None]
    )


def attend_sequence(query_rows, key_rows, value_rows, offsets_row):
    length = query_rows.shape[0]
    local_heads = query_rows.shape[1]
    stride = min(512, length)
    pieces = length // stride

    def one_block(record):
        position, query_part, offset_part = record
        scores = (
            jnp.einsum("qhd,khd->hqk", query_part, key_rows, preferred_element_type=jnp.float32)
            * 0.125
        )
        allowed = block_mask(position * stride, stride, offset_part, length)
        scores = jnp.where(allowed[None], scores, -1e30)
        highest = jnp.max(scores, axis=-1, keepdims=True)
        weights = jnp.exp(scores - highest)
        totals = jnp.sum(weights, axis=-1, keepdims=True)
        chances = (weights / totals).astype(jnp.bfloat16)
        blended = jnp.einsum(
            "hqk,khd->qhd", chances, value_rows, preferred_element_type=jnp.float32
        )
        return (blended.astype(jnp.bfloat16), (highest + jnp.log(totals))[:, :, 0])

    blended, logsum = lax.map(
        one_block,
        (
            jnp.arange(pieces, dtype=jnp.int32),
            query_rows.reshape(pieces, stride, local_heads, HEAD_DIM),
            offsets_row.reshape(pieces, stride),
        ),
    )
    return (blended.reshape(length, local_heads, HEAD_DIM), logsum)


def add_branch(stream, partial_sum, bias_row):
    return stream + (lax.psum(partial_sum, "tensor") + bias_row)


def to_heads(matrix, sequences, local_heads):
    return matrix.reshape(sequences, LEN, local_heads, HEAD_DIM)


def on_device(
    tokens,
    positions,
    norm_gain,
    norm_shift,
    heads_weight,
    offsets,
    merge_weight,
    branch_bias,
    expand_weight,
    hidden_bias,
    shrink_weight,
    cotangent,
):
    row_count = tokens.shape[0]
    local_width = heads_weight.shape[3]
    local_heads = local_width // HEAD_DIM
    sequences = row_count // LEN
    offsets_rows = positions.reshape(sequences, LEN)
    stream = tokens.astype(jnp.float32)
    kept, lses = [], []
    for layer_index in range(LAYERS):
        normed = layer_norm(stream, norm_gain[layer_index, 0], norm_shift[layer_index, 0]).astype(
            jnp.bfloat16
        )
        projected = jnp.einsum(
            "td,cde->cte", normed, heads_weight[layer_index], preferred_element_type=jnp.float32
        )
        query_rows = (projected[0] + offsets[layer_index, 0]).astype(jnp.bfloat16)
        key_rows = projected[1].astype(jnp.bfloat16)
        value_rows = (projected[2] + offsets[layer_index, 1]).astype(jnp.bfloat16)
        blended, logsum = lax.map(
            lambda record: attend_sequence(record[0], record[1], record[2], record[3]),
            (
                to_heads(query_rows, sequences, local_heads),
                to_heads(key_rows, sequences, local_heads),
                to_heads(value_rows, sequences, local_heads),
                offsets_rows,
            ),
        )
        blended_rows = blended.reshape(row_count, local_width)
        partial_sum = jnp.dot(
            blended_rows, merge_weight[layer_index], preferred_element_type=jnp.float32
        )
        middle = add_branch(stream, partial_sum, branch_bias[layer_index, 0])
        normed_two = layer_norm(
            middle, norm_gain[layer_index, 1], norm_shift[layer_index, 1]
        ).astype(jnp.bfloat16)
        hidden = (
            jnp.dot(normed_two, expand_weight[layer_index], preferred_element_type=jnp.float32)
            + hidden_bias[layer_index]
        )
        active = gelu_tanh(hidden).astype(jnp.bfloat16)
        partial_sum = jnp.dot(
            active, shrink_weight[layer_index], preferred_element_type=jnp.float32
        )
        kept.append(
            dict(
                act=active, pre=hidden, norm=(normed, normed_two), h=(stream, middle), att=blended_rows,
                q=query_rows, k=key_rows, v=value_rows,
            )
        )
        lses.append(jnp.pad(logsum[0].transpose(1, 0, 2).reshape(local_heads, row_count), ((0, 2), (0, 0))))
        stream = add_branch(middle, partial_sum, branch_bias[layer_index, 1])
    output = stream.astype(jnp.bfloat16)
    weights = dict(shrink=shrink_weight, expand=expand_weight, merge=merge_weight, heads=heads_weight)
    flat, grad_tokens, small = backward(
        kept, weights, norm_gain[:, :, None], jnp.stack(lses), positions[None], cotangent
    )
    ranks = lax.axis_size("dp")
    if ranks > BLOCK:
        groups = [[j * BLOCK + i for j in range(ranks // BLOCK)] for i in range(BLOCK)]
        flat, small = lax.psum((flat, small), "dp", axis_index_groups=groups)
    width = tokens.shape[1]
    flat = flat.reshape(LAYERS, PER_LAYER, 2, UNIT, UNIT)[::-1]
    small = small.reshape(LAYERS, SMALL, width)
    shrink = flat[:, 0:4].reshape(LAYERS, 2, 2, 2, UNIT, UNIT).transpose(0, 1, 3, 4, 2, 5).reshape(shrink_weight.shape)
    expand = flat[:, 4:8].transpose(0, 2, 3, 1, 4).reshape(expand_weight.shape)
    merge = flat[:, 8].transpose(0, 2, 1, 3).reshape(merge_weight.shape)
    heads = flat[:, 9:12].reshape(heads_weight.shape)
    return (
        output,
        grad_tokens,
        small[:, GAIN : GAIN + 2],
        small[:, SHIFT : SHIFT + 2],
        heads,
        small[:, OFFSETS].reshape(offsets.shape),
        merge,
        small[:, BRANCH : BRANCH + 2],
        expand,
        small[:, HIDDEN : HIDDEN + 2].reshape(hidden_bias.shape),
        shrink,
    )


def solution(mesh):
    placed = (
        P("dp", None),
        P("dp"),
        P(),
        P(),
        P(None, None, None, "tensor"),
        P(None, None, "tensor"),
        P(None, "tensor", None),
        P(),
        P(None, None, "tensor"),
        P(None, "tensor"),
        P(None, "tensor", None),
        P("dp", None),
    )
    return jax.shard_map(
        on_device,
        mesh=mesh,
        in_specs=placed,
        out_specs=(
            P("dp", None),
            P("dp", None),
            P(),
            P(),
            P(None, None, None, "tensor"),
            P(None, None, "tensor"),
            P(None, "tensor", None),
            P(),
            P(None, None, "tensor"),
            P(None, "tensor"),
            P(None, "tensor", None),
        ),
        check_vma=False,
    )
```

```python
from types import SimpleNamespace

import jax
import jax.numpy as jnp
from jax import lax
from jax.experimental import pallas as pl
from jax.experimental.pallas import tpu as pltpu
from jax.sharding import PartitionSpec as P

LAYERS = 2
UNIT = 384
BLOCK = 16
MESH = pl.DeviceIdType.MESH


class Exchange:
    def __init__(self, groups, rows, cols, slots, lags):
        self.groups, self.rows, self.cols, self.slots = groups, rows, cols, slots
        self.half = rows // 2
        self.chunk = self.half // 4
        starts = [0]
        for lag in lags:
            starts.append(starts[-1] + lag)
        self.starts = starts
        self.ticks = groups + starts[-1]
        self.last_slots = starts[9]
        self.gather_slots = max(starts[8] - starts[1], slots)

    def scratch(self):
        groups, slots, half, chunk, cols = self.groups, self.slots, self.half, self.chunk, self.cols
        dma = pltpu.SemaphoreType.DMA
        plain = pltpu.SemaphoreType.REGULAR
        return dict(
            held=pltpu.VMEM((self.held_slots(), 2, half, cols), jnp.float32),
            swap_in=pltpu.VMEM((slots, 2, half, cols), jnp.float32),
            chain_in=pltpu.VMEM((slots, 3, 2, 2, chunk, cols), jnp.float32),
            third_in=pltpu.VMEM((slots, 2, chunk, cols), jnp.float32),
            swap_s=dma((slots,)), swap_r=dma((slots,)),
            chain_s=dma((slots, 3, 2)), chain_r=dma((slots, 3, 2)),
            third_s=dma((slots,)), third_r=dma((slots,)),
            gather_s=dma((slots, 3, 2)), gather_r=dma((self.gather_slots, 3, 2)),
            last_s=dma((slots,)), last_r=dma((self.last_slots,)),
            own_s=dma((slots,)), load_s=dma((slots,)),
            swap_c=plain((2,)), chain_c=plain((3, 2)), third_c=plain((2,)),
        )

    def held_slots(self):
        return self.groups

    def setup(self, refs):
        self.refs = refs
        dp = lax.axis_index("dp")
        core = lax.axis_index("tensor")
        low = lax.rem(dp, 16)
        self.dp, self.core = dp, core
        self.z = lax.div(low, 4)
        self.y = lax.rem(lax.div(low, 2), 2)
        self.x = lax.rem(low, 2)
        self.step_x = 1 - 2 * self.x
        self.step_y = 2 - 4 * self.y
        self.along = ((dp + 4, core), (dp - 4, core))

    def barrier(self, others=()):
        z = self.z
        bar = pltpu.get_barrier_semaphore()

        def greet(device):
            pl.semaphore_signal(bar, inc=1, device_id=device, device_id_type=MESH)

        for device in ((self.dp + self.step_x, self.core), (self.dp + self.step_y, self.core)) + tuple(others):
            greet(device)

        @pl.when(z < 3)
        def _():
            greet(self.along[0])

        @pl.when(z > 0)
        def _():
            greet(self.along[1])

        pl.semaphore_wait(bar, 2 + len(others) + (z < 3).astype(jnp.int32) + (z > 0).astype(jnp.int32))

    def first(self, g):
        return (self.dp + jnp.where(lax.rem(g, 2) == 0, self.step_x, self.step_y), self.core)

    def third(self, g):
        return (self.dp + jnp.where(lax.rem(g, 2) == 0, self.step_y, self.step_x), self.core)

    def side(self, g):
        return jnp.where(lax.rem(g, 2) == 0, self.x, self.y)

    def copy(self, src, dst, send, recv, device):
        return pltpu.make_async_remote_copy(
            src_ref=src, dst_ref=dst, send_sem=send, recv_sem=recv, device_id=device, device_id_type=MESH
        )

    def rows_of(self, j):
        return pl.ds(pl.multiple_of(j * self.chunk, 8), self.chunk)

    def held(self, g):
        return self.refs.held.at[g]

    def swap(self, g):
        r, k = self.refs, lax.rem(g, self.slots)
        return self.copy(self.sent_half(g), r.swap_in.at[k], r.swap_s.at[k], r.swap_r.at[k], self.first(g))

    def chain_send(self, step, d, g):
        z, r, k = self.z, self.refs, lax.rem(g, self.slots)
        j = 4 - step + z if d == 0 else step - 4 + z
        here = ((z < 3) & (step > z)) if d == 0 else ((z > 0) & (step > 3 - z))
        at = (k, step - 1, d)
        part = self.held(g).at[:, self.rows_of(j)]
        return here, self.copy(part, r.chain_in.at[at], r.chain_s.at[at], r.chain_r.at[at], self.along[d])

    def start_chain(self, step, g):
        for d in range(2):
            here, copy = self.chain_send(step, d, g)

            @pl.when(here)
            def _():
                @pl.when(g >= self.slots)
                def _():
                    pl.semaphore_wait(self.refs.chain_c.at[step - 1, d], 1)

                copy.start()

    def finish_chain(self, step, g):
        z, r, k = self.z, self.refs, lax.rem(g, self.slots)
        for d in range(2):
            here, copy = self.chain_send(step, d, g)

            @pl.when(here)
            def _():
                copy.wait_send()

        for d in range(2):
            here = ((z >= 1) & (step >= z)) if d == 0 else ((z <= 2) & (step >= 3 - z))
            j = 3 - step + z if d == 0 else step - 3 + z
            at = (k, step - 1, d)

            @pl.when(here)
            def _():
                came = r.chain_in.at[at]
                self.copy(came, came, r.chain_s.at[at], r.chain_r.at[at], self.along[1 - d]).wait_recv()
                part = self.held(g).at[:, self.rows_of(j)]
                part[...] = part[...] + came[...]

                @pl.when(g + self.slots < self.groups)
                def _():
                    pl.semaphore_signal(
                        r.chain_c.at[step - 1, d], inc=1, device_id=self.along[1 - d], device_id_type=MESH
                    )

    def third_swap(self, g):
        r, k = self.refs, lax.rem(g, self.slots)
        part = self.held(g).at[:, self.rows_of(self.z)]
        return self.copy(part, r.third_in.at[k], r.third_s.at[k], r.third_r.at[k], self.third(g))

    def gather_copy(self, step, d, g, j, source=None):
        r, k = self.refs, lax.rem(g, self.slots)
        part = self.result(g, self.side(g) * self.half + j * self.chunk, self.chunk)
        return self.copy(
            part if source is None else source,
            part,
            r.gather_s.at[k, step - 1, d],
            r.gather_r.at[lax.rem(g, self.gather_slots), step - 1, d],
            self.along[d],
        )

    def gather_send(self, step, d, g):
        z = self.z
        j = z - (step - 1) if d == 0 else z + step - 1
        here = ((z < 3) & (step - 1 <= z)) if d == 0 else ((z > 0) & (z + step - 1 <= 3))
        source = self.held(g).at[:, self.rows_of(z)] if step == 1 else None
        return here, self.gather_copy(step, d, g, j, source)

    def start_gather(self, step, g):
        for d in range(2):
            here, copy = self.gather_send(step, d, g)

            @pl.when(here)
            def _():
                copy.start()

    def finish_gather(self, step, g):
        z = self.z
        for d in range(2):
            here, copy = self.gather_send(step, d, g)

            @pl.when(here)
            def _():
                copy.wait_send()

        for d in range(2):
            here = (z >= step) if d == 0 else (z + step <= 3)
            j = z - step if d == 0 else z + step

            @pl.when(here)
            def _():
                self.gather_copy(step, d, g, j).wait_recv()

    def own_copy(self, g):
        k = lax.rem(g, self.slots)
        part = self.held(g).at[:, self.rows_of(self.z)]
        return pltpu.make_async_copy(
            part, self.result(g, self.side(g) * self.half + self.z * self.chunk, self.chunk), self.refs.own_s.at[k]
        )

    def last(self, g):
        r, k = self.refs, lax.rem(g, self.slots)
        part = self.result(g, self.side(g) * self.half, self.half)
        return self.copy(part, part, r.last_s.at[k], r.last_r.at[lax.rem(g, self.last_slots)], self.first(g))

    def stage(self, e, g):
        r, slots, groups = self.refs, self.slots, self.groups
        k = lax.rem(g, slots)
        if e == 0:
            self.prepare(g)

            @pl.when(g >= slots)
            def _():
                pl.semaphore_wait(r.swap_c.at[lax.rem(g, 2)], 1)

            self.swap(g).start()
        elif e == 1:
            self.settle(g)
            copy = self.swap(g)
            copy.wait_send()
            copy.wait_recv()
            mine = self.held(g)
            mine[...] = mine[...] + r.swap_in[k]

            @pl.when(g + slots < groups)
            def _():
                pl.semaphore_signal(
                    r.swap_c.at[lax.rem(g, 2)], inc=1, device_id=self.first(g), device_id_type=MESH
                )

            self.start_chain(1, g)
        elif e in (2, 3):
            self.finish_chain(e - 1, g)
            self.start_chain(e, g)
        elif e == 4:
            self.finish_chain(3, g)

            @pl.when(g >= slots)
            def _():
                pl.semaphore_wait(r.third_c.at[lax.rem(g, 2)], 1)

            self.third_swap(g).start()
        elif e == 5:
            copy = self.third_swap(g)
            copy.wait_send()
            copy.wait_recv()
            part = self.held(g).at[:, self.rows_of(self.z)]
            part[...] = part[...] + r.third_in[k]

            @pl.when(g + slots < groups)
            def _():
                pl.semaphore_signal(
                    r.third_c.at[lax.rem(g, 2)], inc=1, device_id=self.third(g), device_id_type=MESH
                )

            self.start_gather(1, g)
            self.own_copy(g).start()
        elif e in (6, 7):
            self.finish_gather(e - 5, g)
            if e == 6:
                self.own_copy(g).wait()
            self.start_gather(e - 4, g)
        elif e == 8:
            self.finish_gather(3, g)
            self.last(g).start()
        else:
            copy = self.last(g)
            copy.wait_send()
            copy.wait_recv()

    def tick(self, t):
        for e in reversed(range(10)):
            g = t - self.starts[e]

            @pl.when((g >= 0) & (g < self.groups))
            def _():
                self.stage(e, g)


class FlatExchange(Exchange):
    def part(self, whole, g, start, size):
        start = lax.rem(g, 2) * self.rows + start
        return whole.at[lax.div(g, 2), :, pl.ds(pl.multiple_of(start, 8), size)]

    def sent_half(self, g):
        return self.part(self.source, g, (1 - self.side(g)) * self.half, self.half)

    def load(self, g):
        k = lax.rem(g, self.slots)
        own = self.part(self.source, g, self.side(g) * self.half, self.half)
        return pltpu.make_async_copy(own, self.held(g), self.refs.load_s.at[k])

    def prepare(self, g):
        self.load(g).start()

    def settle(self, g):
        self.load(g).wait()

    def result(self, g, start, size):
        return self.part(self.target, g, start, size)


ROWS = 256


def dot(a, b, dims):
    return lax.dot_general(a, b, (dims, ((), ())), preferred_element_type=jnp.float32)


NN = ((1,), (0,))
NT = ((1,), (1,))
TN = ((0,), (0,))


def gelu_slope(x):
    t = jnp.tanh(0.7978845608028654 * (x + 0.044715 * x * x * x))
    return 0.5 * (1.0 + t) + 0.5 * x * (1.0 - t * t) * (
        0.7978845608028654 * (1.0 + 3.0 * 0.044715 * x * x)
    )


def norm_parts(h):
    centre = h - jnp.mean(h, axis=-1, keepdims=True)
    r = lax.rsqrt(jnp.mean(centre * centre, axis=-1, keepdims=True) + 1e-05)
    return centre * r, r


GAIN, SHIFT, BRANCH, HIDDEN, OFFSETS, SMALL = 0, 2, 4, 6, 8, 16
PIECES = 21
ATTEND = range(11, 17)
LATE = {1: ((1, 1),), 2: ((0, 2),), 3: ((1, 3),), 7: ((1, 5),), 8: ((0, 6), (1, 7)), 10: ((0, 8),)}
PER_LAYER = 12


ACT, PRE, NORM, H, ATT, Q, K, V = "act", "pre", "norm", "h", "att", "q", "k", "v"
W_SHRINK, W_EXPAND, W_MERGE, W_HEADS = "w_shrink", "w_expand", "w_merge", "w_heads"
NORM1, NORM2, H_MID = "norm1", "norm2", "h_mid"
SHRINK, EXPAND, MERGE, HEADS = "shrink", "expand", "merge", "heads"


class Backward(FlatExchange):
    LOADS = (ACT, PRE, NORM, H, ATT, Q, K, V, W_SHRINK, W_EXPAND, W_MERGE, W_HEADS)

    def more_scratch(self):
        T, D, W, F = self.T, self.D, self.W, self.F
        low, full = jnp.bfloat16, jnp.float32
        dma = pltpu.SemaphoreType.DMA
        return dict(
            act=pltpu.VMEM((T, F), low), pre=pltpu.VMEM((T, F), full), norm=pltpu.VMEM((T, D), low),
            h=pltpu.VMEM((T, D), full), att=pltpu.VMEM((T, W), low), q=pltpu.VMEM((T, W), low),
            k=pltpu.VMEM((T, W), low), v=pltpu.VMEM((T, W), low), w_shrink=pltpu.VMEM((F, D), low),
            w_expand=pltpu.VMEM((D, F), low), w_merge=pltpu.VMEM((W, D), low), w_heads=pltpu.VMEM((3, D, W), low),
            g=pltpu.VMEM((T, D), full), low=pltpu.VMEM((T, D), low), came=pltpu.VMEM((T, D), full),
            datt=pltpu.VMEM((T, W), low), dqkv=pltpu.VMEM((3, T, W), low),
            staged=pltpu.VMEM((2, 2, 384, 384), full), dk=pltpu.VMEM((T, 128), full), dv=pltpu.VMEM((T, 128), full),
            small=pltpu.VMEM((2 * SMALL, D), full), small_in=pltpu.VMEM((4, 2 * SMALL, D), full),
            input_s=dma((len(self.LOADS),)), cot_s=dma, staged_s=dma((2,)), tokens_s=dma,
            core_s=dma((T // ROWS,)), core_r=dma((T // ROWS,)), core_c=pltpu.SemaphoreType.REGULAR,
            small_s=dma((4,)), small_r=dma((4,)),
        )

    def held_slots(self):
        return self.starts[6]

    def held(self, g):
        return self.refs.held.at[lax.rem(g, self.held_slots())]

    def fetch(self, name, layer, second=False):
        source = self.inputs[name][layer]
        if name in (NORM, H):
            source = source[1 if second else 0]
        pltpu.make_async_copy(source, getattr(self.refs, name), self.refs.input_s.at[self.LOADS.index(name)]).start()

    def arrive(self, name):
        source = self.inputs[name][0]
        if name in (NORM, H):
            source = source[0]
        pltpu.make_async_copy(source, getattr(self.refs, name), self.refs.input_s.at[self.LOADS.index(name)]).wait()

    def fetch_next(self, l, *names, second=False):
        @pl.when(l == 1)
        def _():
            for name in names:
                self.fetch(name, 0, second)

    def stage_copy(self, at, g):
        return pltpu.make_async_copy(self.refs.staged.at[at], self.source.at[g], self.refs.staged_s.at[at])

    def core_copy(self, i):
        r = self.refs
        rows = pl.ds(pl.multiple_of(i * ROWS, ROWS), ROWS)
        return self.copy(
            r.pre.at[rows, pl.ds(0, self.D)], r.came.at[rows], r.core_s.at[i], r.core_r.at[i],
            (self.dp, 1 - self.core),
        )

    def partial(self, make, wait):
        @pl.when(wait)
        def _():
            pl.semaphore_wait(self.refs.core_c, 1)

        def block(i, carry):
            rows = pl.ds(pl.multiple_of(i * ROWS, ROWS), ROWS)
            self.refs.pre[rows, 0 : self.D] = make(rows)
            self.core_copy(i).start()
            return carry

        lax.fori_loop(0, self.T // ROWS, block, 0)

    def norm_back(self, l, which, more, after):
        r, D = self.refs, self.D
        gain = self.gain[l, which : which + 1]
        n = 128
        blocks = ROWS // n

        def block(i, carry):
            @pl.when(lax.rem(i, blocks) == 0)
            def _():
                copy = self.core_copy(lax.div(i, blocks))
                copy.wait_send()
                copy.wait_recv()

            rows = pl.ds(pl.multiple_of(i * n, n), n)
            xhat, rstd = norm_parts(r.h[rows])
            d = r.pre[rows, 0:D] + r.came[rows]
            e = d * gain
            spread = xhat * jnp.mean(e * xhat, axis=-1, keepdims=True)
            new = r.g[rows] + rstd * (e - jnp.mean(e, axis=-1, keepdims=True) - spread)
            r.g[rows] = new
            rounded = new.astype(jnp.bfloat16)
            r.low[rows] = rounded
            return (
                carry[0] + jnp.sum(d * xhat, axis=0, keepdims=True),
                carry[1] + jnp.sum(d, axis=0, keepdims=True),
                carry[2] + jnp.sum(rounded.astype(jnp.float32), axis=0, keepdims=True),
            )

        zero = jnp.zeros((1, D), jnp.float32)
        sums = lax.fori_loop(0, self.T // n, block, (zero, zero, zero))
        self.row(l, GAIN + which)[...] = sums[0]
        self.row(l, SHIFT + which)[...] = sums[1]
        after(sums[2])

        @pl.when(more)
        def _():
            pl.semaphore_signal(
                r.core_c, inc=1, device_id=(self.dp, 1 - self.core), device_id_type=MESH
            )

    def row(self, l, at, start=0, size=None):
        size = self.D if size is None else size
        return self.refs.small.at[pl.ds(l * SMALL + at, 1), start : start + size]

    def outer(self, left, left_at, right, right_at, at, job):
        for u in range(2):
            a = left[:, pl.ds(pl.multiple_of(left_at + u * UNIT, 128), UNIT)]
            self.refs.staged[at, u] = dot(a, right[:, right_at * UNIT : (right_at + 1) * UNIT], TN)
        self.stage_copy(at, job).start()

    def shrink_job(self, i, job):
        self.outer(self.refs.act, i // 2 * 2 * UNIT, self.refs.low, i % 2, i % 2, job)

    def expand_job(self, i, job):
        self.outer(self.refs.norm, 0, self.refs.act, i, i % 2, job)

    def slopes(self, first, last, l):
        r, F, D = self.refs, self.F, self.D

        def one(i, carry):
            rows = pl.ds(pl.multiple_of(i * ROWS, ROWS), ROWS)
            sums = []
            for c in range(0, F, 512):
                d_act = dot(r.low[rows], r.w_shrink[c : c + 512], NT)
                d_pre = (d_act * gelu_slope(r.pre[rows, c : c + 512])).astype(jnp.bfloat16)
                r.act[rows, c : c + 512] = d_pre
                sums.append(carry[c // 512] + jnp.sum(d_pre.astype(jnp.float32), axis=0, keepdims=True))
            return tuple(sums)

        sums = lax.fori_loop(first, last, one, (jnp.zeros((1, 512), jnp.float32),) * (F // 512))
        for i, part in enumerate(sums):
            for j in range(2):
                at = i * 512 + j * 256
                row = self.row(l, HIDDEN + at // D, at % D, 256)
                row[...] = row[...] + part[:, j * 256 : (j + 1) * 256]

    def piece(self, p, l):
        r = self.refs
        T, W = self.T, self.W
        blocks = T // ROWS
        base = (1 - l) * PER_LAYER
        for q, job in LATE.get(p - 1, ()):
            self.stage_copy(q, base + job).wait()
        if p == 0:
            self.arrive(ACT)

            @pl.when(l == 1)
            def _():
                pltpu.make_async_copy(self.cotangent, r.low, r.cot_s).wait()
                for name in self.LOADS[1:]:
                    self.fetch(name, 1, second=True)

            self.shrink_job(0, base)
            self.stage_copy(0, base).wait()
        elif p in (1, 2, 3):
            self.shrink_job(p, base + p)
        elif p == 4:
            @pl.when(l == 1)
            def _():
                def widen(i, carry):
                    rows = pl.ds(pl.multiple_of(i * ROWS, ROWS), ROWS)
                    wide = r.low[rows].astype(jnp.float32)
                    r.g[rows] = wide
                    return carry + jnp.sum(wide, axis=0, keepdims=True)

                self.row(l, BRANCH + 1)[...] = lax.fori_loop(0, blocks, widen, jnp.zeros((1, self.D), jnp.float32))

            self.arrive(W_SHRINK)
            self.arrive(PRE)
            self.slopes(0, blocks // 2, l)
        elif p == 5:
            self.slopes(blocks // 2, blocks, l)
            self.fetch_next(l, W_SHRINK)
        elif p == 6:
            self.arrive(W_EXPAND)
            self.partial(lambda rows: dot(r.act[rows], r.w_expand[...], NT), l == 0)
        elif p == 7:
            self.arrive(NORM)
            self.expand_job(0, base + 4)
            self.expand_job(1, base + 5)
            self.stage_copy(0, base + 4).wait()
        elif p == 8:
            self.expand_job(2, base + 6)
            self.expand_job(3, base + 7)
            self.fetch_next(l, W_EXPAND, ACT)
            for layer in range(2):
                @pl.when(l == layer)
                def _():
                    self.fetch(NORM, layer)
        elif p == 9:
            self.arrive(H)

            def after(total):
                self.row(l, BRANCH)[...] = total

            self.norm_back(l, 1, jnp.bool_(True), after)
            for layer in range(2):
                @pl.when(l == layer)
                def _():
                    self.fetch(H, layer)
        elif p == 10:
            self.arrive(W_MERGE)
            self.arrive(ATT)

            def one(i, carry):
                rows = pl.ds(pl.multiple_of(i * ROWS, ROWS), ROWS)
                r.datt[rows] = dot(r.low[rows], r.w_merge[...], NT).astype(jnp.bfloat16)
                return carry

            lax.fori_loop(0, blocks, one, 0)
            for u in range(2):
                r.staged[0, u] = dot(r.att[...], r.low[:, u * UNIT : (u + 1) * UNIT], TN)
            self.stage_copy(0, base + 8).start()
        elif p in ATTEND:
            if p == ATTEND[0]:
                self.fetch_next(l, W_MERGE, ATT)
                self.arrive(Q)
                self.arrive(K)
                self.arrive(V)
            i = p - ATTEND[0]
            self.attend_back(i // 2, l, i % 2)
            if p == ATTEND[-1]:
                self.fetch_next(l, Q, K, V)
        elif p == 17:
            self.arrive(W_HEADS)

            def make(rows):
                total = dot(r.dqkv[0, rows], r.w_heads[0], NT)
                for c in (1, 2):
                    total = total + dot(r.dqkv[c, rows], r.w_heads[c], NT)
                return total

            self.partial(make, jnp.bool_(True))
            self.fetch_next(l, W_HEADS)
        elif p == 18:
            self.arrive(NORM)
            self.heads_job(0, base + 9)
            self.stage_copy(0, base + 9).wait()
        elif p == 19:
            self.heads_job(1, base + 10)
            self.heads_job(2, base + 11)
            for i, c in enumerate((0, 2)):
                self.row(l, OFFSETS, i * W, W)[...] = jnp.sum(r.dqkv[c].astype(jnp.float32), axis=0, keepdims=True)
            self.fetch_next(l, NORM, second=True)
            for c in (1, 2):
                self.stage_copy(c % 2, base + 9 + c).wait()
        else:
            self.arrive(H)

            def after(total):
                @pl.when(l == 1)
                def _():
                    self.row(0, BRANCH + 1)[...] = total

            self.norm_back(l, 0, l == 1, after)
            self.fetch_next(l, PRE)
            self.fetch_next(l, H, second=True)

            @pl.when(l == 0)
            def _():
                pltpu.make_async_copy(r.low, self.grad_tokens, r.tokens_s).start()

    def heads_job(self, c, job):
        r = self.refs
        for u in range(2):
            r.staged[c % 2, u] = dot(r.norm[:, u * UNIT : (u + 1) * UNIT], r.dqkv[c], TN)
        self.stage_copy(c % 2, job).start()

    def attend_back(self, pair, l, turn):
        r = self.refs
        T = self.T
        lanes = slice(pair * 128, (pair + 1) * 128)
        if turn == 0:
            r.dk[...] = jnp.zeros((T, 128), jnp.float32)
            r.dv[...] = jnp.zeros((T, 128), jnp.float32)
        lane = lax.broadcasted_iota(jnp.int32, (1, 128), 1)
        blocks = T // ROWS
        for b in range(blocks - 1) if turn == 0 else (blocks - 1,):
            rows, end = slice(b * ROWS, (b + 1) * ROWS), (b + 1) * ROWS
            query = b * ROWS + lax.broadcasted_iota(jnp.int32, (1, ROWS), 1)
            lowest = query - jnp.concatenate([self.positions[j : j + 1] for j in range(2 * b, 2 * b + 2)], axis=1)
            key = lax.broadcasted_iota(jnp.int32, (end, ROWS), 0)
            allowed = (key <= query) & (key >= lowest)
            q, d = r.q[rows, lanes], r.datt[rows, lanes]
            k, v = r.k[0:end, lanes], r.v[0:end, lanes]
            dq = jnp.zeros((ROWS, 128), jnp.float32)
            for side in range(2):
                mine = (lax.div(lane, 64) == side).astype(jnp.float32).astype(jnp.bfloat16)
                q_own, d_own = q * mine, d * mine
                scores = dot(k, q_own, NT) * 0.125
                lse = self.lse[l, pair * 2 + side : pair * 2 + side + 1, rows]
                probs = jnp.where(allowed, jnp.exp(scores - lse), 0.0)
                dprob = dot(v, d_own, NT)
                centre = jnp.sum(probs * dprob, axis=0, keepdims=True)
                dscore = (probs * (dprob - centre)).astype(jnp.bfloat16)
                r.dv[0:end] = r.dv[0:end] + dot(probs.astype(jnp.bfloat16), d_own, NN)
                r.dk[0:end] = r.dk[0:end] + dot(dscore, q_own, NN)
                dq = dq + dot(dscore, k * mine, TN)
            r.dqkv[0, rows, lanes] = (dq * 0.125).astype(jnp.bfloat16)
        if turn == 1:
            r.dqkv[1, :, lanes] = (r.dk[...] * 0.125).astype(jnp.bfloat16)
            r.dqkv[2, :, lanes] = r.dv[...].astype(jnp.bfloat16)

    def small_swap(self, step):
        r = self.refs
        z = self.z
        to = (
            self.dp + self.step_x,
            self.dp + self.step_y,
            self.dp + 4 - 8 * lax.rem(z, 2),
            self.dp + 8 - 16 * lax.div(z, 2),
        )[step]
        return self.copy(
            r.small, r.small_in.at[step], r.small_s.at[step], r.small_r.at[step], (to, self.core)
        )

    def small_stage(self, step):
        if step > 0:
            copy = self.small_swap(step - 1)
            copy.wait_send()
            copy.wait_recv()
            self.refs.small[...] = self.refs.small[...] + self.refs.small_in[step - 1]
        if step < 4:
            self.small_swap(step).start()

    def run(self):
        r = self.refs
        pltpu.make_async_copy(self.cotangent, r.low, r.cot_s).start()
        self.fetch(ACT, 1)
        r.small[...] = jnp.zeros(r.small.shape, jnp.float32)
        far = (self.dp + 8 - 16 * lax.div(self.z, 2), self.core)
        self.barrier(((self.dp, 1 - self.core), far))

        def step(t, carry):
            l = 1 - lax.div(t, PIECES)
            for p in range(PIECES):
                @pl.when((lax.rem(t, PIECES) == p) & (t < 2 * PIECES))
                def _():
                    self.piece(p, l)

            for s in range(5):
                @pl.when(t == 2 * PIECES + s)
                def _():
                    self.small_stage(s)

            self.tick(t)
            return carry

        lax.fori_loop(0, self.ticks, step, 0)
        pltpu.make_async_copy(r.low, self.grad_tokens, r.tokens_s).wait()
        self.small_out[...] = r.small[...]


def backward(kept, weights, gain, lse, positions, cotangent, slots=6, lags=(4, 2, 2, 2, 2, 2, 2, 2, 4)):
    D = cotangent.shape[1]
    _, T, W = kept[1].shape
    jobs = 2 * PER_LAYER
    plan = Backward(2 * jobs, UNIT // 2, UNIT, slots, lags)
    plan.T, plan.D, plan.W, plan.F = T, D, W, weights[0].shape[1]
    scratch = plan.scratch() | plan.more_scratch()
    n = len(kept)

    def kernel(*refs):
        layers = [[ref.at[i] for i in range(2)] for ref in refs[:n]]
        norm1, q, k, v, att, h_mid, norm2, pre, act, h = layers
        plan.inputs = dict(zip(plan.LOADS, (act, pre, list(zip(norm1, norm2)), list(zip(h, h_mid)), att, q, k, v)))
        for name, weight in zip((W_SHRINK, W_EXPAND, W_MERGE, W_HEADS), refs[n : n + 4]):
            plan.inputs[name] = [weight.at[i] for i in range(2)]
        plan.cotangent, plan.gain, plan.lse, plan.positions = refs[n + 4 : n + 8]
        plan.target, plan.source, plan.grad_tokens, plan.small_out = refs[n + 8 : n + 12]
        plan.setup(SimpleNamespace(**dict(zip(scratch, refs[n + 12 :]))))
        plan.run()

    hbm = pl.BlockSpec(memory_space=pl.ANY)
    vmem = pl.BlockSpec(memory_space=pltpu.VMEM)
    flat = jax.ShapeDtypeStruct((jobs, 2, UNIT, UNIT), jnp.float32)
    target, _, grad_tokens, small = pl.pallas_call(
        kernel,
        out_shape=(
            flat,
            flat,
            jax.ShapeDtypeStruct((T, D), jnp.bfloat16),
            jax.ShapeDtypeStruct((2 * SMALL, D), jnp.float32),
        ),
        in_specs=[hbm] * (n + 5) + [vmem] * 3,
        out_specs=(hbm, hbm, hbm, vmem),
        scratch_shapes=list(scratch.values()),
        compiler_params=pltpu.CompilerParams(
            collective_id=0, has_side_effects=True, vmem_limit_bytes=61 * 2**20
        ),
    )(*kept, *weights, cotangent, gain, lse, positions)
    return target, grad_tokens, small


def gelu(x):
    return 0.5 * x * (1.0 + jnp.tanh(0.7978845608028654 * (x + 0.044715 * x * x * x)))


class Forward:
    KEPT = (NORM1, Q, K, V, ATT, H_MID, NORM2, PRE, ACT, H)

    WEIGHTS = (HEADS, MERGE, EXPAND, SHRINK)

    def scratch(self):
        T, D, W, F = self.T, self.D, self.W, self.F
        low, full = jnp.bfloat16, jnp.float32
        dma = pltpu.SemaphoreType.DMA
        n = T // ROWS
        return dict(
            norm1=pltpu.VMEM((T, D), low), q=pltpu.VMEM((T, W), low), k=pltpu.VMEM((T, W), low), v=pltpu.VMEM((T, W), low),
            att=pltpu.VMEM((T, W), low), h_mid=pltpu.VMEM((T, D), full), norm2=pltpu.VMEM((T, D), low),
            pre=pltpu.VMEM((T, F), full), act=pltpu.VMEM((T, F), low), h=pltpu.VMEM((T, D), full),
            low=pltpu.VMEM((T, D), low), part=pltpu.VMEM((2, T, D), full), came=pltpu.VMEM((2, T, D), full),
            bias=pltpu.VMEM((n, ROWS, T), full),
            heads=pltpu.VMEM((2, 3, D, W), low), merge=pltpu.VMEM((2, W, D), low),
            expand=pltpu.VMEM((2, D, F), low), shrink=pltpu.VMEM((2, F, D), low),
            kept_s=dma((len(self.KEPT), n)), weight_s=dma((4, 2)), token_s=dma, out_s=dma((n,)),
            core_s=dma((2, n)), core_r=dma((2, n)),
        )

    def rows(self, b):
        return pl.ds(pl.multiple_of(b * ROWS, ROWS), ROWS)

    def keep_copy(self, name, l, b):
        at = self.rows(b)
        return pltpu.make_async_copy(
            getattr(self.refs, name).at[at], self.kept[name].at[l, at], self.refs.kept_s.at[self.KEPT.index(name), b]
        )

    def free(self, l, b, *names):
        @pl.when(l == 1)
        def _():
            for name in names:
                self.keep_copy(name, 0, b).wait()

    def keep(self, l, b, *names):
        for name in names:
            self.keep_copy(name, l, b).start()

    def weight_copy(self, name, l):
        at = self.WEIGHTS.index(name)
        return pltpu.make_async_copy(self.weights[name].at[l], getattr(self.refs, name).at[l], self.refs.weight_s.at[at, l])

    def core_copy(self, kind, b):
        r, at = self.refs, self.rows(b)
        return pltpu.make_async_remote_copy(
            src_ref=r.part.at[kind, at], dst_ref=r.came.at[kind, at],
            send_sem=r.core_s.at[kind, b], recv_sem=r.core_r.at[kind, b],
            device_id=(lax.axis_index("dp"), 1 - lax.axis_index("tensor")), device_id_type=MESH,
        )

    def summed(self, kind, b):
        copy = self.core_copy(kind, b)
        copy.wait_send()
        copy.wait_recv()
        at = self.rows(b)
        return self.refs.part[kind, at] + self.refs.came[kind, at]

    def norm(self, x, l, which):
        xhat, _ = norm_parts(x)
        return (xhat * self.gain[l, which : which + 1] + self.shift[l, which : which + 1]).astype(jnp.bfloat16)

    def first(self, l, b):
        r, at = self.refs, self.rows(b)
        W = self.W
        self.free(l, b, H)

        @pl.when(l == 0)
        def _():
            r.h[at] = r.low[at].astype(jnp.float32)

        @pl.when(l == 1)
        def _():
            r.h[at] = r.h_mid[at] + (self.summed(1, b) + self.branch[0, 1:2])

        self.free(l, b, NORM1, Q, K, V, ATT)
        low = self.norm(r.h[at], l, 0)
        r.norm1[at] = low
        r.q[at] = (dot(low, r.heads[l, 0], NN) + self.offsets[l, 0:1]).astype(jnp.bfloat16)
        r.k[at] = dot(low, r.heads[l, 1], NN).astype(jnp.bfloat16)
        r.v[at] = (dot(low, r.heads[l, 2], NN) + self.offsets[l, 1:2]).astype(jnp.bfloat16)
        for i in range(self.T // ROWS):
            @pl.when(b == i)
            def _():
                self.attend(l, i)

        r.part[0, at] = dot(r.att[at], r.merge[l], NN)
        self.core_copy(0, b).start()
        self.keep(l, b, H, NORM1, Q, K, V, ATT)

    def attend(self, l, b):
        r = self.refs
        rows, end = slice(b * ROWS, (b + 1) * ROWS), (b + 1) * ROWS

        @pl.when(l == 0)
        def _():
            query = b * ROWS + lax.broadcasted_iota(jnp.int32, (ROWS, 1), 0)
            spread = jnp.concatenate([self.positions[...].astype(jnp.float32)] * 16, axis=0).T
            column = jnp.concatenate([spread[:, j : j + 1] for j in range(2 * b, 2 * b + 2)], axis=0)
            lowest = query - column.astype(jnp.int32)
            key = lax.broadcasted_iota(jnp.int32, (ROWS, end), 1)
            r.bias[b, :, 0:end] = jnp.where((key <= query) & (key >= lowest), 0.0, -1e30)

        lane = lax.broadcasted_iota(jnp.int32, (1, 128), 1)
        logs = jnp.zeros((ROWS, 128), jnp.float32)
        for pair in range(self.W // 128):
            lanes = slice(pair * 128, (pair + 1) * 128)
            q, k, v = r.q[rows, lanes], r.k[0:end, lanes], r.v[0:end, lanes]
            total = jnp.zeros((ROWS, 128), jnp.float32)
            for side in range(2):
                mine = (lax.div(lane, 64) == side).astype(jnp.float32)
                scores = dot(q * (mine * 0.125).astype(jnp.bfloat16), k, NT) + r.bias[b, :, 0:end]
                highest = jnp.max(scores, axis=-1, keepdims=True)
                weights = jnp.exp(scores - highest)
                amount = jnp.sum(weights, axis=-1, keepdims=True)
                probs = (weights * (1.0 / amount)).astype(jnp.bfloat16)
                total = total + dot(probs, v * mine.astype(jnp.bfloat16), NN)
                logs = jnp.where(lane == pair * 2 + side, highest + jnp.log(amount), logs)
            r.att[rows, lanes] = total.astype(jnp.bfloat16)
        self.lse[l, :, rows] = logs.T[0:8]

    def second(self, l, b):
        r, at = self.refs, self.rows(b)
        self.free(l, b, H_MID, NORM2, PRE, ACT)
        middle = r.h[at] + (self.summed(0, b) + self.branch[l, 0:1])
        r.h_mid[at] = middle
        low = self.norm(middle, l, 1)
        r.norm2[at] = low
        for c in range(0, self.F, 512):
            pre = dot(low, r.expand[l, :, c : c + 512], NN) + self.hidden[pl.ds(l, 1), c : c + 512]
            r.pre[at, c : c + 512] = pre
            r.act[at, c : c + 512] = gelu(pre).astype(jnp.bfloat16)
        r.part[1, at] = dot(r.act[at], r.shrink[l], NN)
        self.core_copy(1, b).start()
        self.keep(l, b, H_MID, NORM2, PRE, ACT)

    def finish(self, b):
        r, at = self.refs, self.rows(b)
        r.low[at] = (r.h_mid[at] + (self.summed(1, b) + self.branch[1, 1:2])).astype(jnp.bfloat16)
        pltpu.make_async_copy(r.low.at[at], self.output.at[at], r.out_s.at[b]).start()

    def run(self):
        r = self.refs
        n = self.T // ROWS
        load = pltpu.make_async_copy(self.tokens, r.low, r.token_s)
        load.start()
        for name in self.WEIGHTS:
            self.weight_copy(name, 0).start()
        other = (lax.axis_index("dp"), 1 - lax.axis_index("tensor"))
        bar = pltpu.get_barrier_semaphore()
        pl.semaphore_signal(bar, inc=1, device_id=other, device_id_type=MESH)
        pl.semaphore_wait(bar, 1)
        load.wait()

        def turn(t, carry):
            for l in range(2):
                @pl.when(t == l * n)
                def _():
                    self.weight_copy(HEADS, l).wait()
                    self.weight_copy(MERGE, l).wait()

            @pl.when(t < 2 * n)
            def _():
                self.first(lax.div(t, n), lax.rem(t, n))

            for l in range(2):
                @pl.when(t == l * n + 1)
                def _():
                    self.weight_copy(EXPAND, l).wait()
                    self.weight_copy(SHRINK, l).wait()

            @pl.when(t == 1)
            def _():
                for name in self.WEIGHTS:
                    self.weight_copy(name, 1).start()

            @pl.when((t >= 1) & (t < 2 * n + 1))
            def _():
                self.second(lax.div(t - 1, n), lax.rem(t - 1, n))

            @pl.when(t >= n + 2)
            def _():
                self.finish(t - n - 2)

            return carry

        lax.fori_loop(0, 2 * n + 2, turn, 0)
        for b in range(n):
            for name in self.KEPT:
                self.keep_copy(name, 1, b).wait()
            pltpu.make_async_copy(r.low.at[self.rows(b)], self.output.at[self.rows(b)], r.out_s.at[b]).wait()


def forward(tokens, positions, weights, rows):
    plan = Forward()
    T, D = tokens.shape
    plan.T, plan.D, plan.W, plan.F = T, D, weights[0].shape[3], weights[2].shape[2]
    scratch = plan.scratch()
    kinds = plan.KEPT

    def kernel(tokens, heads, merge, expand, shrink, positions, gain, shift, offsets, branch, hidden, output, lse, *refs):
        plan.tokens, plan.positions, plan.output, plan.lse = tokens, positions, output, lse
        plan.weights = dict(zip(plan.WEIGHTS, (heads, merge, expand, shrink)))
        plan.gain, plan.shift, plan.offsets, plan.branch, plan.hidden = gain, shift, offsets, branch, hidden
        plan.kept = dict(zip(kinds, refs))
        plan.refs = SimpleNamespace(**dict(zip(scratch, refs[len(kinds) :])))
        plan.run()

    hbm = pl.BlockSpec(memory_space=pl.ANY)
    vmem = pl.BlockSpec(memory_space=pltpu.VMEM)
    kept_shapes = [jax.ShapeDtypeStruct((2,) + scratch[name].shape, scratch[name].dtype) for name in kinds]
    out = pl.pallas_call(
        kernel,
        out_shape=[jax.ShapeDtypeStruct((T, D), jnp.bfloat16), jax.ShapeDtypeStruct((2, 8, T), jnp.float32)] + kept_shapes,
        in_specs=[hbm] * 5 + [vmem] * 6,
        out_specs=[hbm, vmem] + [hbm] * len(kept_shapes),
        scratch_shapes=list(scratch.values()),
        compiler_params=pltpu.CompilerParams(
            collective_id=1, has_side_effects=True, vmem_limit_bytes=61 * 2**20
        ),
    )(tokens, *weights, positions, *rows)
    return out[0], out[1], out[2:]


def spread(flat, small, shapes, dtype=jnp.float32):
    half = flat.shape[0] // 2
    width = small.shape[1]

    def kernel(source, sums, gain, shift, heads, offsets, merge, branch, expand, hidden, shrink, held, into, out):
        loads, copies = [], []

        def put(g, u, target):
            i = len(copies)
            loads.append(pltpu.make_async_copy(source.at[g, u], held.at[i], into.at[i]))
            copies.append(pltpu.make_async_copy(held.at[i], target, out.at[i]))
            loads[-1].start()

        for l in range(2):
            base = (1 - l) * half
            for u in range(2):
                rows = pl.ds(u * UNIT, UNIT)
                for i in range(4):
                    at = pl.ds((i // 2) * 2 * UNIT + u * UNIT, UNIT)
                    put(base + i, u, shrink.at[l, at, pl.ds((i % 2) * UNIT, UNIT)])
                    put(base + 4 + i, u, expand.at[l, rows, pl.ds(i * UNIT, UNIT)])
                put(base + 8, u, merge.at[l, :, rows])
                for c in range(3):
                    put(base + 9 + c, u, heads.at[l, c, rows])
            for target, at in ((gain, GAIN), (shift, SHIFT), (branch, BRANCH)):
                target[l] = sums[l * SMALL + at : l * SMALL + at + 2]
            for i in range(2):
                at = l * SMALL + HIDDEN + i
                hidden[l : l + 1, i * width : (i + 1) * width] = sums[at : at + 1]
                at = l * SMALL + OFFSETS
                offsets[l, i : i + 1] = sums[at : at + 1, i * UNIT : (i + 1) * UNIT]
        for load, copy in zip(loads, copies):
            load.wait()
            copy.start()
        for copy in copies:
            copy.wait()

    hbm = pl.BlockSpec(memory_space=pl.ANY)
    vmem = pl.BlockSpec(memory_space=pltpu.VMEM)
    return pl.pallas_call(
        kernel,
        out_shape=[jax.ShapeDtypeStruct(s, dtype) for s in shapes],
        in_specs=[hbm, vmem],
        out_specs=[vmem, vmem, hbm, vmem, hbm, vmem, hbm, vmem, hbm],
        scratch_shapes=[
            pltpu.VMEM((2 * flat.shape[0], UNIT, UNIT), dtype),
            pltpu.SemaphoreType.DMA((2 * flat.shape[0],)),
            pltpu.SemaphoreType.DMA((2 * flat.shape[0],)),
        ],
        compiler_params=pltpu.CompilerParams(has_side_effects=True, vmem_limit_bytes=48 * 2**20),
    )(flat, small)


def on_device(
    tokens,
    positions,
    norm_gain,
    norm_shift,
    heads_weight,
    offsets,
    merge_weight,
    branch_bias,
    expand_weight,
    hidden_bias,
    shrink_weight,
    cotangent,
):
    rows = (norm_gain, norm_shift, offsets, branch_bias, hidden_bias)
    places = positions.reshape(-1, 128)
    output, lse, kept = forward(
        tokens, places, (heads_weight, merge_weight, expand_weight, shrink_weight), rows
    )
    flat, grad_tokens, small = backward(
        kept, (shrink_weight, expand_weight, merge_weight, heads_weight), norm_gain, lse, places, cotangent
    )
    ranks = lax.axis_size("dp")
    if ranks > BLOCK:
        groups = [[j * BLOCK + i for j in range(ranks // BLOCK)] for i in range(BLOCK)]
        flat, small = lax.psum((flat, small), "dp", axis_index_groups=groups)
    shapes = [norm_gain, norm_shift, heads_weight, offsets, merge_weight, branch_bias, expand_weight, hidden_bias, shrink_weight]
    return (output, grad_tokens, *spread(flat, small, [like.shape for like in shapes]))


def solution(mesh):
    placed = (
        P("dp", None),
        P("dp"),
        P(),
        P(),
        P(None, None, None, "tensor"),
        P(None, None, "tensor"),
        P(None, "tensor", None),
        P(),
        P(None, None, "tensor"),
        P(None, "tensor"),
        P(None, "tensor", None),
        P("dp", None),
    )
    return jax.shard_map(
        on_device,
        mesh=mesh,
        in_specs=placed,
        out_specs=(
            P("dp", None),
            P("dp", None),
            P(),
            P(),
            P(None, None, None, "tensor"),
            P(None, None, "tensor"),
            P(None, "tensor", None),
            P(),
            P(None, None, "tensor"),
            P(None, "tensor"),
            P(None, "tensor", None),
        ),
        check_vma=False,
    )
```

```python
from types import SimpleNamespace

import jax
import jax.numpy as jnp
from jax import lax
from jax.experimental import pallas as pl
from jax.experimental.pallas import tpu as pltpu
from jax.sharding import PartitionSpec as P

LAYERS = 2
UNIT = 384
BLOCK = 16
MESH = pl.DeviceIdType.MESH


class Exchange:
    def __init__(self, groups, rows, cols, slots, lags):
        self.groups, self.rows, self.cols, self.slots = groups, rows, cols, slots
        self.half = rows // 2
        self.chunk = self.half // 4
        starts = [0]
        for lag in lags:
            starts.append(starts[-1] + lag)
        self.starts = starts
        self.ticks = groups + starts[-1]
        self.last_slots = starts[9]
        self.gather_slots = max(starts[8] - starts[1], slots)

    def scratch(self):
        groups, slots, half, chunk, cols = self.groups, self.slots, self.half, self.chunk, self.cols
        dma = pltpu.SemaphoreType.DMA
        plain = pltpu.SemaphoreType.REGULAR
        return dict(
            held=pltpu.VMEM((self.held_slots(), 2, half, cols), jnp.float32),
            swap_in=pltpu.VMEM((slots, 2, half, cols), jnp.float32),
            chain_in=pltpu.VMEM((slots, 3, 2, 2, chunk, cols), jnp.float32),
            third_in=pltpu.VMEM((slots, 2, chunk, cols), jnp.float32),
            swap_s=dma((slots,)), swap_r=dma((slots,)),
            chain_s=dma((slots, 3, 2)), chain_r=dma((slots, 3, 2)),
            third_s=dma((slots,)), third_r=dma((slots,)),
            gather_s=dma((slots, 3, 2)), gather_r=dma((self.gather_slots, 3, 2)),
            last_s=dma((slots,)), last_r=dma((self.last_slots,)),
            own_s=dma((slots,)), load_s=dma((slots,)),
            swap_c=plain((2,)), chain_c=plain((3, 2)), third_c=plain((2,)),
        )

    def held_slots(self):
        return self.groups

    def setup(self, refs):
        self.refs = refs
        dp = lax.axis_index("dp")
        core = lax.axis_index("tensor")
        low = lax.rem(dp, 16)
        self.dp, self.core = dp, core
        self.z = lax.div(low, 4)
        self.y = lax.rem(lax.div(low, 2), 2)
        self.x = lax.rem(low, 2)
        self.step_x = 1 - 2 * self.x
        self.step_y = 2 - 4 * self.y
        self.along = ((dp + 4, core), (dp - 4, core))

    def barrier(self, others=()):
        z = self.z
        bar = pltpu.get_barrier_semaphore()

        def greet(device):
            pl.semaphore_signal(bar, inc=1, device_id=device, device_id_type=MESH)

        for device in ((self.dp + self.step_x, self.core), (self.dp + self.step_y, self.core)) + tuple(others):
            greet(device)

        @pl.when(z < 3)
        def _():
            greet(self.along[0])

        @pl.when(z > 0)
        def _():
            greet(self.along[1])

        pl.semaphore_wait(bar, 2 + len(others) + (z < 3).astype(jnp.int32) + (z > 0).astype(jnp.int32))

    def first(self, g):
        return (self.dp + jnp.where(lax.rem(g, 2) == 0, self.step_x, self.step_y), self.core)

    def third(self, g):
        return (self.dp + jnp.where(lax.rem(g, 2) == 0, self.step_y, self.step_x), self.core)

    def side(self, g):
        return jnp.where(lax.rem(g, 2) == 0, self.x, self.y)

    def copy(self, src, dst, send, recv, device):
        return pltpu.make_async_remote_copy(
            src_ref=src, dst_ref=dst, send_sem=send, recv_sem=recv, device_id=device, device_id_type=MESH
        )

    def rows_of(self, j):
        return pl.ds(pl.multiple_of(j * self.chunk, 8), self.chunk)

    def held(self, g):
        return self.refs.held.at[g]

    def swap(self, g):
        r, k = self.refs, lax.rem(g, self.slots)
        return self.copy(self.sent_half(g), r.swap_in.at[k], r.swap_s.at[k], r.swap_r.at[k], self.first(g))

    def chain_send(self, step, d, g):
        z, r, k = self.z, self.refs, lax.rem(g, self.slots)
        j = 4 - step + z if d == 0 else step - 4 + z
        here = ((z < 3) & (step > z)) if d == 0 else ((z > 0) & (step > 3 - z))
        at = (k, step - 1, d)
        part = self.held(g).at[:, self.rows_of(j)]
        return here, self.copy(part, r.chain_in.at[at], r.chain_s.at[at], r.chain_r.at[at], self.along[d])

    def start_chain(self, step, g):
        for d in range(2):
            here, copy = self.chain_send(step, d, g)

            @pl.when(here)
            def _():
                @pl.when(g >= self.slots)
                def _():
                    pl.semaphore_wait(self.refs.chain_c.at[step - 1, d], 1)

                copy.start()

    def finish_chain(self, step, g):
        z, r, k = self.z, self.refs, lax.rem(g, self.slots)
        for d in range(2):
            here, copy = self.chain_send(step, d, g)

            @pl.when(here)
            def _():
                copy.wait_send()

        for d in range(2):
            here = ((z >= 1) & (step >= z)) if d == 0 else ((z <= 2) & (step >= 3 - z))
            j = 3 - step + z if d == 0 else step - 3 + z
            at = (k, step - 1, d)

            @pl.when(here)
            def _():
                came = r.chain_in.at[at]
                self.copy(came, came, r.chain_s.at[at], r.chain_r.at[at], self.along[1 - d]).wait_recv()
                part = self.held(g).at[:, self.rows_of(j)]
                part[...] = part[...] + came[...]

                @pl.when(g + self.slots < self.groups)
                def _():
                    pl.semaphore_signal(
                        r.chain_c.at[step - 1, d], inc=1, device_id=self.along[1 - d], device_id_type=MESH
                    )

    def third_swap(self, g):
        r, k = self.refs, lax.rem(g, self.slots)
        part = self.held(g).at[:, self.rows_of(self.z)]
        return self.copy(part, r.third_in.at[k], r.third_s.at[k], r.third_r.at[k], self.third(g))

    def gather_copy(self, step, d, g, j, source=None):
        r, k = self.refs, lax.rem(g, self.slots)
        part = self.result(g, self.side(g) * self.half + j * self.chunk, self.chunk)
        return self.copy(
            part if source is None else source,
            part,
            r.gather_s.at[k, step - 1, d],
            r.gather_r.at[lax.rem(g, self.gather_slots), step - 1, d],
            self.along[d],
        )

    def gather_send(self, step, d, g):
        z = self.z
        j = z - (step - 1) if d == 0 else z + step - 1
        here = ((z < 3) & (step - 1 <= z)) if d == 0 else ((z > 0) & (z + step - 1 <= 3))
        source = self.held(g).at[:, self.rows_of(z)] if step == 1 else None
        return here, self.gather_copy(step, d, g, j, source)

    def start_gather(self, step, g):
        for d in range(2):
            here, copy = self.gather_send(step, d, g)

            @pl.when(here)
            def _():
                copy.start()

    def finish_gather(self, step, g):
        z = self.z
        for d in range(2):
            here, copy = self.gather_send(step, d, g)

            @pl.when(here)
            def _():
                copy.wait_send()

        for d in range(2):
            here = (z >= step) if d == 0 else (z + step <= 3)
            j = z - step if d == 0 else z + step

            @pl.when(here)
            def _():
                self.gather_copy(step, d, g, j).wait_recv()

    def own_copy(self, g):
        k = lax.rem(g, self.slots)
        part = self.held(g).at[:, self.rows_of(self.z)]
        return pltpu.make_async_copy(
            part, self.result(g, self.side(g) * self.half + self.z * self.chunk, self.chunk), self.refs.own_s.at[k]
        )

    def last(self, g):
        r, k = self.refs, lax.rem(g, self.slots)
        part = self.result(g, self.side(g) * self.half, self.half)
        return self.copy(part, part, r.last_s.at[k], r.last_r.at[lax.rem(g, self.last_slots)], self.first(g))

    def stage(self, e, g):
        r, slots, groups = self.refs, self.slots, self.groups
        k = lax.rem(g, slots)
        if e == 0:
            self.prepare(g)

            @pl.when(g >= slots)
            def _():
                pl.semaphore_wait(r.swap_c.at[lax.rem(g, 2)], 1)

            self.swap(g).start()
        elif e == 1:
            self.settle(g)
            copy = self.swap(g)
            copy.wait_send()
            copy.wait_recv()
            mine = self.held(g)
            mine[...] = mine[...] + r.swap_in[k]

            @pl.when(g + slots < groups)
            def _():
                pl.semaphore_signal(
                    r.swap_c.at[lax.rem(g, 2)], inc=1, device_id=self.first(g), device_id_type=MESH
                )

            self.start_chain(1, g)
        elif e in (2, 3):
            self.finish_chain(e - 1, g)
            self.start_chain(e, g)
        elif e == 4:
            self.finish_chain(3, g)

            @pl.when(g >= slots)
            def _():
                pl.semaphore_wait(r.third_c.at[lax.rem(g, 2)], 1)

            self.third_swap(g).start()
        elif e == 5:
            copy = self.third_swap(g)
            copy.wait_send()
            copy.wait_recv()
            part = self.held(g).at[:, self.rows_of(self.z)]
            part[...] = part[...] + r.third_in[k]

            @pl.when(g + slots < groups)
            def _():
                pl.semaphore_signal(
                    r.third_c.at[lax.rem(g, 2)], inc=1, device_id=self.third(g), device_id_type=MESH
                )

            self.start_gather(1, g)
            self.own_copy(g).start()
        elif e in (6, 7):
            self.finish_gather(e - 5, g)
            if e == 6:
                self.own_copy(g).wait()
            self.start_gather(e - 4, g)
        elif e == 8:
            self.finish_gather(3, g)
            self.last(g).start()
        else:
            copy = self.last(g)
            copy.wait_send()
            copy.wait_recv()

    def tick(self, t):
        for e in reversed(range(10)):
            g = t - self.starts[e]

            @pl.when((g >= 0) & (g < self.groups))
            def _():
                self.stage(e, g)


class FlatExchange(Exchange):
    def part(self, whole, g, start, size):
        start = lax.rem(g, 2) * self.rows + start
        return whole.at[lax.div(g, 2), :, pl.ds(pl.multiple_of(start, 8), size)]

    def sent_half(self, g):
        return self.part(self.source, g, (1 - self.side(g)) * self.half, self.half)

    def load(self, g):
        k = lax.rem(g, self.slots)
        own = self.part(self.source, g, self.side(g) * self.half, self.half)
        return pltpu.make_async_copy(own, self.held(g), self.refs.load_s.at[k])

    def prepare(self, g):
        self.load(g).start()

    def settle(self, g):
        self.load(g).wait()

    def result(self, g, start, size):
        return self.part(self.target, g, start, size)


ROWS = 256


def dot(a, b, dims):
    return lax.dot_general(a, b, (dims, ((), ())), preferred_element_type=jnp.float32)


NN = ((1,), (0,))
NT = ((1,), (1,))
TN = ((0,), (0,))


def gelu_slope(x):
    t = jnp.tanh(0.7978845608028654 * (x + 0.044715 * x * x * x))
    return 0.5 * (1.0 + t) + 0.5 * x * (1.0 - t * t) * (
        0.7978845608028654 * (1.0 + 3.0 * 0.044715 * x * x)
    )


def norm_parts(h):
    centre = h - jnp.mean(h, axis=-1, keepdims=True)
    r = lax.rsqrt(jnp.mean(centre * centre, axis=-1, keepdims=True) + 1e-05)
    return centre * r, r


GAIN, SHIFT, BRANCH, HIDDEN, OFFSETS, SMALL = 0, 2, 4, 6, 8, 16
PIECES = 21
ATTEND = range(11, 17)
LATE = {1: ((1, 1),), 2: ((0, 2),), 3: ((1, 3),), 7: ((1, 5),), 8: ((0, 6), (1, 7)), 10: ((0, 8),)}
PER_LAYER = 12


ACT, PRE, NORM, H, ATT, Q, K, V = "act", "pre", "norm", "h", "att", "q", "k", "v"
W_SHRINK, W_EXPAND, W_MERGE, W_HEADS = "w_shrink", "w_expand", "w_merge", "w_heads"
NORM1, NORM2, H_MID = "norm1", "norm2", "h_mid"
SHRINK, EXPAND, MERGE, HEADS = "shrink", "expand", "merge", "heads"


class Backward(FlatExchange):
    LOADS = (ACT, PRE, NORM, H, ATT, Q, K, V, W_SHRINK, W_EXPAND, W_MERGE, W_HEADS)

    def more_scratch(self):
        T, D, W, F = self.T, self.D, self.W, self.F
        low, full = jnp.bfloat16, jnp.float32
        dma = pltpu.SemaphoreType.DMA
        return dict(
            act=pltpu.VMEM((T, F), low), pre=pltpu.VMEM((T, F), full), norm=pltpu.VMEM((T, D), low),
            h=pltpu.VMEM((T, D), full), att=pltpu.VMEM((T, W), low), q=pltpu.VMEM((T, W), low),
            k=pltpu.VMEM((T, W), low), v=pltpu.VMEM((T, W), low), w_shrink=pltpu.VMEM((F, D), low),
            w_expand=pltpu.VMEM((D, F), low), w_merge=pltpu.VMEM((W, D), low), w_heads=pltpu.VMEM((3, D, W), low),
            g=pltpu.VMEM((T, D), full), low=pltpu.VMEM((T, D), low), came=pltpu.VMEM((T, D), full),
            datt=pltpu.VMEM((T, W), low), dqkv=pltpu.VMEM((3, T, W), low),
            staged=pltpu.VMEM((2, 2, 384, 384), full), dk=pltpu.VMEM((T, 128), full), dv=pltpu.VMEM((T, 128), full),
            small=pltpu.VMEM((2 * SMALL, D), full), small_in=pltpu.VMEM((4, 2 * SMALL, D), full),
            input_s=dma((len(self.LOADS),)), cot_s=dma, staged_s=dma((2,)), tokens_s=dma,
            core_s=dma((T // ROWS,)), core_r=dma((T // ROWS,)), core_c=pltpu.SemaphoreType.REGULAR,
            small_s=dma((4,)), small_r=dma((4,)),
        )

    def held_slots(self):
        return self.starts[6]

    def held(self, g):
        return self.refs.held.at[lax.rem(g, self.held_slots())]

    def fetch(self, name, layer, second=False):
        source = self.inputs[name][layer]
        if name in (NORM, H):
            source = source[1 if second else 0]
        pltpu.make_async_copy(source, getattr(self.refs, name), self.refs.input_s.at[self.LOADS.index(name)]).start()

    def arrive(self, name):
        source = self.inputs[name][0]
        if name in (NORM, H):
            source = source[0]
        pltpu.make_async_copy(source, getattr(self.refs, name), self.refs.input_s.at[self.LOADS.index(name)]).wait()

    def fetch_next(self, l, *names, second=False):
        @pl.when(l == 1)
        def _():
            for name in names:
                self.fetch(name, 0, second)

    def stage_copy(self, at, g):
        return pltpu.make_async_copy(self.refs.staged.at[at], self.source.at[g], self.refs.staged_s.at[at])

    def core_copy(self, i):
        r = self.refs
        rows = pl.ds(pl.multiple_of(i * ROWS, ROWS), ROWS)
        return self.copy(
            r.pre.at[rows, pl.ds(0, self.D)], r.came.at[rows], r.core_s.at[i], r.core_r.at[i],
            (self.dp, 1 - self.core),
        )

    def partial(self, make, wait):
        @pl.when(wait)
        def _():
            pl.semaphore_wait(self.refs.core_c, 1)

        def block(i, carry):
            rows = pl.ds(pl.multiple_of(i * ROWS, ROWS), ROWS)
            self.refs.pre[rows, 0 : self.D] = make(rows)
            self.core_copy(i).start()
            return carry

        lax.fori_loop(0, self.T // ROWS, block, 0)

    def norm_back(self, l, which, more, after):
        r, D = self.refs, self.D
        gain = self.gain[l, which : which + 1]
        n = 128
        blocks = ROWS // n

        def block(i, carry):
            @pl.when(lax.rem(i, blocks) == 0)
            def _():
                copy = self.core_copy(lax.div(i, blocks))
                copy.wait_send()
                copy.wait_recv()

            rows = pl.ds(pl.multiple_of(i * n, n), n)
            xhat, rstd = norm_parts(r.h[rows])
            d = r.pre[rows, 0:D] + r.came[rows]
            e = d * gain
            spread = xhat * jnp.mean(e * xhat, axis=-1, keepdims=True)
            new = r.g[rows] + rstd * (e - jnp.mean(e, axis=-1, keepdims=True) - spread)
            r.g[rows] = new
            rounded = new.astype(jnp.bfloat16)
            r.low[rows] = rounded
            return (
                carry[0] + jnp.sum(d * xhat, axis=0, keepdims=True),
                carry[1] + jnp.sum(d, axis=0, keepdims=True),
                carry[2] + jnp.sum(rounded.astype(jnp.float32), axis=0, keepdims=True),
            )

        zero = jnp.zeros((1, D), jnp.float32)
        sums = lax.fori_loop(0, self.T // n, block, (zero, zero, zero))
        self.row(l, GAIN + which)[...] = sums[0]
        self.row(l, SHIFT + which)[...] = sums[1]
        after(sums[2])

        @pl.when(more)
        def _():
            pl.semaphore_signal(
                r.core_c, inc=1, device_id=(self.dp, 1 - self.core), device_id_type=MESH
            )

    def row(self, l, at, start=0, size=None):
        size = self.D if size is None else size
        return self.refs.small.at[pl.ds(l * SMALL + at, 1), start : start + size]

    def outer(self, left, left_at, right, right_at, at, job):
        for u in range(2):
            a = left[:, pl.ds(pl.multiple_of(left_at + u * UNIT, 128), UNIT)]
            self.refs.staged[at, u] = dot(a, right[:, right_at * UNIT : (right_at + 1) * UNIT], TN)
        self.stage_copy(at, job).start()

    def shrink_job(self, i, job):
        self.outer(self.refs.act, i // 2 * 2 * UNIT, self.refs.low, i % 2, i % 2, job)

    def expand_job(self, i, job):
        self.outer(self.refs.norm, 0, self.refs.act, i, i % 2, job)

    def slopes(self, first, last, l):
        r, F, D = self.refs, self.F, self.D

        def one(i, carry):
            rows = pl.ds(pl.multiple_of(i * ROWS, ROWS), ROWS)
            sums = []
            for c in range(0, F, 512):
                d_act = dot(r.low[rows], r.w_shrink[c : c + 512], NT)
                d_pre = (d_act * gelu_slope(r.pre[rows, c : c + 512])).astype(jnp.bfloat16)
                r.act[rows, c : c + 512] = d_pre
                sums.append(carry[c // 512] + jnp.sum(d_pre.astype(jnp.float32), axis=0, keepdims=True))
            return tuple(sums)

        sums = lax.fori_loop(first, last, one, (jnp.zeros((1, 512), jnp.float32),) * (F // 512))
        for i, part in enumerate(sums):
            for j in range(2):
                at = i * 512 + j * 256
                row = self.row(l, HIDDEN + at // D, at % D, 256)
                row[...] = row[...] + part[:, j * 256 : (j + 1) * 256]

    def piece(self, p, l):
        r = self.refs
        T, W = self.T, self.W
        blocks = T // ROWS
        base = (1 - l) * PER_LAYER
        for q, job in LATE.get(p - 1, ()):
            self.stage_copy(q, base + job).wait()
        if p == 0:
            self.arrive(ACT)

            @pl.when(l == 1)
            def _():
                pltpu.make_async_copy(self.cotangent, r.low, r.cot_s).wait()
                for name in self.LOADS[1:]:
                    self.fetch(name, 1, second=True)

            self.shrink_job(0, base)
            self.stage_copy(0, base).wait()
        elif p in (1, 2, 3):
            self.shrink_job(p, base + p)
        elif p == 4:
            @pl.when(l == 1)
            def _():
                def widen(i, carry):
                    rows = pl.ds(pl.multiple_of(i * ROWS, ROWS), ROWS)
                    wide = r.low[rows].astype(jnp.float32)
                    r.g[rows] = wide
                    return carry + jnp.sum(wide, axis=0, keepdims=True)

                self.row(l, BRANCH + 1)[...] = lax.fori_loop(0, blocks, widen, jnp.zeros((1, self.D), jnp.float32))

            self.arrive(W_SHRINK)
            self.arrive(PRE)
            self.slopes(0, blocks // 2, l)
        elif p == 5:
            self.slopes(blocks // 2, blocks, l)
            self.fetch_next(l, W_SHRINK)
        elif p == 6:
            self.arrive(W_EXPAND)
            self.partial(lambda rows: dot(r.act[rows], r.w_expand[...], NT), l == 0)
        elif p == 7:
            self.arrive(NORM)
            self.expand_job(0, base + 4)
            self.expand_job(1, base + 5)
            self.stage_copy(0, base + 4).wait()
        elif p == 8:
            self.expand_job(2, base + 6)
            self.expand_job(3, base + 7)
            self.fetch_next(l, W_EXPAND, ACT)
            for layer in range(2):
                @pl.when(l == layer)
                def _():
                    self.fetch(NORM, layer)
        elif p == 9:
            self.arrive(H)

            def after(total):
                self.row(l, BRANCH)[...] = total

            self.norm_back(l, 1, jnp.bool_(True), after)
            for layer in range(2):
                @pl.when(l == layer)
                def _():
                    self.fetch(H, layer)
        elif p == 10:
            self.arrive(W_MERGE)
            self.arrive(ATT)

            def one(i, carry):
                rows = pl.ds(pl.multiple_of(i * ROWS, ROWS), ROWS)
                r.datt[rows] = dot(r.low[rows], r.w_merge[...], NT).astype(jnp.bfloat16)
                return carry

            lax.fori_loop(0, blocks, one, 0)
            for u in range(2):
                r.staged[0, u] = dot(r.att[...], r.low[:, u * UNIT : (u + 1) * UNIT], TN)
            self.stage_copy(0, base + 8).start()
        elif p in ATTEND:
            if p == ATTEND[0]:
                self.fetch_next(l, W_MERGE, ATT)
                self.arrive(Q)
                self.arrive(K)
                self.arrive(V)
            i = p - ATTEND[0]
            self.attend_back(i // 2, l, i % 2)
            if p == ATTEND[-1]:
                self.fetch_next(l, Q, K, V)
        elif p == 17:
            self.arrive(W_HEADS)

            def make(rows):
                total = dot(r.dqkv[0, rows], r.w_heads[0], NT)
                for c in (1, 2):
                    total = total + dot(r.dqkv[c, rows], r.w_heads[c], NT)
                return total

            self.partial(make, jnp.bool_(True))
            self.fetch_next(l, W_HEADS)
        elif p == 18:
            self.arrive(NORM)
            self.heads_job(0, base + 9)
            self.stage_copy(0, base + 9).wait()
        elif p == 19:
            self.heads_job(1, base + 10)
            self.heads_job(2, base + 11)
            for i, c in enumerate((0, 2)):
                self.row(l, OFFSETS, i * W, W)[...] = jnp.sum(r.dqkv[c].astype(jnp.float32), axis=0, keepdims=True)
            self.fetch_next(l, NORM, second=True)
            for c in (1, 2):
                self.stage_copy(c % 2, base + 9 + c).wait()
        else:
            self.arrive(H)

            def after(total):
                @pl.when(l == 1)
                def _():
                    self.row(0, BRANCH + 1)[...] = total

            self.norm_back(l, 0, l == 1, after)
            self.fetch_next(l, PRE)
            self.fetch_next(l, H, second=True)

            @pl.when(l == 0)
            def _():
                pltpu.make_async_copy(r.low, self.grad_tokens, r.tokens_s).start()

    def heads_job(self, c, job):
        r = self.refs
        for u in range(2):
            r.staged[c % 2, u] = dot(r.norm[:, u * UNIT : (u + 1) * UNIT], r.dqkv[c], TN)
        self.stage_copy(c % 2, job).start()

    def attend_back(self, pair, l, turn):
        r = self.refs
        T = self.T
        lanes = slice(pair * 128, (pair + 1) * 128)
        if turn == 0:
            r.dk[...] = jnp.zeros((T, 128), jnp.float32)
            r.dv[...] = jnp.zeros((T, 128), jnp.float32)
        lane = lax.broadcasted_iota(jnp.int32, (1, 128), 1)
        blocks = T // ROWS
        for b in range(blocks - 1) if turn == 0 else (blocks - 1,):
            rows, end = slice(b * ROWS, (b + 1) * ROWS), (b + 1) * ROWS
            query = b * ROWS + lax.broadcasted_iota(jnp.int32, (1, ROWS), 1)
            lowest = query - jnp.concatenate([self.positions[j : j + 1] for j in range(2 * b, 2 * b + 2)], axis=1)
            key = lax.broadcasted_iota(jnp.int32, (end, ROWS), 0)
            allowed = (key <= query) & (key >= lowest)
            q, d = r.q[rows, lanes], r.datt[rows, lanes]
            k, v = r.k[0:end, lanes], r.v[0:end, lanes]
            dq = jnp.zeros((ROWS, 128), jnp.float32)
            for side in range(2):
                mine = (lax.div(lane, 64) == side).astype(jnp.float32)
                low, eighth = mine.astype(jnp.bfloat16), (mine * 0.125).astype(jnp.bfloat16)
                q_own, d_own = q * eighth, d * low
                scores = dot(k, q_own, NT)
                lse = self.lse[l, pair * 2 + side : pair * 2 + side + 1, rows]
                probs = jnp.where(allowed, jnp.exp(scores - lse), 0.0)
                dprob = dot(v, d_own, NT)
                centre = jnp.sum(probs * dprob, axis=0, keepdims=True)
                dscore = (probs * (dprob - centre)).astype(jnp.bfloat16)
                r.dv[0:end] = r.dv[0:end] + dot(probs.astype(jnp.bfloat16), d_own, NN)
                r.dk[0:end] = r.dk[0:end] + dot(dscore, q_own, NN)
                dq = dq + dot(dscore, k * eighth, TN)
            r.dqkv[0, rows, lanes] = dq.astype(jnp.bfloat16)
        if turn == 1:
            r.dqkv[1, :, lanes] = r.dk[...].astype(jnp.bfloat16)
            r.dqkv[2, :, lanes] = r.dv[...].astype(jnp.bfloat16)

    def small_swap(self, step):
        r = self.refs
        z = self.z
        to = (
            self.dp + self.step_x,
            self.dp + self.step_y,
            self.dp + 4 - 8 * lax.rem(z, 2),
            self.dp + 8 - 16 * lax.div(z, 2),
        )[step]
        return self.copy(
            r.small, r.small_in.at[step], r.small_s.at[step], r.small_r.at[step], (to, self.core)
        )

    def small_stage(self, step):
        if step > 0:
            copy = self.small_swap(step - 1)
            copy.wait_send()
            copy.wait_recv()
            self.refs.small[...] = self.refs.small[...] + self.refs.small_in[step - 1]
        if step < 4:
            self.small_swap(step).start()

    def run(self):
        r = self.refs
        pltpu.make_async_copy(self.cotangent, r.low, r.cot_s).start()
        self.fetch(ACT, 1)
        r.small[...] = jnp.zeros(r.small.shape, jnp.float32)
        far = (self.dp + 8 - 16 * lax.div(self.z, 2), self.core)
        self.barrier(((self.dp, 1 - self.core), far))

        def step(t, carry):
            l = 1 - lax.div(t, PIECES)
            for p in range(PIECES):
                @pl.when((lax.rem(t, PIECES) == p) & (t < 2 * PIECES))
                def _():
                    self.piece(p, l)

            for s in range(5):
                @pl.when(t == 2 * PIECES + s)
                def _():
                    self.small_stage(s)

            self.tick(t)
            return carry

        lax.fori_loop(0, self.ticks, step, 0)
        pltpu.make_async_copy(r.low, self.grad_tokens, r.tokens_s).wait()
        self.small_out[...] = r.small[...]


def backward(kept, weights, gain, lse, positions, cotangent, slots=6, lags=(4, 2, 2, 2, 2, 2, 2, 2, 4)):
    D = cotangent.shape[1]
    _, T, W = kept[1].shape
    jobs = 2 * PER_LAYER
    plan = Backward(2 * jobs, UNIT // 2, UNIT, slots, lags)
    plan.T, plan.D, plan.W, plan.F = T, D, W, weights[0].shape[1]
    scratch = plan.scratch() | plan.more_scratch()
    n = len(kept)

    def kernel(*refs):
        layers = [[ref.at[i] for i in range(2)] for ref in refs[:n]]
        norm1, q, k, v, att, h_mid, norm2, pre, act, h = layers
        plan.inputs = dict(zip(plan.LOADS, (act, pre, list(zip(norm1, norm2)), list(zip(h, h_mid)), att, q, k, v)))
        for name, weight in zip((W_SHRINK, W_EXPAND, W_MERGE, W_HEADS), refs[n : n + 4]):
            plan.inputs[name] = [weight.at[i] for i in range(2)]
        plan.cotangent, plan.gain, plan.lse, plan.positions = refs[n + 4 : n + 8]
        plan.target, plan.source, plan.grad_tokens, plan.small_out = refs[n + 8 : n + 12]
        plan.setup(SimpleNamespace(**dict(zip(scratch, refs[n + 12 :]))))
        plan.run()

    hbm = pl.BlockSpec(memory_space=pl.ANY)
    vmem = pl.BlockSpec(memory_space=pltpu.VMEM)
    flat = jax.ShapeDtypeStruct((jobs, 2, UNIT, UNIT), jnp.float32)
    target, _, grad_tokens, small = pl.pallas_call(
        kernel,
        out_shape=(
            flat,
            flat,
            jax.ShapeDtypeStruct((T, D), jnp.bfloat16),
            jax.ShapeDtypeStruct((2 * SMALL, D), jnp.float32),
        ),
        in_specs=[hbm] * (n + 5) + [vmem] * 3,
        out_specs=(hbm, hbm, hbm, vmem),
        scratch_shapes=list(scratch.values()),
        compiler_params=pltpu.CompilerParams(
            collective_id=0, has_side_effects=True, vmem_limit_bytes=61 * 2**20
        ),
    )(*kept, *weights, cotangent, gain, lse, positions)
    return target, grad_tokens, small


def gelu(x):
    return 0.5 * x * (1.0 + jnp.tanh(0.7978845608028654 * (x + 0.044715 * x * x * x)))


class Forward:
    KEPT = (NORM1, Q, K, V, ATT, H_MID, NORM2, PRE, ACT, H)

    WEIGHTS = (HEADS, MERGE, EXPAND, SHRINK)

    def scratch(self):
        T, D, W, F = self.T, self.D, self.W, self.F
        low, full = jnp.bfloat16, jnp.float32
        dma = pltpu.SemaphoreType.DMA
        n = T // ROWS
        return dict(
            norm1=pltpu.VMEM((T, D), low), q=pltpu.VMEM((T, W), low), k=pltpu.VMEM((T, W), low), v=pltpu.VMEM((T, W), low),
            att=pltpu.VMEM((T, W), low), h_mid=pltpu.VMEM((T, D), full), norm2=pltpu.VMEM((T, D), low),
            pre=pltpu.VMEM((T, F), full), act=pltpu.VMEM((T, F), low), h=pltpu.VMEM((T, D), full),
            low=pltpu.VMEM((T, D), low), part=pltpu.VMEM((2, T, D), full), came=pltpu.VMEM((2, T, D), full),
            bias=pltpu.VMEM((n, ROWS, T), full),
            heads=pltpu.VMEM((2, 3, D, W), low), merge=pltpu.VMEM((2, W, D), low),
            expand=pltpu.VMEM((2, D, F), low), shrink=pltpu.VMEM((2, F, D), low),
            kept_s=dma((len(self.KEPT), n)), weight_s=dma((4, 2)), token_s=dma, out_s=dma((n,)),
            core_s=dma((2, n)), core_r=dma((2, n)),
        )

    def rows(self, b):
        return pl.ds(pl.multiple_of(b * ROWS, ROWS), ROWS)

    def keep_copy(self, name, l, b):
        at = self.rows(b)
        return pltpu.make_async_copy(
            getattr(self.refs, name).at[at], self.kept[name].at[l, at], self.refs.kept_s.at[self.KEPT.index(name), b]
        )

    def free(self, l, b, *names):
        @pl.when(l == 1)
        def _():
            for name in names:
                self.keep_copy(name, 0, b).wait()

    def keep(self, l, b, *names):
        for name in names:
            self.keep_copy(name, l, b).start()

    def weight_copy(self, name, l):
        at = self.WEIGHTS.index(name)
        return pltpu.make_async_copy(self.weights[name].at[l], getattr(self.refs, name).at[l], self.refs.weight_s.at[at, l])

    def core_copy(self, kind, b):
        r, at = self.refs, self.rows(b)
        return pltpu.make_async_remote_copy(
            src_ref=r.part.at[kind, at], dst_ref=r.came.at[kind, at],
            send_sem=r.core_s.at[kind, b], recv_sem=r.core_r.at[kind, b],
            device_id=(lax.axis_index("dp"), 1 - lax.axis_index("tensor")), device_id_type=MESH,
        )

    def summed(self, kind, b):
        copy = self.core_copy(kind, b)
        copy.wait_send()
        copy.wait_recv()
        at = self.rows(b)
        return self.refs.part[kind, at] + self.refs.came[kind, at]

    def norm(self, x, l, which):
        xhat, _ = norm_parts(x)
        return (xhat * self.gain[l, which : which + 1] + self.shift[l, which : which + 1]).astype(jnp.bfloat16)

    def before_first(self, l, b):
        r, at = self.refs, self.rows(b)
        self.free(l, b, H, NORM1, Q, K, V)

        @pl.when(l == 0)
        def _():
            r.h[at] = r.low[at].astype(jnp.float32)

        @pl.when(l == 1)
        def _():
            r.h[at] = r.h_mid[at] + (self.summed(1, b) + self.branch[0, 1:2])

    def first(self, l, b):
        r, at = self.refs, self.rows(b)
        low = self.norm(r.h[at], l, 0)
        r.norm1[at] = low
        r.q[at] = (dot(low, r.heads[l, 0], NN) + self.offsets[l, 0:1]).astype(jnp.bfloat16)
        r.k[at] = dot(low, r.heads[l, 1], NN).astype(jnp.bfloat16)
        r.v[at] = (dot(low, r.heads[l, 2], NN) + self.offsets[l, 1:2]).astype(jnp.bfloat16)

    def after_first(self, l, b):
        self.keep(l, b, H, NORM1, Q, K, V)

    def mix(self, l, b):
        r, at = self.refs, self.rows(b)
        self.free(l, b, ATT)
        for i in range(self.T // ROWS):
            @pl.when(b == i)
            def _():
                self.attend(l, i)

        r.part[0, at] = dot(r.att[at], r.merge[l], NN)
        self.core_copy(0, b).start()
        self.keep(l, b, ATT)

    def attend(self, l, b):
        r = self.refs
        rows, end = slice(b * ROWS, (b + 1) * ROWS), (b + 1) * ROWS

        @pl.when(l == 0)
        def _():
            query = b * ROWS + lax.broadcasted_iota(jnp.int32, (ROWS, 1), 0)
            spread = jnp.concatenate([self.positions[...].astype(jnp.float32)] * 16, axis=0).T
            column = jnp.concatenate([spread[:, j : j + 1] for j in range(2 * b, 2 * b + 2)], axis=0)
            lowest = query - column.astype(jnp.int32)
            key = lax.broadcasted_iota(jnp.int32, (ROWS, end), 1)
            r.bias[b, :, 0:end] = jnp.where((key <= query) & (key >= lowest), 0.0, -1e30)

        lane = lax.broadcasted_iota(jnp.int32, (1, 128), 1)
        logs = jnp.zeros((ROWS, 128), jnp.float32)
        for pair in range(self.W // 128):
            lanes = slice(pair * 128, (pair + 1) * 128)
            q, k, v = r.q[rows, lanes], r.k[0:end, lanes], r.v[0:end, lanes]
            total = jnp.zeros((ROWS, 128), jnp.float32)
            for side in range(2):
                mine = (lax.div(lane, 64) == side).astype(jnp.float32)
                scores = dot(q * (mine * 0.125).astype(jnp.bfloat16), k, NT) + r.bias[b, :, 0:end]
                highest = jnp.max(scores, axis=-1, keepdims=True)
                weights = jnp.exp(scores - highest)
                amount = jnp.sum(weights, axis=-1, keepdims=True)
                probs = (weights * (1.0 / amount)).astype(jnp.bfloat16)
                total = total + dot(probs, v * mine.astype(jnp.bfloat16), NN)
                logs = jnp.where(lane == pair * 2 + side, highest + jnp.log(amount), logs)
            r.att[rows, lanes] = total.astype(jnp.bfloat16)
        self.lse[l, :, rows] = logs.T[0:8]

    def before_second(self, l, b):
        self.free(l, b, H_MID, NORM2, PRE, ACT)
        copy = self.core_copy(0, b)
        copy.wait_send()
        copy.wait_recv()

    def second(self, l, b):
        r, at = self.refs, self.rows(b)
        middle = r.h[at] + (r.part[0, at] + r.came[0, at] + self.branch[l, 0:1])
        r.h_mid[at] = middle
        low = self.norm(middle, l, 1)
        r.norm2[at] = low
        for c in range(0, self.F, 512):
            pre = dot(low, r.expand[l, :, c : c + 512], NN) + self.hidden[pl.ds(l, 1), c : c + 512]
            r.pre[at, c : c + 512] = pre
            r.act[at, c : c + 512] = gelu(pre).astype(jnp.bfloat16)
        r.part[1, at] = dot(r.act[at], r.shrink[l], NN)

    def after_second(self, l, b):
        self.core_copy(1, b).start()
        self.keep(l, b, H_MID, NORM2, PRE, ACT)

    def finish(self, b):
        r, at = self.refs, self.rows(b)
        r.low[at] = (r.h_mid[at] + (self.summed(1, b) + self.branch[1, 1:2])).astype(jnp.bfloat16)
        pltpu.make_async_copy(r.low.at[at], self.output.at[at], r.out_s.at[b]).start()

    def run(self):
        r = self.refs
        n = self.T // ROWS
        load = pltpu.make_async_copy(self.tokens, r.low, r.token_s)
        load.start()
        for name in self.WEIGHTS:
            self.weight_copy(name, 0).start()
        other = (lax.axis_index("dp"), 1 - lax.axis_index("tensor"))
        bar = pltpu.get_barrier_semaphore()
        pl.semaphore_signal(bar, inc=1, device_id=other, device_id_type=MESH)
        pl.semaphore_wait(bar, 1)
        load.wait()

        self.weight_copy(HEADS, 0).wait()
        self.before_first(0, 0)
        self.first(0, 0)
        self.after_first(0, 0)

        def turn(t, carry):
            for l in range(2):
                @pl.when(t == l * n)
                def _():
                    self.weight_copy(MERGE, l).wait()

            @pl.when(t < 2 * n)
            def _():
                self.mix(lax.div(t, n), lax.rem(t, n))

            for l in range(2):
                @pl.when(t == l * n + 1)
                def _():
                    self.weight_copy(EXPAND, l).wait()
                    self.weight_copy(SHRINK, l).wait()

            @pl.when(t == 1)
            def _():
                for name in self.WEIGHTS:
                    self.weight_copy(name, 1).start()

            @pl.when(t == n - 1)
            def _():
                self.weight_copy(HEADS, 1).wait()

            old, new = t - 1, t + 1
            goes = (new < 2 * n, lax.div(new, n), lax.rem(new, n))
            comes = ((old >= 0) & (old < 2 * n), lax.div(old, n), lax.rem(old, n))

            @pl.when(comes[0])
            def _():
                self.before_second(*comes[1:])

            @pl.when(goes[0])
            def _():
                self.before_first(*goes[1:])

            @pl.when(comes[0] & goes[0])
            def _():
                self.second(*comes[1:])
                self.first(*goes[1:])

            @pl.when(comes[0] & jnp.logical_not(goes[0]))
            def _():
                self.second(*comes[1:])

            @pl.when(goes[0] & jnp.logical_not(comes[0]))
            def _():
                self.first(*goes[1:])

            @pl.when(comes[0])
            def _():
                self.after_second(*comes[1:])

            @pl.when(goes[0])
            def _():
                self.after_first(*goes[1:])

            @pl.when(t >= n + 2)
            def _():
                self.finish(t - n - 2)

            return carry

        lax.fori_loop(0, 2 * n + 2, turn, 0)
        for b in range(n):
            for name in self.KEPT:
                self.keep_copy(name, 1, b).wait()
            pltpu.make_async_copy(r.low.at[self.rows(b)], self.output.at[self.rows(b)], r.out_s.at[b]).wait()


def forward(tokens, positions, weights, rows):
    plan = Forward()
    T, D = tokens.shape
    plan.T, plan.D, plan.W, plan.F = T, D, weights[0].shape[3], weights[2].shape[2]
    scratch = plan.scratch()
    kinds = plan.KEPT

    def kernel(tokens, heads, merge, expand, shrink, positions, gain, shift, offsets, branch, hidden, output, lse, *refs):
        plan.tokens, plan.positions, plan.output, plan.lse = tokens, positions, output, lse
        plan.weights = dict(zip(plan.WEIGHTS, (heads, merge, expand, shrink)))
        plan.gain, plan.shift, plan.offsets, plan.branch, plan.hidden = gain, shift, offsets, branch, hidden
        plan.kept = dict(zip(kinds, refs))
        plan.refs = SimpleNamespace(**dict(zip(scratch, refs[len(kinds) :])))
        plan.run()

    hbm = pl.BlockSpec(memory_space=pl.ANY)
    vmem = pl.BlockSpec(memory_space=pltpu.VMEM)
    kept_shapes = [jax.ShapeDtypeStruct((2,) + scratch[name].shape, scratch[name].dtype) for name in kinds]
    out = pl.pallas_call(
        kernel,
        out_shape=[jax.ShapeDtypeStruct((T, D), jnp.bfloat16), jax.ShapeDtypeStruct((2, 8, T), jnp.float32)] + kept_shapes,
        in_specs=[hbm] * 5 + [vmem] * 6,
        out_specs=[hbm, vmem] + [hbm] * len(kept_shapes),
        scratch_shapes=list(scratch.values()),
        compiler_params=pltpu.CompilerParams(
            collective_id=1, has_side_effects=True, vmem_limit_bytes=61 * 2**20
        ),
    )(tokens, *weights, positions, *rows)
    return out[0], out[1], out[2:]


def spread(flat, small, shapes, dtype=jnp.float32):
    half = flat.shape[0] // 2
    width = small.shape[1]

    def kernel(source, sums, gain, shift, heads, offsets, merge, branch, expand, hidden, shrink, held, into, out):
        loads, copies = [], []

        def put(g, u, target):
            i = len(copies)
            loads.append(pltpu.make_async_copy(source.at[g, u], held.at[i], into.at[i]))
            copies.append(pltpu.make_async_copy(held.at[i], target, out.at[i]))
            loads[-1].start()

        for l in range(2):
            base = (1 - l) * half
            for u in range(2):
                rows = pl.ds(u * UNIT, UNIT)
                for i in range(4):
                    at = pl.ds((i // 2) * 2 * UNIT + u * UNIT, UNIT)
                    put(base + i, u, shrink.at[l, at, pl.ds((i % 2) * UNIT, UNIT)])
                    put(base + 4 + i, u, expand.at[l, rows, pl.ds(i * UNIT, UNIT)])
                put(base + 8, u, merge.at[l, :, rows])
                for c in range(3):
                    put(base + 9 + c, u, heads.at[l, c, rows])
            for target, at in ((gain, GAIN), (shift, SHIFT), (branch, BRANCH)):
                target[l] = sums[l * SMALL + at : l * SMALL + at + 2]
            for i in range(2):
                at = l * SMALL + HIDDEN + i
                hidden[l : l + 1, i * width : (i + 1) * width] = sums[at : at + 1]
                at = l * SMALL + OFFSETS
                offsets[l, i : i + 1] = sums[at : at + 1, i * UNIT : (i + 1) * UNIT]
        for load, copy in zip(loads, copies):
            load.wait()
            copy.start()
        for copy in copies:
            copy.wait()

    hbm = pl.BlockSpec(memory_space=pl.ANY)
    vmem = pl.BlockSpec(memory_space=pltpu.VMEM)
    return pl.pallas_call(
        kernel,
        out_shape=[jax.ShapeDtypeStruct(s, dtype) for s in shapes],
        in_specs=[hbm, vmem],
        out_specs=[vmem, vmem, hbm, vmem, hbm, vmem, hbm, vmem, hbm],
        scratch_shapes=[
            pltpu.VMEM((2 * flat.shape[0], UNIT, UNIT), dtype),
            pltpu.SemaphoreType.DMA((2 * flat.shape[0],)),
            pltpu.SemaphoreType.DMA((2 * flat.shape[0],)),
        ],
        compiler_params=pltpu.CompilerParams(has_side_effects=True, vmem_limit_bytes=48 * 2**20),
    )(flat, small)


def on_device(
    tokens,
    positions,
    norm_gain,
    norm_shift,
    heads_weight,
    offsets,
    merge_weight,
    branch_bias,
    expand_weight,
    hidden_bias,
    shrink_weight,
    cotangent,
):
    rows = (norm_gain, norm_shift, offsets, branch_bias, hidden_bias)
    places = positions.reshape(-1, 128)
    output, lse, kept = forward(
        tokens, places, (heads_weight, merge_weight, expand_weight, shrink_weight), rows
    )
    flat, grad_tokens, small = backward(
        kept, (shrink_weight, expand_weight, merge_weight, heads_weight), norm_gain, lse, places, cotangent
    )
    ranks = lax.axis_size("dp")
    if ranks > BLOCK:
        groups = [[j * BLOCK + i for j in range(ranks // BLOCK)] for i in range(BLOCK)]
        flat, small = lax.psum((flat, small), "dp", axis_index_groups=groups)
    shapes = [norm_gain, norm_shift, heads_weight, offsets, merge_weight, branch_bias, expand_weight, hidden_bias, shrink_weight]
    return (output, grad_tokens, *spread(flat, small, [like.shape for like in shapes]))


def solution(mesh):
    placed = (
        P("dp", None),
        P("dp"),
        P(),
        P(),
        P(None, None, None, "tensor"),
        P(None, None, "tensor"),
        P(None, "tensor", None),
        P(),
        P(None, None, "tensor"),
        P(None, "tensor"),
        P(None, "tensor", None),
        P("dp", None),
    )
    return jax.shard_map(
        on_device,
        mesh=mesh,
        in_specs=placed,
        out_specs=(
            P("dp", None),
            P("dp", None),
            P(),
            P(),
            P(None, None, None, "tensor"),
            P(None, None, "tensor"),
            P(None, "tensor", None),
            P(),
            P(None, None, "tensor"),
            P(None, "tensor"),
            P(None, "tensor", None),
        ),
        check_vma=False,
    )
```

```python
from types import SimpleNamespace

import jax
import jax.numpy as jnp
from jax import lax
from jax.experimental import pallas as pl
from jax.experimental.pallas import tpu as pltpu
from jax.sharding import PartitionSpec as P

LAYERS = 2
UNIT = 384
BLOCK = 16
MESH = pl.DeviceIdType.MESH


class Exchange:
    def __init__(self, groups, rows, cols, slots, lags):
        self.groups, self.rows, self.cols, self.slots = groups, rows, cols, slots
        self.half = rows // 2
        self.chunk = self.half // 4
        starts = [0]
        for lag in lags:
            starts.append(starts[-1] + lag)
        self.starts = starts
        self.ticks = groups + starts[-1]
        self.last_slots = starts[9]
        self.gather_slots = max(starts[8] - starts[1], slots)

    def scratch(self):
        groups, slots, half, chunk, cols = self.groups, self.slots, self.half, self.chunk, self.cols
        dma = pltpu.SemaphoreType.DMA
        plain = pltpu.SemaphoreType.REGULAR
        return dict(
            held=pltpu.VMEM((self.held_slots(), 2, half, cols), jnp.float32),
            swap_in=pltpu.VMEM((slots, 2, half, cols), jnp.float32),
            chain_in=pltpu.VMEM((slots, 3, 2, 2, chunk, cols), jnp.float32),
            third_in=pltpu.VMEM((slots, 2, chunk, cols), jnp.float32),
            swap_s=dma((slots,)), swap_r=dma((slots,)),
            chain_s=dma((slots, 3, 2)), chain_r=dma((slots, 3, 2)),
            third_s=dma((slots,)), third_r=dma((slots,)),
            gather_s=dma((slots, 3, 2)), gather_r=dma((self.gather_slots, 3, 2)),
            last_s=dma((slots,)), last_r=dma((self.last_slots,)),
            own_s=dma((slots,)), load_s=dma((slots,)),
            swap_c=plain((2,)), chain_c=plain((3, 2)), third_c=plain((2,)),
        )

    def held_slots(self):
        return self.groups

    def setup(self, refs):
        self.refs = refs
        dp = lax.axis_index("dp")
        core = lax.axis_index("tensor")
        low = lax.rem(dp, 16)
        self.dp, self.core = dp, core
        self.z = lax.div(low, 4)
        self.y = lax.rem(lax.div(low, 2), 2)
        self.x = lax.rem(low, 2)
        self.step_x = 1 - 2 * self.x
        self.step_y = 2 - 4 * self.y
        self.along = ((dp + 4, core), (dp - 4, core))

    def barrier(self, others=()):
        z = self.z
        bar = pltpu.get_barrier_semaphore()

        def greet(device):
            pl.semaphore_signal(bar, inc=1, device_id=device, device_id_type=MESH)

        for device in ((self.dp + self.step_x, self.core), (self.dp + self.step_y, self.core)) + tuple(others):
            greet(device)

        @pl.when(z < 3)
        def _():
            greet(self.along[0])

        @pl.when(z > 0)
        def _():
            greet(self.along[1])

        pl.semaphore_wait(bar, 2 + len(others) + (z < 3).astype(jnp.int32) + (z > 0).astype(jnp.int32))

    def first(self, g):
        return (self.dp + jnp.where(lax.rem(g, 2) == 0, self.step_x, self.step_y), self.core)

    def third(self, g):
        return (self.dp + jnp.where(lax.rem(g, 2) == 0, self.step_y, self.step_x), self.core)

    def side(self, g):
        return jnp.where(lax.rem(g, 2) == 0, self.x, self.y)

    def copy(self, src, dst, send, recv, device):
        return pltpu.make_async_remote_copy(
            src_ref=src, dst_ref=dst, send_sem=send, recv_sem=recv, device_id=device, device_id_type=MESH
        )

    def rows_of(self, j):
        return pl.ds(pl.multiple_of(j * self.chunk, 8), self.chunk)

    def held(self, g):
        return self.refs.held.at[g]

    def swap(self, g):
        r, k = self.refs, lax.rem(g, self.slots)
        return self.copy(self.sent_half(g), r.swap_in.at[k], r.swap_s.at[k], r.swap_r.at[k], self.first(g))

    def chain_send(self, step, d, g):
        z, r, k = self.z, self.refs, lax.rem(g, self.slots)
        j = 4 - step + z if d == 0 else step - 4 + z
        here = ((z < 3) & (step > z)) if d == 0 else ((z > 0) & (step > 3 - z))
        at = (k, step - 1, d)
        part = self.held(g).at[:, self.rows_of(j)]
        return here, self.copy(part, r.chain_in.at[at], r.chain_s.at[at], r.chain_r.at[at], self.along[d])

    def start_chain(self, step, g):
        for d in range(2):
            here, copy = self.chain_send(step, d, g)

            @pl.when(here)
            def _():
                @pl.when(g >= self.slots)
                def _():
                    pl.semaphore_wait(self.refs.chain_c.at[step - 1, d], 1)

                copy.start()

    def finish_chain(self, step, g):
        z, r, k = self.z, self.refs, lax.rem(g, self.slots)
        for d in range(2):
            here, copy = self.chain_send(step, d, g)

            @pl.when(here)
            def _():
                copy.wait_send()

        for d in range(2):
            here = ((z >= 1) & (step >= z)) if d == 0 else ((z <= 2) & (step >= 3 - z))
            j = 3 - step + z if d == 0 else step - 3 + z
            at = (k, step - 1, d)

            @pl.when(here)
            def _():
                came = r.chain_in.at[at]
                self.copy(came, came, r.chain_s.at[at], r.chain_r.at[at], self.along[1 - d]).wait_recv()
                part = self.held(g).at[:, self.rows_of(j)]
                part[...] = part[...] + came[...]

                @pl.when(g + self.slots < self.groups)
                def _():
                    pl.semaphore_signal(
                        r.chain_c.at[step - 1, d], inc=1, device_id=self.along[1 - d], device_id_type=MESH
                    )

    def third_swap(self, g):
        r, k = self.refs, lax.rem(g, self.slots)
        part = self.held(g).at[:, self.rows_of(self.z)]
        return self.copy(part, r.third_in.at[k], r.third_s.at[k], r.third_r.at[k], self.third(g))

    def gather_copy(self, step, d, g, j, source=None):
        r, k = self.refs, lax.rem(g, self.slots)
        part = self.result(g, self.side(g) * self.half + j * self.chunk, self.chunk)
        return self.copy(
            part if source is None else source,
            part,
            r.gather_s.at[k, step - 1, d],
            r.gather_r.at[lax.rem(g, self.gather_slots), step - 1, d],
            self.along[d],
        )

    def gather_send(self, step, d, g):
        z = self.z
        j = z - (step - 1) if d == 0 else z + step - 1
        here = ((z < 3) & (step - 1 <= z)) if d == 0 else ((z > 0) & (z + step - 1 <= 3))
        source = self.held(g).at[:, self.rows_of(z)] if step == 1 else None
        return here, self.gather_copy(step, d, g, j, source)

    def start_gather(self, step, g):
        for d in range(2):
            here, copy = self.gather_send(step, d, g)

            @pl.when(here)
            def _():
                copy.start()

    def finish_gather(self, step, g):
        z = self.z
        for d in range(2):
            here, copy = self.gather_send(step, d, g)

            @pl.when(here)
            def _():
                copy.wait_send()

        for d in range(2):
            here = (z >= step) if d == 0 else (z + step <= 3)
            j = z - step if d == 0 else z + step

            @pl.when(here)
            def _():
                self.gather_copy(step, d, g, j).wait_recv()

    def own_copy(self, g):
        k = lax.rem(g, self.slots)
        part = self.held(g).at[:, self.rows_of(self.z)]
        return pltpu.make_async_copy(
            part, self.result(g, self.side(g) * self.half + self.z * self.chunk, self.chunk), self.refs.own_s.at[k]
        )

    def last(self, g):
        r, k = self.refs, lax.rem(g, self.slots)
        part = self.result(g, self.side(g) * self.half, self.half)
        return self.copy(part, part, r.last_s.at[k], r.last_r.at[lax.rem(g, self.last_slots)], self.first(g))

    def stage(self, e, g):
        r, slots, groups = self.refs, self.slots, self.groups
        k = lax.rem(g, slots)
        if e == 0:
            self.prepare(g)

            @pl.when(g >= slots)
            def _():
                pl.semaphore_wait(r.swap_c.at[lax.rem(g, 2)], 1)

            self.swap(g).start()
        elif e == 1:
            self.settle(g)
            copy = self.swap(g)
            copy.wait_send()
            copy.wait_recv()
            mine = self.held(g)
            mine[...] = mine[...] + r.swap_in[k]

            @pl.when(g + slots < groups)
            def _():
                pl.semaphore_signal(
                    r.swap_c.at[lax.rem(g, 2)], inc=1, device_id=self.first(g), device_id_type=MESH
                )

            self.start_chain(1, g)
        elif e in (2, 3):
            self.finish_chain(e - 1, g)
            self.start_chain(e, g)
        elif e == 4:
            self.finish_chain(3, g)

            @pl.when(g >= slots)
            def _():
                pl.semaphore_wait(r.third_c.at[lax.rem(g, 2)], 1)

            self.third_swap(g).start()
        elif e == 5:
            copy = self.third_swap(g)
            copy.wait_send()
            copy.wait_recv()
            part = self.held(g).at[:, self.rows_of(self.z)]
            part[...] = part[...] + r.third_in[k]

            @pl.when(g + slots < groups)
            def _():
                pl.semaphore_signal(
                    r.third_c.at[lax.rem(g, 2)], inc=1, device_id=self.third(g), device_id_type=MESH
                )

            self.start_gather(1, g)
            self.own_copy(g).start()
        elif e in (6, 7):
            self.finish_gather(e - 5, g)
            if e == 6:
                self.own_copy(g).wait()
            self.start_gather(e - 4, g)
        elif e == 8:
            self.finish_gather(3, g)
            self.last(g).start()
        else:
            copy = self.last(g)
            copy.wait_send()
            copy.wait_recv()

    def tick(self, t):
        for e in reversed(range(10)):
            g = t - self.starts[e]

            @pl.when((g >= 0) & (g < self.groups))
            def _():
                self.stage(e, g)


class FlatExchange(Exchange):
    def part(self, whole, g, start, size):
        start = lax.rem(g, 2) * self.rows + start
        return whole.at[lax.div(g, 2), :, pl.ds(pl.multiple_of(start, 8), size)]

    def sent_half(self, g):
        return self.part(self.source, g, (1 - self.side(g)) * self.half, self.half)

    def load(self, g):
        k = lax.rem(g, self.slots)
        own = self.part(self.source, g, self.side(g) * self.half, self.half)
        return pltpu.make_async_copy(own, self.held(g), self.refs.load_s.at[k])

    def prepare(self, g):
        self.load(g).start()

    def settle(self, g):
        self.load(g).wait()

    def result(self, g, start, size):
        return self.part(self.target, g, start, size)


ROWS = 256


def dot(a, b, dims):
    return lax.dot_general(a, b, (dims, ((), ())), preferred_element_type=jnp.float32)


NN = ((1,), (0,))
NT = ((1,), (1,))
TN = ((0,), (0,))


def gelu_slope(x):
    t = jnp.tanh(0.7978845608028654 * (x + 0.044715 * x * x * x))
    return 0.5 * (1.0 + t) + 0.5 * x * (1.0 - t * t) * (
        0.7978845608028654 * (1.0 + 3.0 * 0.044715 * x * x)
    )


def norm_parts(h):
    centre = h - jnp.mean(h, axis=-1, keepdims=True)
    r = lax.rsqrt(jnp.mean(centre * centre, axis=-1, keepdims=True) + 1e-05)
    return centre * r, r


GAIN, SHIFT, BRANCH, HIDDEN, OFFSETS, SMALL = 0, 2, 4, 6, 8, 16
PIECES = 21
ATTEND = range(11, 17)
LATE = {1: ((1, 1),), 2: ((0, 2),), 3: ((1, 3),), 7: ((1, 5),), 8: ((0, 6), (1, 7)), 10: ((0, 8),)}
PER_LAYER = 12


ACT, PRE, NORM, H, ATT, Q, K, V = "act", "pre", "norm", "h", "att", "q", "k", "v"
W_SHRINK, W_EXPAND, W_MERGE, W_HEADS = "w_shrink", "w_expand", "w_merge", "w_heads"
NORM1, NORM2, H_MID = "norm1", "norm2", "h_mid"
SHRINK, EXPAND, MERGE, HEADS = "shrink", "expand", "merge", "heads"


class Backward(FlatExchange):
    LOADS = (ACT, PRE, NORM, H, ATT, Q, K, V, W_SHRINK, W_EXPAND, W_MERGE, W_HEADS)

    def more_scratch(self):
        T, D, W, F = self.T, self.D, self.W, self.F
        low, full = jnp.bfloat16, jnp.float32
        dma = pltpu.SemaphoreType.DMA
        return dict(
            act=pltpu.VMEM((T, F), low), pre=pltpu.VMEM((T, F), full), norm=pltpu.VMEM((T, D), low),
            h=pltpu.VMEM((T, D), full), att=pltpu.VMEM((T, W), low), q=pltpu.VMEM((T, W), low),
            k=pltpu.VMEM((T, W), low), v=pltpu.VMEM((T, W), low), w_shrink=pltpu.VMEM((F, D), low),
            w_expand=pltpu.VMEM((D, F), low), w_merge=pltpu.VMEM((W, D), low), w_heads=pltpu.VMEM((3, D, W), low),
            g=pltpu.VMEM((T, D), full), low=pltpu.VMEM((T, D), low), came=pltpu.VMEM((T, D), full),
            datt=pltpu.VMEM((T, W), low), dqkv=pltpu.VMEM((3, T, W), low),
            staged=pltpu.VMEM((2, 2, 384, 384), full), dk=pltpu.VMEM((T, 128), full), dv=pltpu.VMEM((T, 128), full),
            small=pltpu.VMEM((2 * SMALL, D), full), small_in=pltpu.VMEM((4, 2 * SMALL, D), full),
            input_s=dma((len(self.LOADS),)), cot_s=dma, staged_s=dma((2,)), tokens_s=dma,
            core_s=dma((T // ROWS,)), core_r=dma((T // ROWS,)), core_c=pltpu.SemaphoreType.REGULAR,
            small_s=dma((4,)), small_r=dma((4,)),
        )

    def held_slots(self):
        return self.starts[6]

    def held(self, g):
        return self.refs.held.at[lax.rem(g, self.held_slots())]

    def fetch(self, name, layer, second=False):
        source = self.inputs[name][layer]
        if name in (NORM, H):
            source = source[1 if second else 0]
        pltpu.make_async_copy(source, getattr(self.refs, name), self.refs.input_s.at[self.LOADS.index(name)]).start()

    def arrive(self, name):
        source = self.inputs[name][0]
        if name in (NORM, H):
            source = source[0]
        pltpu.make_async_copy(source, getattr(self.refs, name), self.refs.input_s.at[self.LOADS.index(name)]).wait()

    def fetch_next(self, l, *names, second=False):
        @pl.when(l == 1)
        def _():
            for name in names:
                self.fetch(name, 0, second)

    def stage_copy(self, at, g):
        return pltpu.make_async_copy(self.refs.staged.at[at], self.source.at[g], self.refs.staged_s.at[at])

    def core_copy(self, i):
        r = self.refs
        rows = pl.ds(pl.multiple_of(i * ROWS, ROWS), ROWS)
        return self.copy(
            r.pre.at[rows, pl.ds(0, self.D)], r.came.at[rows], r.core_s.at[i], r.core_r.at[i],
            (self.dp, 1 - self.core),
        )

    def partial(self, make, wait):
        @pl.when(wait)
        def _():
            pl.semaphore_wait(self.refs.core_c, 1)

        def block(i, carry):
            rows = pl.ds(pl.multiple_of(i * ROWS, ROWS), ROWS)
            self.refs.pre[rows, 0 : self.D] = make(rows)
            self.core_copy(i).start()
            return carry

        lax.fori_loop(0, self.T // ROWS, block, 0)

    def norm_back(self, l, which, more, after):
        r, D = self.refs, self.D
        gain = self.gain[l, which : which + 1]
        n = 128
        blocks = ROWS // n

        def block(i, carry):
            @pl.when(lax.rem(i, blocks) == 0)
            def _():
                copy = self.core_copy(lax.div(i, blocks))
                copy.wait_send()
                copy.wait_recv()

            rows = pl.ds(pl.multiple_of(i * n, n), n)
            xhat, rstd = norm_parts(r.h[rows])
            d = r.pre[rows, 0:D] + r.came[rows]
            e = d * gain
            spread = xhat * jnp.mean(e * xhat, axis=-1, keepdims=True)
            new = r.g[rows] + rstd * (e - jnp.mean(e, axis=-1, keepdims=True) - spread)
            r.g[rows] = new
            rounded = new.astype(jnp.bfloat16)
            r.low[rows] = rounded
            return (
                carry[0] + jnp.sum(d * xhat, axis=0, keepdims=True),
                carry[1] + jnp.sum(d, axis=0, keepdims=True),
                carry[2] + jnp.sum(rounded.astype(jnp.float32), axis=0, keepdims=True),
            )

        zero = jnp.zeros((1, D), jnp.float32)
        sums = lax.fori_loop(0, self.T // n, block, (zero, zero, zero))
        self.row(l, GAIN + which)[...] = sums[0]
        self.row(l, SHIFT + which)[...] = sums[1]
        after(sums[2])

        @pl.when(more)
        def _():
            pl.semaphore_signal(
                r.core_c, inc=1, device_id=(self.dp, 1 - self.core), device_id_type=MESH
            )

    def row(self, l, at, start=0, size=None):
        size = self.D if size is None else size
        return self.refs.small.at[pl.ds(l * SMALL + at, 1), start : start + size]

    def outer(self, left, left_at, right, right_at, at, job):
        for u in range(2):
            a = left[:, pl.ds(pl.multiple_of(left_at + u * UNIT, 128), UNIT)]
            self.refs.staged[at, u] = dot(a, right[:, right_at * UNIT : (right_at + 1) * UNIT], TN)
        self.stage_copy(at, job).start()

    def shrink_job(self, i, job):
        self.outer(self.refs.act, i // 2 * 2 * UNIT, self.refs.low, i % 2, i % 2, job)

    def expand_job(self, i, job):
        self.outer(self.refs.norm, 0, self.refs.act, i, i % 2, job)

    def slopes(self, first, last, l):
        r, F, D = self.refs, self.F, self.D

        def one(i, carry):
            rows = pl.ds(pl.multiple_of(i * ROWS, ROWS), ROWS)
            sums = []
            for c in range(0, F, 512):
                d_act = dot(r.low[rows], r.w_shrink[c : c + 512], NT)
                d_pre = (d_act * gelu_slope(r.pre[rows, c : c + 512])).astype(jnp.bfloat16)
                r.act[rows, c : c + 512] = d_pre
                sums.append(carry[c // 512] + jnp.sum(d_pre.astype(jnp.float32), axis=0, keepdims=True))
            return tuple(sums)

        sums = lax.fori_loop(first, last, one, (jnp.zeros((1, 512), jnp.float32),) * (F // 512))
        for i, part in enumerate(sums):
            for j in range(2):
                at = i * 512 + j * 256
                row = self.row(l, HIDDEN + at // D, at % D, 256)
                row[...] = row[...] + part[:, j * 256 : (j + 1) * 256]

    def piece(self, p, l):
        r = self.refs
        T, W = self.T, self.W
        blocks = T // ROWS
        base = (1 - l) * PER_LAYER
        for q, job in LATE.get(p - 1, ()):
            self.stage_copy(q, base + job).wait()
        if p == 0:
            self.arrive(ACT)

            @pl.when(l == 1)
            def _():
                pltpu.make_async_copy(self.cotangent, r.low, r.cot_s).wait()
                for name in self.LOADS[1:]:
                    self.fetch(name, 1, second=True)

            self.shrink_job(0, base)
            self.stage_copy(0, base).wait()
        elif p in (1, 2, 3):
            self.shrink_job(p, base + p)
        elif p == 4:
            @pl.when(l == 1)
            def _():
                def widen(i, carry):
                    rows = pl.ds(pl.multiple_of(i * ROWS, ROWS), ROWS)
                    wide = r.low[rows].astype(jnp.float32)
                    r.g[rows] = wide
                    return carry + jnp.sum(wide, axis=0, keepdims=True)

                self.row(l, BRANCH + 1)[...] = lax.fori_loop(0, blocks, widen, jnp.zeros((1, self.D), jnp.float32))

            self.arrive(W_SHRINK)
            self.arrive(PRE)
            self.slopes(0, blocks // 2, l)
        elif p == 5:
            self.slopes(blocks // 2, blocks, l)
            self.fetch_next(l, W_SHRINK)
        elif p == 6:
            self.arrive(W_EXPAND)
            self.partial(lambda rows: dot(r.act[rows], r.w_expand[...], NT), l == 0)
        elif p == 7:
            self.arrive(NORM)
            self.expand_job(0, base + 4)
            self.expand_job(1, base + 5)
            self.stage_copy(0, base + 4).wait()
        elif p == 8:
            self.expand_job(2, base + 6)
            self.expand_job(3, base + 7)
            self.fetch_next(l, W_EXPAND, ACT)
            for layer in range(2):
                @pl.when(l == layer)
                def _():
                    self.fetch(NORM, layer)
        elif p == 9:
            self.arrive(H)

            def after(total):
                self.row(l, BRANCH)[...] = total

            self.norm_back(l, 1, jnp.bool_(True), after)
            for layer in range(2):
                @pl.when(l == layer)
                def _():
                    self.fetch(H, layer)
        elif p == 10:
            self.arrive(W_MERGE)
            self.arrive(ATT)

            def one(i, carry):
                rows = pl.ds(pl.multiple_of(i * ROWS, ROWS), ROWS)
                r.datt[rows] = dot(r.low[rows], r.w_merge[...], NT).astype(jnp.bfloat16)
                return carry

            lax.fori_loop(0, blocks, one, 0)
            for u in range(2):
                r.staged[0, u] = dot(r.att[...], r.low[:, u * UNIT : (u + 1) * UNIT], TN)
            self.stage_copy(0, base + 8).start()
        elif p in ATTEND:
            if p == ATTEND[0]:
                self.fetch_next(l, W_MERGE, ATT)
                self.arrive(Q)
                self.arrive(K)
                self.arrive(V)
            i = p - ATTEND[0]
            self.attend_back(i // 2, l, i % 2)
            if p == ATTEND[-1]:
                self.fetch_next(l, Q, K, V)
        elif p == 17:
            self.arrive(W_HEADS)

            def make(rows):
                total = dot(r.dqkv[0, rows], r.w_heads[0], NT)
                for c in (1, 2):
                    total = total + dot(r.dqkv[c, rows], r.w_heads[c], NT)
                return total

            self.partial(make, jnp.bool_(True))
            self.fetch_next(l, W_HEADS)
        elif p == 18:
            self.arrive(NORM)
            self.heads_job(0, base + 9)
            self.stage_copy(0, base + 9).wait()
        elif p == 19:
            self.heads_job(1, base + 10)
            self.heads_job(2, base + 11)
            for i, c in enumerate((0, 2)):
                self.row(l, OFFSETS, i * W, W)[...] = jnp.sum(r.dqkv[c].astype(jnp.float32), axis=0, keepdims=True)
            self.fetch_next(l, NORM, second=True)
            for c in (1, 2):
                self.stage_copy(c % 2, base + 9 + c).wait()
        else:
            self.arrive(H)

            def after(total):
                @pl.when(l == 1)
                def _():
                    self.row(0, BRANCH + 1)[...] = total

            self.norm_back(l, 0, l == 1, after)
            self.fetch_next(l, PRE)
            self.fetch_next(l, H, second=True)

            @pl.when(l == 0)
            def _():
                pltpu.make_async_copy(r.low, self.grad_tokens, r.tokens_s).start()

    def heads_job(self, c, job):
        r = self.refs
        for u in range(2):
            r.staged[c % 2, u] = dot(r.norm[:, u * UNIT : (u + 1) * UNIT], r.dqkv[c], TN)
        self.stage_copy(c % 2, job).start()

    def attend_back(self, pair, l, turn):
        r = self.refs
        T = self.T
        lanes = slice(pair * 128, (pair + 1) * 128)
        if turn == 0:
            r.dk[...] = jnp.zeros((T, 128), jnp.float32)
            r.dv[...] = jnp.zeros((T, 128), jnp.float32)
        lane = lax.broadcasted_iota(jnp.int32, (1, 128), 1)
        blocks = T // ROWS
        for b in range(blocks - 1) if turn == 0 else (blocks - 1,):
            rows, end = slice(b * ROWS, (b + 1) * ROWS), (b + 1) * ROWS
            query = b * ROWS + lax.broadcasted_iota(jnp.int32, (1, ROWS), 1)
            lowest = query - jnp.concatenate([self.positions[j : j + 1] for j in range(2 * b, 2 * b + 2)], axis=1)
            key = lax.broadcasted_iota(jnp.int32, (end, ROWS), 0)
            allowed = (key <= query) & (key >= lowest)
            q, d = r.q[rows, lanes], r.datt[rows, lanes]
            k, v = r.k[0:end, lanes], r.v[0:end, lanes]
            dq = jnp.zeros((ROWS, 128), jnp.float32)
            for side in range(2):
                mine = (lax.div(lane, 64) == side).astype(jnp.float32)
                low, eighth = mine.astype(jnp.bfloat16), (mine * 0.125).astype(jnp.bfloat16)
                q_own, d_own = q * eighth, d * low
                scores = dot(k, q_own, NT)
                lse = self.lse[l, pair * 2 + side : pair * 2 + side + 1, rows]
                probs = jnp.where(allowed, jnp.exp(scores - lse), 0.0)
                dprob = dot(v, d_own, NT)
                centre = jnp.sum(probs * dprob, axis=0, keepdims=True)
                dscore = (probs * (dprob - centre)).astype(jnp.bfloat16)
                r.dv[0:end] = r.dv[0:end] + dot(probs.astype(jnp.bfloat16), d_own, NN)
                r.dk[0:end] = r.dk[0:end] + dot(dscore, q_own, NN)
                dq = dq + dot(dscore, k * eighth, TN)
            r.dqkv[0, rows, lanes] = dq.astype(jnp.bfloat16)
        if turn == 1:
            r.dqkv[1, :, lanes] = r.dk[...].astype(jnp.bfloat16)
            r.dqkv[2, :, lanes] = r.dv[...].astype(jnp.bfloat16)

    def small_swap(self, step):
        r = self.refs
        z = self.z
        to = (
            self.dp + self.step_x,
            self.dp + self.step_y,
            self.dp + 4 - 8 * lax.rem(z, 2),
            self.dp + 8 - 16 * lax.div(z, 2),
        )[step]
        return self.copy(
            r.small, r.small_in.at[step], r.small_s.at[step], r.small_r.at[step], (to, self.core)
        )

    def small_stage(self, step):
        if step > 0:
            copy = self.small_swap(step - 1)
            copy.wait_send()
            copy.wait_recv()
            self.refs.small[...] = self.refs.small[...] + self.refs.small_in[step - 1]
        if step < 4:
            self.small_swap(step).start()

    def run(self):
        r = self.refs
        pltpu.make_async_copy(self.cotangent, r.low, r.cot_s).start()
        self.fetch(ACT, 1)
        r.small[...] = jnp.zeros(r.small.shape, jnp.float32)
        far = (self.dp + 8 - 16 * lax.div(self.z, 2), self.core)
        self.barrier(((self.dp, 1 - self.core), far))

        def step(t, carry):
            l = 1 - lax.div(t, PIECES)
            for p in range(PIECES):
                @pl.when((lax.rem(t, PIECES) == p) & (t < 2 * PIECES))
                def _():
                    self.piece(p, l)

            for s in range(5):
                @pl.when(t == 2 * PIECES + s)
                def _():
                    self.small_stage(s)

            self.tick(t)
            return carry

        lax.fori_loop(0, self.ticks, step, 0)
        pltpu.make_async_copy(r.low, self.grad_tokens, r.tokens_s).wait()
        self.small_out[...] = r.small[...]


def backward(kept, weights, gain, lse, positions, cotangent, slots=6, lags=(2, 1, 1, 1, 1, 1, 1, 1, 3)):
    D = cotangent.shape[1]
    _, T, W = kept[1].shape
    jobs = 2 * PER_LAYER
    plan = Backward(2 * jobs, UNIT // 2, UNIT, slots, lags)
    plan.T, plan.D, plan.W, plan.F = T, D, W, weights[0].shape[1]
    scratch = plan.scratch() | plan.more_scratch()
    n = len(kept)

    def kernel(*refs):
        layers = [[ref.at[i] for i in range(2)] for ref in refs[:n]]
        norm1, q, k, v, att, h_mid, norm2, pre, act, h = layers
        plan.inputs = dict(zip(plan.LOADS, (act, pre, list(zip(norm1, norm2)), list(zip(h, h_mid)), att, q, k, v)))
        for name, weight in zip((W_SHRINK, W_EXPAND, W_MERGE, W_HEADS), refs[n : n + 4]):
            plan.inputs[name] = [weight.at[i] for i in range(2)]
        plan.cotangent, plan.gain, plan.lse, plan.positions = refs[n + 4 : n + 8]
        plan.target, plan.source, plan.grad_tokens, plan.small_out = refs[n + 8 : n + 12]
        plan.setup(SimpleNamespace(**dict(zip(scratch, refs[n + 12 :]))))
        plan.run()

    hbm = pl.BlockSpec(memory_space=pl.ANY)
    vmem = pl.BlockSpec(memory_space=pltpu.VMEM)
    flat = jax.ShapeDtypeStruct((jobs, 2, UNIT, UNIT), jnp.float32)
    target, _, grad_tokens, small = pl.pallas_call(
        kernel,
        out_shape=(
            flat,
            flat,
            jax.ShapeDtypeStruct((T, D), jnp.bfloat16),
            jax.ShapeDtypeStruct((2 * SMALL, D), jnp.float32),
        ),
        in_specs=[hbm] * (n + 5) + [vmem] * 3,
        out_specs=(hbm, hbm, hbm, vmem),
        scratch_shapes=list(scratch.values()),
        compiler_params=pltpu.CompilerParams(
            collective_id=0, has_side_effects=True, vmem_limit_bytes=61 * 2**20
        ),
    )(*kept, *weights, cotangent, gain, lse, positions)
    return target, grad_tokens, small


def gelu(x):
    return 0.5 * x * (1.0 + jnp.tanh(0.7978845608028654 * (x + 0.044715 * x * x * x)))


class Forward:
    KEPT = (NORM1, Q, K, V, ATT, H_MID, NORM2, PRE, ACT, H)

    WEIGHTS = (HEADS, MERGE, EXPAND, SHRINK)

    def scratch(self):
        T, D, W, F = self.T, self.D, self.W, self.F
        low, full = jnp.bfloat16, jnp.float32
        dma = pltpu.SemaphoreType.DMA
        n = T // ROWS
        return dict(
            norm1=pltpu.VMEM((T, D), low), q=pltpu.VMEM((T, W), low), k=pltpu.VMEM((T, W), low), v=pltpu.VMEM((T, W), low),
            att=pltpu.VMEM((T, W), low), h_mid=pltpu.VMEM((T, D), full), norm2=pltpu.VMEM((T, D), low),
            pre=pltpu.VMEM((T, F), full), act=pltpu.VMEM((T, F), low), h=pltpu.VMEM((T, D), full),
            low=pltpu.VMEM((T, D), low), part=pltpu.VMEM((2, T, D), full), came=pltpu.VMEM((2, T, D), full),
            bias=pltpu.VMEM((n, ROWS, T), full),
            heads=pltpu.VMEM((2, 3, D, W), low), merge=pltpu.VMEM((2, W, D), low),
            expand=pltpu.VMEM((2, D, F), low), shrink=pltpu.VMEM((2, F, D), low),
            kept_s=dma((len(self.KEPT), n)), weight_s=dma((4, 2)), token_s=dma, out_s=dma((n,)),
            core_s=dma((2, n)), core_r=dma((2, n)),
        )

    def rows(self, b):
        return pl.ds(pl.multiple_of(b * ROWS, ROWS), ROWS)

    def keep_copy(self, name, l, b):
        at = self.rows(b)
        return pltpu.make_async_copy(
            getattr(self.refs, name).at[at], self.kept[name].at[l, at], self.refs.kept_s.at[self.KEPT.index(name), b]
        )

    def free(self, l, b, *names):
        @pl.when(l == 1)
        def _():
            for name in names:
                self.keep_copy(name, 0, b).wait()

    def keep(self, l, b, *names):
        for name in names:
            self.keep_copy(name, l, b).start()

    def weight_copy(self, name, l):
        at = self.WEIGHTS.index(name)
        return pltpu.make_async_copy(self.weights[name].at[l], getattr(self.refs, name).at[l], self.refs.weight_s.at[at, l])

    def core_copy(self, kind, b):
        r, at = self.refs, self.rows(b)
        return pltpu.make_async_remote_copy(
            src_ref=r.part.at[kind, at], dst_ref=r.came.at[kind, at],
            send_sem=r.core_s.at[kind, b], recv_sem=r.core_r.at[kind, b],
            device_id=(lax.axis_index("dp"), 1 - lax.axis_index("tensor")), device_id_type=MESH,
        )

    def summed(self, kind, b):
        copy = self.core_copy(kind, b)
        copy.wait_send()
        copy.wait_recv()
        at = self.rows(b)
        return self.refs.part[kind, at] + self.refs.came[kind, at]

    def norm(self, x, l, which):
        xhat, _ = norm_parts(x)
        return (xhat * self.gain[l, which : which + 1] + self.shift[l, which : which + 1]).astype(jnp.bfloat16)

    def before_first(self, l, b):
        r, at = self.refs, self.rows(b)
        self.free(l, b, H, NORM1, Q, K, V)

        @pl.when(l == 0)
        def _():
            r.h[at] = r.low[at].astype(jnp.float32)

        @pl.when(l == 1)
        def _():
            r.h[at] = r.h_mid[at] + (self.summed(1, b) + self.branch[0, 1:2])

    def first(self, l, b):
        r, at = self.refs, self.rows(b)
        low = self.norm(r.h[at], l, 0)
        r.norm1[at] = low
        r.q[at] = (dot(low, r.heads[l, 0], NN) + self.offsets[l, 0:1]).astype(jnp.bfloat16)
        r.k[at] = dot(low, r.heads[l, 1], NN).astype(jnp.bfloat16)
        r.v[at] = (dot(low, r.heads[l, 2], NN) + self.offsets[l, 1:2]).astype(jnp.bfloat16)

    def after_first(self, l, b):
        self.keep(l, b, H, NORM1, Q, K, V)

    def mix(self, l, b):
        r, at = self.refs, self.rows(b)
        self.free(l, b, ATT)
        for i in range(self.T // ROWS):
            @pl.when(b == i)
            def _():
                self.attend(l, i)

        r.part[0, at] = dot(r.att[at], r.merge[l], NN)
        self.core_copy(0, b).start()
        self.keep(l, b, ATT)

    def attend(self, l, b):
        r = self.refs
        rows, end = slice(b * ROWS, (b + 1) * ROWS), (b + 1) * ROWS

        @pl.when(l == 0)
        def _():
            query = b * ROWS + lax.broadcasted_iota(jnp.int32, (ROWS, 1), 0)
            spread = jnp.concatenate([self.positions[...].astype(jnp.float32)] * 16, axis=0).T
            column = jnp.concatenate([spread[:, j : j + 1] for j in range(2 * b, 2 * b + 2)], axis=0)
            lowest = query - column.astype(jnp.int32)
            key = lax.broadcasted_iota(jnp.int32, (ROWS, end), 1)
            r.bias[b, :, 0:end] = jnp.where((key <= query) & (key >= lowest), 0.0, -1e30)

        lane = lax.broadcasted_iota(jnp.int32, (1, 128), 1)
        logs = jnp.zeros((ROWS, 128), jnp.float32)
        for pair in range(self.W // 128):
            lanes = slice(pair * 128, (pair + 1) * 128)
            q, k, v = r.q[rows, lanes], r.k[0:end, lanes], r.v[0:end, lanes]
            total = jnp.zeros((ROWS, 128), jnp.float32)
            for side in range(2):
                mine = (lax.div(lane, 64) == side).astype(jnp.float32)
                scores = dot(q * (mine * 0.125).astype(jnp.bfloat16), k, NT) + r.bias[b, :, 0:end]
                highest = jnp.max(scores, axis=-1, keepdims=True)
                weights = jnp.exp(scores - highest)
                amount = jnp.sum(weights, axis=-1, keepdims=True)
                probs = (weights * (1.0 / amount)).astype(jnp.bfloat16)
                total = total + dot(probs, v * mine.astype(jnp.bfloat16), NN)
                logs = jnp.where(lane == pair * 2 + side, highest + jnp.log(amount), logs)
            r.att[rows, lanes] = total.astype(jnp.bfloat16)
        self.lse[l, :, rows] = logs.T[0:8]

    def before_second(self, l, b):
        self.free(l, b, H_MID, NORM2, PRE, ACT)
        copy = self.core_copy(0, b)
        copy.wait_send()
        copy.wait_recv()

    def second(self, l, b):
        r, at = self.refs, self.rows(b)
        middle = r.h[at] + (r.part[0, at] + r.came[0, at] + self.branch[l, 0:1])
        r.h_mid[at] = middle
        low = self.norm(middle, l, 1)
        r.norm2[at] = low
        for c in range(0, self.F, 512):
            pre = dot(low, r.expand[l, :, c : c + 512], NN) + self.hidden[pl.ds(l, 1), c : c + 512]
            r.pre[at, c : c + 512] = pre
            r.act[at, c : c + 512] = gelu(pre).astype(jnp.bfloat16)
        r.part[1, at] = dot(r.act[at], r.shrink[l], NN)

    def after_second(self, l, b):
        self.core_copy(1, b).start()
        self.keep(l, b, H_MID, NORM2, PRE, ACT)

    def finish(self, b):
        r, at = self.refs, self.rows(b)
        r.low[at] = (r.h_mid[at] + (self.summed(1, b) + self.branch[1, 1:2])).astype(jnp.bfloat16)
        pltpu.make_async_copy(r.low.at[at], self.output.at[at], r.out_s.at[b]).start()

    def run(self):
        r = self.refs
        n = self.T // ROWS
        load = pltpu.make_async_copy(self.tokens, r.low, r.token_s)
        load.start()
        for name in self.WEIGHTS:
            self.weight_copy(name, 0).start()
        other = (lax.axis_index("dp"), 1 - lax.axis_index("tensor"))
        bar = pltpu.get_barrier_semaphore()
        pl.semaphore_signal(bar, inc=1, device_id=other, device_id_type=MESH)
        pl.semaphore_wait(bar, 1)
        load.wait()

        self.weight_copy(HEADS, 0).wait()
        self.before_first(0, 0)
        self.first(0, 0)
        self.after_first(0, 0)

        def turn(t, carry):
            for l in range(2):
                @pl.when(t == l * n)
                def _():
                    self.weight_copy(MERGE, l).wait()

            @pl.when(t < 2 * n)
            def _():
                self.mix(lax.div(t, n), lax.rem(t, n))

            for l in range(2):
                @pl.when(t == l * n + 1)
                def _():
                    self.weight_copy(EXPAND, l).wait()
                    self.weight_copy(SHRINK, l).wait()

            @pl.when(t == 1)
            def _():
                for name in self.WEIGHTS:
                    self.weight_copy(name, 1).start()

            @pl.when(t == n - 1)
            def _():
                self.weight_copy(HEADS, 1).wait()

            old, new = t - 1, t + 1
            goes = (new < 2 * n, lax.div(new, n), lax.rem(new, n))
            comes = ((old >= 0) & (old < 2 * n), lax.div(old, n), lax.rem(old, n))

            @pl.when(comes[0])
            def _():
                self.before_second(*comes[1:])

            @pl.when(goes[0])
            def _():
                self.before_first(*goes[1:])

            @pl.when(comes[0] & goes[0])
            def _():
                self.second(*comes[1:])
                self.first(*goes[1:])

            @pl.when(comes[0] & jnp.logical_not(goes[0]))
            def _():
                self.second(*comes[1:])

            @pl.when(goes[0] & jnp.logical_not(comes[0]))
            def _():
                self.first(*goes[1:])

            @pl.when(comes[0])
            def _():
                self.after_second(*comes[1:])

            @pl.when(goes[0])
            def _():
                self.after_first(*goes[1:])

            @pl.when(t >= n + 2)
            def _():
                self.finish(t - n - 2)

            return carry

        lax.fori_loop(0, 2 * n + 2, turn, 0)
        for b in range(n):
            for name in self.KEPT:
                self.keep_copy(name, 1, b).wait()
            pltpu.make_async_copy(r.low.at[self.rows(b)], self.output.at[self.rows(b)], r.out_s.at[b]).wait()


def forward(tokens, positions, weights, rows):
    plan = Forward()
    T, D = tokens.shape
    plan.T, plan.D, plan.W, plan.F = T, D, weights[0].shape[3], weights[2].shape[2]
    scratch = plan.scratch()
    kinds = plan.KEPT

    def kernel(tokens, heads, merge, expand, shrink, positions, gain, shift, offsets, branch, hidden, output, lse, *refs):
        plan.tokens, plan.positions, plan.output, plan.lse = tokens, positions, output, lse
        plan.weights = dict(zip(plan.WEIGHTS, (heads, merge, expand, shrink)))
        plan.gain, plan.shift, plan.offsets, plan.branch, plan.hidden = gain, shift, offsets, branch, hidden
        plan.kept = dict(zip(kinds, refs))
        plan.refs = SimpleNamespace(**dict(zip(scratch, refs[len(kinds) :])))
        plan.run()

    hbm = pl.BlockSpec(memory_space=pl.ANY)
    vmem = pl.BlockSpec(memory_space=pltpu.VMEM)
    kept_shapes = [jax.ShapeDtypeStruct((2,) + scratch[name].shape, scratch[name].dtype) for name in kinds]
    out = pl.pallas_call(
        kernel,
        out_shape=[jax.ShapeDtypeStruct((T, D), jnp.bfloat16), jax.ShapeDtypeStruct((2, 8, T), jnp.float32)] + kept_shapes,
        in_specs=[hbm] * 5 + [vmem] * 6,
        out_specs=[hbm, vmem] + [hbm] * len(kept_shapes),
        scratch_shapes=list(scratch.values()),
        compiler_params=pltpu.CompilerParams(
            collective_id=1, has_side_effects=True, vmem_limit_bytes=61 * 2**20
        ),
    )(tokens, *weights, positions, *rows)
    return out[0], out[1], out[2:]


def spread(flat, small, shapes, dtype=jnp.float32):
    half = flat.shape[0] // 2
    width = small.shape[1]

    def kernel(source, sums, gain, shift, heads, offsets, merge, branch, expand, hidden, shrink, held, into, out):
        loads, copies = [], []

        def put(g, u, target):
            i = len(copies)
            loads.append(pltpu.make_async_copy(source.at[g, u], held.at[i], into.at[i]))
            copies.append(pltpu.make_async_copy(held.at[i], target, out.at[i]))
            loads[-1].start()

        for l in range(2):
            base = (1 - l) * half
            for u in range(2):
                rows = pl.ds(u * UNIT, UNIT)
                for i in range(4):
                    at = pl.ds((i // 2) * 2 * UNIT + u * UNIT, UNIT)
                    put(base + i, u, shrink.at[l, at, pl.ds((i % 2) * UNIT, UNIT)])
                    put(base + 4 + i, u, expand.at[l, rows, pl.ds(i * UNIT, UNIT)])
                put(base + 8, u, merge.at[l, :, rows])
                for c in range(3):
                    put(base + 9 + c, u, heads.at[l, c, rows])
            for target, at in ((gain, GAIN), (shift, SHIFT), (branch, BRANCH)):
                target[l] = sums[l * SMALL + at : l * SMALL + at + 2]
            for i in range(2):
                at = l * SMALL + HIDDEN + i
                hidden[l : l + 1, i * width : (i + 1) * width] = sums[at : at + 1]
                at = l * SMALL + OFFSETS
                offsets[l, i : i + 1] = sums[at : at + 1, i * UNIT : (i + 1) * UNIT]
        for load, copy in zip(loads, copies):
            load.wait()
            copy.start()
        for copy in copies:
            copy.wait()

    hbm = pl.BlockSpec(memory_space=pl.ANY)
    vmem = pl.BlockSpec(memory_space=pltpu.VMEM)
    return pl.pallas_call(
        kernel,
        out_shape=[jax.ShapeDtypeStruct(s, dtype) for s in shapes],
        in_specs=[hbm, vmem],
        out_specs=[vmem, vmem, hbm, vmem, hbm, vmem, hbm, vmem, hbm],
        scratch_shapes=[
            pltpu.VMEM((2 * flat.shape[0], UNIT, UNIT), dtype),
            pltpu.SemaphoreType.DMA((2 * flat.shape[0],)),
            pltpu.SemaphoreType.DMA((2 * flat.shape[0],)),
        ],
        compiler_params=pltpu.CompilerParams(has_side_effects=True, vmem_limit_bytes=48 * 2**20),
    )(flat, small)


def on_device(
    tokens,
    positions,
    norm_gain,
    norm_shift,
    heads_weight,
    offsets,
    merge_weight,
    branch_bias,
    expand_weight,
    hidden_bias,
    shrink_weight,
    cotangent,
):
    rows = (norm_gain, norm_shift, offsets, branch_bias, hidden_bias)
    places = positions.reshape(-1, 128)
    output, lse, kept = forward(
        tokens, places, (heads_weight, merge_weight, expand_weight, shrink_weight), rows
    )
    flat, grad_tokens, small = backward(
        kept, (shrink_weight, expand_weight, merge_weight, heads_weight), norm_gain, lse, places, cotangent
    )
    ranks = lax.axis_size("dp")
    if ranks > BLOCK:
        groups = [[j * BLOCK + i for j in range(ranks // BLOCK)] for i in range(BLOCK)]
        flat, small = lax.psum((flat, small), "dp", axis_index_groups=groups)
    shapes = [norm_gain, norm_shift, heads_weight, offsets, merge_weight, branch_bias, expand_weight, hidden_bias, shrink_weight]
    return (output, grad_tokens, *spread(flat, small, [like.shape for like in shapes]))


def solution(mesh):
    placed = (
        P("dp", None),
        P("dp"),
        P(),
        P(),
        P(None, None, None, "tensor"),
        P(None, None, "tensor"),
        P(None, "tensor", None),
        P(),
        P(None, None, "tensor"),
        P(None, "tensor"),
        P(None, "tensor", None),
        P("dp", None),
    )
    return jax.shard_map(
        on_device,
        mesh=mesh,
        in_specs=placed,
        out_specs=(
            P("dp", None),
            P("dp", None),
            P(),
            P(),
            P(None, None, None, "tensor"),
            P(None, None, "tensor"),
            P(None, "tensor", None),
            P(),
            P(None, None, "tensor"),
            P(None, "tensor"),
            P(None, "tensor", None),
        ),
        check_vma=False,
    )
```

```python
from types import SimpleNamespace

import jax
import jax.numpy as jnp
from jax import lax
from jax.experimental import pallas as pl
from jax.experimental.pallas import tpu as pltpu
from jax.sharding import PartitionSpec as P

LAYERS = 2
UNIT = 384
BLOCK = 16
MESH = pl.DeviceIdType.MESH


class Exchange:
    def __init__(self, groups, rows, cols, slots, lags):
        self.groups, self.rows, self.cols, self.slots = groups, rows, cols, slots
        self.half = rows // 2
        self.chunk = self.half // 4
        starts = [0]
        for lag in lags:
            starts.append(starts[-1] + lag)
        self.starts = starts
        self.ticks = groups + starts[-1]
        self.last_slots = starts[9]
        self.gather_slots = max(starts[8] - starts[1], slots)

    def scratch(self):
        groups, slots, half, chunk, cols = self.groups, self.slots, self.half, self.chunk, self.cols
        dma = pltpu.SemaphoreType.DMA
        plain = pltpu.SemaphoreType.REGULAR
        return dict(
            held=pltpu.VMEM((self.held_slots(), 2, half, cols), jnp.float32),
            swap_in=pltpu.VMEM((slots, 2, half, cols), jnp.float32),
            chain_in=pltpu.VMEM((slots, 3, 2, 2, chunk, cols), jnp.float32),
            third_in=pltpu.VMEM((slots, 2, chunk, cols), jnp.float32),
            swap_s=dma((slots,)), swap_r=dma((slots,)),
            chain_s=dma((slots, 3, 2)), chain_r=dma((slots, 3, 2)),
            third_s=dma((slots,)), third_r=dma((slots,)),
            gather_s=dma((slots, 3, 2)), gather_r=dma((self.gather_slots, 3, 2)),
            last_s=dma((slots,)), last_r=dma((self.last_slots,)),
            own_s=dma((slots,)), load_s=dma((slots,)),
            swap_c=plain((2,)), chain_c=plain((3, 2)), third_c=plain((2,)),
        )

    def held_slots(self):
        return self.groups

    def setup(self, refs):
        self.refs = refs
        dp = lax.axis_index("dp")
        core = lax.axis_index("tensor")
        low = lax.rem(dp, 16)
        self.dp, self.core = dp, core
        self.z = lax.div(low, 4)
        self.y = lax.rem(lax.div(low, 2), 2)
        self.x = lax.rem(low, 2)
        self.step_x = 1 - 2 * self.x
        self.step_y = 2 - 4 * self.y
        self.along = ((dp + 4, core), (dp - 4, core))

    def barrier(self, others=()):
        z = self.z
        bar = pltpu.get_barrier_semaphore()

        def greet(device):
            pl.semaphore_signal(bar, inc=1, device_id=device, device_id_type=MESH)

        for device in ((self.dp + self.step_x, self.core), (self.dp + self.step_y, self.core)) + tuple(others):
            greet(device)

        @pl.when(z < 3)
        def _():
            greet(self.along[0])

        @pl.when(z > 0)
        def _():
            greet(self.along[1])

        pl.semaphore_wait(bar, 2 + len(others) + (z < 3).astype(jnp.int32) + (z > 0).astype(jnp.int32))

    def first(self, g):
        return (self.dp + jnp.where(lax.rem(g, 2) == 0, self.step_x, self.step_y), self.core)

    def third(self, g):
        return (self.dp + jnp.where(lax.rem(g, 2) == 0, self.step_y, self.step_x), self.core)

    def side(self, g):
        return jnp.where(lax.rem(g, 2) == 0, self.x, self.y)

    def copy(self, src, dst, send, recv, device):
        return pltpu.make_async_remote_copy(
            src_ref=src, dst_ref=dst, send_sem=send, recv_sem=recv, device_id=device, device_id_type=MESH
        )

    def rows_of(self, j):
        return pl.ds(pl.multiple_of(j * self.chunk, 8), self.chunk)

    def held(self, g):
        return self.refs.held.at[g]

    def swap(self, g):
        r, k = self.refs, lax.rem(g, self.slots)
        return self.copy(self.sent_half(g), r.swap_in.at[k], r.swap_s.at[k], r.swap_r.at[k], self.first(g))

    def chain_send(self, step, d, g):
        z, r, k = self.z, self.refs, lax.rem(g, self.slots)
        j = 4 - step + z if d == 0 else step - 4 + z
        here = ((z < 3) & (step > z)) if d == 0 else ((z > 0) & (step > 3 - z))
        at = (k, step - 1, d)
        part = self.held(g).at[:, self.rows_of(j)]
        return here, self.copy(part, r.chain_in.at[at], r.chain_s.at[at], r.chain_r.at[at], self.along[d])

    def start_chain(self, step, g):
        for d in range(2):
            here, copy = self.chain_send(step, d, g)

            @pl.when(here)
            def _():
                @pl.when(g >= self.slots)
                def _():
                    pl.semaphore_wait(self.refs.chain_c.at[step - 1, d], 1)

                copy.start()

    def finish_chain(self, step, g):
        z, r, k = self.z, self.refs, lax.rem(g, self.slots)
        for d in range(2):
            here, copy = self.chain_send(step, d, g)

            @pl.when(here)
            def _():
                copy.wait_send()

        for d in range(2):
            here = ((z >= 1) & (step >= z)) if d == 0 else ((z <= 2) & (step >= 3 - z))
            j = 3 - step + z if d == 0 else step - 3 + z
            at = (k, step - 1, d)

            @pl.when(here)
            def _():
                came = r.chain_in.at[at]
                self.copy(came, came, r.chain_s.at[at], r.chain_r.at[at], self.along[1 - d]).wait_recv()
                part = self.held(g).at[:, self.rows_of(j)]
                part[...] = part[...] + came[...]

                @pl.when(g + self.slots < self.groups)
                def _():
                    pl.semaphore_signal(
                        r.chain_c.at[step - 1, d], inc=1, device_id=self.along[1 - d], device_id_type=MESH
                    )

    def third_swap(self, g):
        r, k = self.refs, lax.rem(g, self.slots)
        part = self.held(g).at[:, self.rows_of(self.z)]
        return self.copy(part, r.third_in.at[k], r.third_s.at[k], r.third_r.at[k], self.third(g))

    def gather_copy(self, step, d, g, j, source=None):
        r, k = self.refs, lax.rem(g, self.slots)
        part = self.result(g, self.side(g) * self.half + j * self.chunk, self.chunk)
        return self.copy(
            part if source is None else source,
            part,
            r.gather_s.at[k, step - 1, d],
            r.gather_r.at[lax.rem(g, self.gather_slots), step - 1, d],
            self.along[d],
        )

    def gather_send(self, step, d, g):
        z = self.z
        j = z - (step - 1) if d == 0 else z + step - 1
        here = ((z < 3) & (step - 1 <= z)) if d == 0 else ((z > 0) & (z + step - 1 <= 3))
        source = self.held(g).at[:, self.rows_of(z)] if step == 1 else None
        return here, self.gather_copy(step, d, g, j, source)

    def start_gather(self, step, g):
        for d in range(2):
            here, copy = self.gather_send(step, d, g)

            @pl.when(here)
            def _():
                copy.start()

    def finish_gather(self, step, g):
        z = self.z
        for d in range(2):
            here, copy = self.gather_send(step, d, g)

            @pl.when(here)
            def _():
                copy.wait_send()

        for d in range(2):
            here = (z >= step) if d == 0 else (z + step <= 3)
            j = z - step if d == 0 else z + step

            @pl.when(here)
            def _():
                self.gather_copy(step, d, g, j).wait_recv()

    def own_copy(self, g):
        k = lax.rem(g, self.slots)
        part = self.held(g).at[:, self.rows_of(self.z)]
        return pltpu.make_async_copy(
            part, self.result(g, self.side(g) * self.half + self.z * self.chunk, self.chunk), self.refs.own_s.at[k]
        )

    def last(self, g):
        r, k = self.refs, lax.rem(g, self.slots)
        part = self.result(g, self.side(g) * self.half, self.half)
        return self.copy(part, part, r.last_s.at[k], r.last_r.at[lax.rem(g, self.last_slots)], self.first(g))

    def stage(self, e, g):
        r, slots, groups = self.refs, self.slots, self.groups
        k = lax.rem(g, slots)
        if e == 0:
            self.prepare(g)

            @pl.when(g >= slots)
            def _():
                pl.semaphore_wait(r.swap_c.at[lax.rem(g, 2)], 1)

            self.swap(g).start()
        elif e == 1:
            self.settle(g)
            copy = self.swap(g)
            copy.wait_send()
            copy.wait_recv()
            mine = self.held(g)
            mine[...] = mine[...] + r.swap_in[k]

            @pl.when(g + slots < groups)
            def _():
                pl.semaphore_signal(
                    r.swap_c.at[lax.rem(g, 2)], inc=1, device_id=self.first(g), device_id_type=MESH
                )

            self.start_chain(1, g)
        elif e in (2, 3):
            self.finish_chain(e - 1, g)
            self.start_chain(e, g)
        elif e == 4:
            self.finish_chain(3, g)

            @pl.when(g >= slots)
            def _():
                pl.semaphore_wait(r.third_c.at[lax.rem(g, 2)], 1)

            self.third_swap(g).start()
        elif e == 5:
            copy = self.third_swap(g)
            copy.wait_send()
            copy.wait_recv()
            part = self.held(g).at[:, self.rows_of(self.z)]
            part[...] = part[...] + r.third_in[k]

            @pl.when(g + slots < groups)
            def _():
                pl.semaphore_signal(
                    r.third_c.at[lax.rem(g, 2)], inc=1, device_id=self.third(g), device_id_type=MESH
                )

            self.start_gather(1, g)
            self.own_copy(g).start()
        elif e in (6, 7):
            self.finish_gather(e - 5, g)
            if e == 6:
                self.own_copy(g).wait()
            self.start_gather(e - 4, g)
        elif e == 8:
            self.finish_gather(3, g)
            self.last(g).start()
        else:
            copy = self.last(g)
            copy.wait_send()
            copy.wait_recv()

    def tick(self, t):
        for e in reversed(range(10)):
            g = t - self.starts[e]

            @pl.when((g >= 0) & (g < self.groups))
            def _():
                self.stage(e, g)


class FlatExchange(Exchange):
    def part(self, whole, g, start, size):
        start = lax.rem(g, 2) * self.rows + start
        return whole.at[lax.div(g, 2), :, pl.ds(pl.multiple_of(start, 8), size)]

    def sent_half(self, g):
        return self.part(self.source, g, (1 - self.side(g)) * self.half, self.half)

    def load(self, g):
        k = lax.rem(g, self.slots)
        own = self.part(self.source, g, self.side(g) * self.half, self.half)
        return pltpu.make_async_copy(own, self.held(g), self.refs.load_s.at[k])

    def prepare(self, g):
        self.load(g).start()

    def settle(self, g):
        self.load(g).wait()

    def result(self, g, start, size):
        return self.part(self.target, g, start, size)


ROWS = 256


def dot(a, b, dims):
    return lax.dot_general(a, b, (dims, ((), ())), preferred_element_type=jnp.float32)


NN = ((1,), (0,))
NT = ((1,), (1,))
TN = ((0,), (0,))


def gelu_slope(x):
    t = jnp.tanh(0.7978845608028654 * (x + 0.044715 * x * x * x))
    return 0.5 * (1.0 + t) + 0.5 * x * (1.0 - t * t) * (
        0.7978845608028654 * (1.0 + 3.0 * 0.044715 * x * x)
    )


def norm_parts(h):
    centre = h - jnp.mean(h, axis=-1, keepdims=True)
    r = lax.rsqrt(jnp.mean(centre * centre, axis=-1, keepdims=True) + 1e-05)
    return centre * r, r


GAIN, SHIFT, BRANCH, HIDDEN, OFFSETS, SMALL = 0, 2, 4, 6, 8, 16
PIECES = 21
ATTEND = range(11, 17)
LATE = {1: ((1, 1),), 2: ((0, 2),), 3: ((1, 3),), 7: ((1, 5),), 8: ((0, 6), (1, 7)), 10: ((0, 8),)}
PER_LAYER = 12


ACT, PRE, NORM, H, ATT, Q, K, V = "act", "pre", "norm", "h", "att", "q", "k", "v"
W_SHRINK, W_EXPAND, W_MERGE, W_HEADS = "w_shrink", "w_expand", "w_merge", "w_heads"
NORM1, NORM2, H_MID = "norm1", "norm2", "h_mid"
SHRINK, EXPAND, MERGE, HEADS = "shrink", "expand", "merge", "heads"


class Backward(FlatExchange):
    LOADS = (ACT, PRE, NORM, H, ATT, Q, K, V, W_SHRINK, W_EXPAND, W_MERGE, W_HEADS)

    def more_scratch(self):
        T, D, W, F = self.T, self.D, self.W, self.F
        low, full = jnp.bfloat16, jnp.float32
        dma = pltpu.SemaphoreType.DMA
        return dict(
            act=pltpu.VMEM((T, F), low), pre=pltpu.VMEM((T, F), full), norm=pltpu.VMEM((T, D), low),
            h=pltpu.VMEM((T, D), full), att=pltpu.VMEM((T, W), low), q=pltpu.VMEM((T, W), low),
            k=pltpu.VMEM((T, W), low), v=pltpu.VMEM((T, W), low), w_shrink=pltpu.VMEM((F, D), low),
            w_expand=pltpu.VMEM((D, F), low), w_merge=pltpu.VMEM((W, D), low), w_heads=pltpu.VMEM((3, D, W), low),
            g=pltpu.VMEM((T, D), full), low=pltpu.VMEM((T, D), low), came=pltpu.VMEM((T, D), full),
            datt=pltpu.VMEM((T, W), low), dqkv=pltpu.VMEM((3, T, W), low),
            staged=pltpu.VMEM((2, 2, 384, 384), full), centre=pltpu.VMEM((8, T), full), dk=pltpu.VMEM((T, 128), full), dv=pltpu.VMEM((T, 128), full),
            small=pltpu.VMEM((2 * SMALL, D), full), small_in=pltpu.VMEM((4, 2 * SMALL, D), full),
            input_s=dma((len(self.LOADS),)), cot_s=dma, staged_s=dma((2,)), tokens_s=dma,
            core_s=dma((T // ROWS,)), core_r=dma((T // ROWS,)), core_c=pltpu.SemaphoreType.REGULAR,
            small_s=dma((4,)), small_r=dma((4,)),
        )

    def held_slots(self):
        return self.starts[6]

    def held(self, g):
        return self.refs.held.at[lax.rem(g, self.held_slots())]

    def fetch(self, name, layer, second=False):
        source = self.inputs[name][layer]
        if name in (NORM, H):
            source = source[1 if second else 0]
        pltpu.make_async_copy(source, getattr(self.refs, name), self.refs.input_s.at[self.LOADS.index(name)]).start()

    def arrive(self, name):
        source = self.inputs[name][0]
        if name in (NORM, H):
            source = source[0]
        pltpu.make_async_copy(source, getattr(self.refs, name), self.refs.input_s.at[self.LOADS.index(name)]).wait()

    def fetch_next(self, l, *names, second=False):
        @pl.when(l == 1)
        def _():
            for name in names:
                self.fetch(name, 0, second)

    def stage_copy(self, at, g):
        return pltpu.make_async_copy(self.refs.staged.at[at], self.source.at[g], self.refs.staged_s.at[at])

    def core_copy(self, i):
        r = self.refs
        rows = pl.ds(pl.multiple_of(i * ROWS, ROWS), ROWS)
        return self.copy(
            r.pre.at[rows, pl.ds(0, self.D)], r.came.at[rows], r.core_s.at[i], r.core_r.at[i],
            (self.dp, 1 - self.core),
        )

    def partial(self, make, wait):
        @pl.when(wait)
        def _():
            pl.semaphore_wait(self.refs.core_c, 1)

        def block(i, carry):
            rows = pl.ds(pl.multiple_of(i * ROWS, ROWS), ROWS)
            self.refs.pre[rows, 0 : self.D] = make(rows)
            self.core_copy(i).start()
            return carry

        lax.fori_loop(0, self.T // ROWS, block, 0)

    def norm_back(self, l, which, more, after):
        r, D = self.refs, self.D
        gain = self.gain[l, which : which + 1]
        n = 128
        blocks = ROWS // n

        def block(i, carry):
            @pl.when(lax.rem(i, blocks) == 0)
            def _():
                copy = self.core_copy(lax.div(i, blocks))
                copy.wait_send()
                copy.wait_recv()

            rows = pl.ds(pl.multiple_of(i * n, n), n)
            xhat, rstd = norm_parts(r.h[rows])
            d = r.pre[rows, 0:D] + r.came[rows]
            e = d * gain
            spread = xhat * jnp.mean(e * xhat, axis=-1, keepdims=True)
            new = r.g[rows] + rstd * (e - jnp.mean(e, axis=-1, keepdims=True) - spread)
            r.g[rows] = new
            rounded = new.astype(jnp.bfloat16)
            r.low[rows] = rounded
            return (
                carry[0] + jnp.sum(d * xhat, axis=0, keepdims=True),
                carry[1] + jnp.sum(d, axis=0, keepdims=True),
                carry[2] + jnp.sum(rounded.astype(jnp.float32), axis=0, keepdims=True),
            )

        zero = jnp.zeros((1, D), jnp.float32)
        sums = lax.fori_loop(0, self.T // n, block, (zero, zero, zero))
        self.row(l, GAIN + which)[...] = sums[0]
        self.row(l, SHIFT + which)[...] = sums[1]
        after(sums[2])

        @pl.when(more)
        def _():
            pl.semaphore_signal(
                r.core_c, inc=1, device_id=(self.dp, 1 - self.core), device_id_type=MESH
            )

    def row(self, l, at, start=0, size=None):
        size = self.D if size is None else size
        return self.refs.small.at[pl.ds(l * SMALL + at, 1), start : start + size]

    def outer(self, left, left_at, right, right_at, at, job):
        for u in range(2):
            a = left[:, pl.ds(pl.multiple_of(left_at + u * UNIT, 128), UNIT)]
            self.refs.staged[at, u] = dot(a, right[:, right_at * UNIT : (right_at + 1) * UNIT], TN)
        self.stage_copy(at, job).start()

    def shrink_job(self, i, job):
        self.outer(self.refs.act, i // 2 * 2 * UNIT, self.refs.low, i % 2, i % 2, job)

    def expand_job(self, i, job):
        self.outer(self.refs.norm, 0, self.refs.act, i, i % 2, job)

    def slopes(self, first, last, l):
        r, F, D = self.refs, self.F, self.D

        def one(i, carry):
            rows = pl.ds(pl.multiple_of(i * ROWS, ROWS), ROWS)
            sums = []
            for c in range(0, F, 512):
                d_act = dot(r.low[rows], r.w_shrink[c : c + 512], NT)
                d_pre = (d_act * gelu_slope(r.pre[rows, c : c + 512])).astype(jnp.bfloat16)
                r.act[rows, c : c + 512] = d_pre
                sums.append(carry[c // 512] + jnp.sum(d_pre.astype(jnp.float32), axis=0, keepdims=True))
            return tuple(sums)

        sums = lax.fori_loop(first, last, one, (jnp.zeros((1, 512), jnp.float32),) * (F // 512))
        for i, part in enumerate(sums):
            for j in range(2):
                at = i * 512 + j * 256
                row = self.row(l, HIDDEN + at // D, at % D, 256)
                row[...] = row[...] + part[:, j * 256 : (j + 1) * 256]

    def piece(self, p, l):
        r = self.refs
        T, W = self.T, self.W
        blocks = T // ROWS
        base = (1 - l) * PER_LAYER
        for q, job in LATE.get(p - 1, ()):
            self.stage_copy(q, base + job).wait()
        if p == 0:
            self.arrive(ACT)

            @pl.when(l == 1)
            def _():
                pltpu.make_async_copy(self.cotangent, r.low, r.cot_s).wait()
                for name in self.LOADS[1:]:
                    self.fetch(name, 1, second=True)

            self.shrink_job(0, base)
            self.stage_copy(0, base).wait()
        elif p in (1, 2, 3):
            self.shrink_job(p, base + p)
        elif p == 4:
            @pl.when(l == 1)
            def _():
                def widen(i, carry):
                    rows = pl.ds(pl.multiple_of(i * ROWS, ROWS), ROWS)
                    wide = r.low[rows].astype(jnp.float32)
                    r.g[rows] = wide
                    return carry + jnp.sum(wide, axis=0, keepdims=True)

                self.row(l, BRANCH + 1)[...] = lax.fori_loop(0, blocks, widen, jnp.zeros((1, self.D), jnp.float32))

            self.arrive(W_SHRINK)
            self.arrive(PRE)
            self.slopes(0, blocks // 2, l)
        elif p == 5:
            self.slopes(blocks // 2, blocks, l)
            self.fetch_next(l, W_SHRINK)
        elif p == 6:
            self.arrive(W_EXPAND)
            self.partial(lambda rows: dot(r.act[rows], r.w_expand[...], NT), l == 0)
        elif p == 7:
            self.arrive(NORM)
            self.expand_job(0, base + 4)
            self.expand_job(1, base + 5)
            self.stage_copy(0, base + 4).wait()
        elif p == 8:
            self.expand_job(2, base + 6)
            self.expand_job(3, base + 7)
            self.fetch_next(l, W_EXPAND, ACT)
            for layer in range(2):
                @pl.when(l == layer)
                def _():
                    self.fetch(NORM, layer)
        elif p == 9:
            self.arrive(H)

            def after(total):
                self.row(l, BRANCH)[...] = total

            self.norm_back(l, 1, jnp.bool_(True), after)
            for layer in range(2):
                @pl.when(l == layer)
                def _():
                    self.fetch(H, layer)
        elif p == 10:
            self.arrive(W_MERGE)
            self.arrive(ATT)
            lane = lax.broadcasted_iota(jnp.int32, (8, W), 1)
            heads = (lax.div(lane, 64) == lax.broadcasted_iota(jnp.int32, (8, W), 0)).astype(jnp.float32)

            def one(i, carry):
                rows = pl.ds(pl.multiple_of(i * ROWS, ROWS), ROWS)
                d = dot(r.low[rows], r.w_merge[...], NT).astype(jnp.bfloat16)
                r.datt[rows] = d
                r.centre[:, rows] = lax.dot_general(
                    heads, d.astype(jnp.float32) * r.att[rows].astype(jnp.float32), (NT, ((), ())),
                    precision=lax.Precision.HIGHEST, preferred_element_type=jnp.float32,
                )
                return carry

            lax.fori_loop(0, blocks, one, 0)
            for u in range(2):
                r.staged[0, u] = dot(r.att[...], r.low[:, u * UNIT : (u + 1) * UNIT], TN)
            self.stage_copy(0, base + 8).start()
        elif p in ATTEND:
            if p == ATTEND[0]:
                self.fetch_next(l, W_MERGE, ATT)
                self.arrive(Q)
                self.arrive(K)
                self.arrive(V)
            i = p - ATTEND[0]
            self.attend_back(i // 2, l, i % 2)
            if p == ATTEND[-1]:
                self.fetch_next(l, Q, K, V)
        elif p == 17:
            self.arrive(W_HEADS)

            def make(rows):
                total = dot(r.dqkv[0, rows], r.w_heads[0], NT)
                for c in (1, 2):
                    total = total + dot(r.dqkv[c, rows], r.w_heads[c], NT)
                return total

            self.partial(make, jnp.bool_(True))
            self.fetch_next(l, W_HEADS)
        elif p == 18:
            self.arrive(NORM)
            self.heads_job(0, base + 9)
            self.stage_copy(0, base + 9).wait()
        elif p == 19:
            self.heads_job(1, base + 10)
            self.heads_job(2, base + 11)
            for i, c in enumerate((0, 2)):
                self.row(l, OFFSETS, i * W, W)[...] = jnp.sum(r.dqkv[c].astype(jnp.float32), axis=0, keepdims=True)
            self.fetch_next(l, NORM, second=True)
            for c in (1, 2):
                self.stage_copy(c % 2, base + 9 + c).wait()
        else:
            self.arrive(H)

            def after(total):
                @pl.when(l == 1)
                def _():
                    self.row(0, BRANCH + 1)[...] = total

            self.norm_back(l, 0, l == 1, after)
            self.fetch_next(l, PRE)
            self.fetch_next(l, H, second=True)

            @pl.when(l == 0)
            def _():
                pltpu.make_async_copy(r.low, self.grad_tokens, r.tokens_s).start()

    def heads_job(self, c, job):
        r = self.refs
        for u in range(2):
            r.staged[c % 2, u] = dot(r.norm[:, u * UNIT : (u + 1) * UNIT], r.dqkv[c], TN)
        self.stage_copy(c % 2, job).start()

    def attend_back(self, pair, l, turn):
        r = self.refs
        T = self.T
        lanes = slice(pair * 128, (pair + 1) * 128)
        if turn == 0:
            r.dk[...] = jnp.zeros((T, 128), jnp.float32)
            r.dv[...] = jnp.zeros((T, 128), jnp.float32)
        lane = lax.broadcasted_iota(jnp.int32, (1, 128), 1)
        blocks = T // ROWS
        for b in range(blocks - 1) if turn == 0 else (blocks - 1,):
            rows, end = slice(b * ROWS, (b + 1) * ROWS), (b + 1) * ROWS
            query = b * ROWS + lax.broadcasted_iota(jnp.int32, (1, ROWS), 1)
            lowest = query - jnp.concatenate([self.positions[j : j + 1] for j in range(2 * b, 2 * b + 2)], axis=1)
            key = lax.broadcasted_iota(jnp.int32, (end, ROWS), 0)
            allowed = (key <= query) & (key >= lowest)
            q, d = r.q[rows, lanes], r.datt[rows, lanes]
            k, v = r.k[0:end, lanes], r.v[0:end, lanes]
            dq = jnp.zeros((ROWS, 128), jnp.float32)
            for side in range(2):
                mine = (lax.div(lane, 64) == side).astype(jnp.float32)
                low, eighth = mine.astype(jnp.bfloat16), (mine * 0.125).astype(jnp.bfloat16)
                q_own, d_own = q * eighth, d * low
                scores = dot(k, q_own, NT)
                lse = self.lse[l, pair * 2 + side : pair * 2 + side + 1, rows]
                probs = jnp.where(allowed, jnp.exp(scores - lse), 0.0)
                dprob = dot(v, d_own, NT)
                centre = r.centre[pair * 2 + side : pair * 2 + side + 1, rows]
                dscore = (probs * (dprob - centre)).astype(jnp.bfloat16)
                r.dv[0:end] = r.dv[0:end] + dot(probs.astype(jnp.bfloat16), d_own, NN)
                r.dk[0:end] = r.dk[0:end] + dot(dscore, q_own, NN)
                dq = dq + dot(dscore, k * eighth, TN)
            r.dqkv[0, rows, lanes] = dq.astype(jnp.bfloat16)
        if turn == 1:
            r.dqkv[1, :, lanes] = r.dk[...].astype(jnp.bfloat16)
            r.dqkv[2, :, lanes] = r.dv[...].astype(jnp.bfloat16)

    def small_swap(self, step):
        r = self.refs
        z = self.z
        to = (
            self.dp + self.step_x,
            self.dp + self.step_y,
            self.dp + 4 - 8 * lax.rem(z, 2),
            self.dp + 8 - 16 * lax.div(z, 2),
        )[step]
        return self.copy(
            r.small, r.small_in.at[step], r.small_s.at[step], r.small_r.at[step], (to, self.core)
        )

    def small_stage(self, step):
        if step > 0:
            copy = self.small_swap(step - 1)
            copy.wait_send()
            copy.wait_recv()
            self.refs.small[...] = self.refs.small[...] + self.refs.small_in[step - 1]
        if step < 4:
            self.small_swap(step).start()

    def run(self):
        r = self.refs
        pltpu.make_async_copy(self.cotangent, r.low, r.cot_s).start()
        self.fetch(ACT, 1)
        r.small[...] = jnp.zeros(r.small.shape, jnp.float32)
        far = (self.dp + 8 - 16 * lax.div(self.z, 2), self.core)
        self.barrier(((self.dp, 1 - self.core), far))

        def step(t, carry):
            l = 1 - lax.div(t, PIECES)
            for p in range(PIECES):
                @pl.when((lax.rem(t, PIECES) == p) & (t < 2 * PIECES))
                def _():
                    self.piece(p, l)

            for s in range(5):
                @pl.when(t == 2 * PIECES + s)
                def _():
                    self.small_stage(s)

            self.tick(t)
            return carry

        lax.fori_loop(0, self.ticks, step, 0)
        pltpu.make_async_copy(r.low, self.grad_tokens, r.tokens_s).wait()
        self.small_out[...] = r.small[...]


def backward(kept, weights, gain, lse, positions, cotangent, slots=6, lags=(2, 1, 1, 1, 1, 1, 1, 1, 3)):
    D = cotangent.shape[1]
    _, T, W = kept[1].shape
    jobs = 2 * PER_LAYER
    plan = Backward(2 * jobs, UNIT // 2, UNIT, slots, lags)
    plan.T, plan.D, plan.W, plan.F = T, D, W, weights[0].shape[1]
    scratch = plan.scratch() | plan.more_scratch()
    n = len(kept)

    def kernel(*refs):
        layers = [[ref.at[i] for i in range(2)] for ref in refs[:n]]
        norm1, q, k, v, att, h_mid, norm2, pre, act, h = layers
        plan.inputs = dict(zip(plan.LOADS, (act, pre, list(zip(norm1, norm2)), list(zip(h, h_mid)), att, q, k, v)))
        for name, weight in zip((W_SHRINK, W_EXPAND, W_MERGE, W_HEADS), refs[n : n + 4]):
            plan.inputs[name] = [weight.at[i] for i in range(2)]
        plan.cotangent, plan.gain, plan.lse, plan.positions = refs[n + 4 : n + 8]
        plan.target, plan.source, plan.grad_tokens, plan.small_out = refs[n + 8 : n + 12]
        plan.setup(SimpleNamespace(**dict(zip(scratch, refs[n + 12 :]))))
        plan.run()

    hbm = pl.BlockSpec(memory_space=pl.ANY)
    vmem = pl.BlockSpec(memory_space=pltpu.VMEM)
    flat = jax.ShapeDtypeStruct((jobs, 2, UNIT, UNIT), jnp.float32)
    target, _, grad_tokens, small = pl.pallas_call(
        kernel,
        out_shape=(
            flat,
            flat,
            jax.ShapeDtypeStruct((T, D), jnp.bfloat16),
            jax.ShapeDtypeStruct((2 * SMALL, D), jnp.float32),
        ),
        in_specs=[hbm] * (n + 5) + [vmem] * 3,
        out_specs=(hbm, hbm, hbm, vmem),
        scratch_shapes=list(scratch.values()),
        compiler_params=pltpu.CompilerParams(
            collective_id=0, has_side_effects=True, vmem_limit_bytes=61 * 2**20
        ),
    )(*kept, *weights, cotangent, gain, lse, positions)
    return target, grad_tokens, small


def gelu(x):
    return 0.5 * x * (1.0 + jnp.tanh(0.7978845608028654 * (x + 0.044715 * x * x * x)))


class Forward:
    KEPT = (NORM1, Q, K, V, ATT, H_MID, NORM2, PRE, ACT, H)

    WEIGHTS = (HEADS, MERGE, EXPAND, SHRINK)

    def scratch(self):
        T, D, W, F = self.T, self.D, self.W, self.F
        low, full = jnp.bfloat16, jnp.float32
        dma = pltpu.SemaphoreType.DMA
        n = T // ROWS
        return dict(
            norm1=pltpu.VMEM((T, D), low), q=pltpu.VMEM((T, W), low), k=pltpu.VMEM((T, W), low), v=pltpu.VMEM((T, W), low),
            att=pltpu.VMEM((T, W), low), h_mid=pltpu.VMEM((T, D), full), norm2=pltpu.VMEM((T, D), low),
            pre=pltpu.VMEM((T, F), full), act=pltpu.VMEM((T, F), low), h=pltpu.VMEM((T, D), full),
            low=pltpu.VMEM((T, D), low), part=pltpu.VMEM((2, T, D), full), came=pltpu.VMEM((2, T, D), full),
            bias=pltpu.VMEM((n, ROWS, T), full),
            heads=pltpu.VMEM((2, 3, D, W), low), merge=pltpu.VMEM((2, W, D), low),
            expand=pltpu.VMEM((2, D, F), low), shrink=pltpu.VMEM((2, F, D), low),
            kept_s=dma((len(self.KEPT), n)), weight_s=dma((4, 2)), token_s=dma, out_s=dma((n,)),
            core_s=dma((2, n)), core_r=dma((2, n)),
        )

    def rows(self, b):
        return pl.ds(pl.multiple_of(b * ROWS, ROWS), ROWS)

    def keep_copy(self, name, l, b):
        at = self.rows(b)
        return pltpu.make_async_copy(
            getattr(self.refs, name).at[at], self.kept[name].at[l, at], self.refs.kept_s.at[self.KEPT.index(name), b]
        )

    def free(self, l, b, *names):
        @pl.when(l == 1)
        def _():
            for name in names:
                self.keep_copy(name, 0, b).wait()

    def keep(self, l, b, *names):
        for name in names:
            self.keep_copy(name, l, b).start()

    def weight_copy(self, name, l):
        at = self.WEIGHTS.index(name)
        return pltpu.make_async_copy(self.weights[name].at[l], getattr(self.refs, name).at[l], self.refs.weight_s.at[at, l])

    def core_copy(self, kind, b):
        r, at = self.refs, self.rows(b)
        return pltpu.make_async_remote_copy(
            src_ref=r.part.at[kind, at], dst_ref=r.came.at[kind, at],
            send_sem=r.core_s.at[kind, b], recv_sem=r.core_r.at[kind, b],
            device_id=(lax.axis_index("dp"), 1 - lax.axis_index("tensor")), device_id_type=MESH,
        )

    def summed(self, kind, b):
        copy = self.core_copy(kind, b)
        copy.wait_send()
        copy.wait_recv()
        at = self.rows(b)
        return self.refs.part[kind, at] + self.refs.came[kind, at]

    def norm(self, x, l, which):
        xhat, _ = norm_parts(x)
        return (xhat * self.gain[l, which : which + 1] + self.shift[l, which : which + 1]).astype(jnp.bfloat16)

    def before_first(self, l, b):
        r, at = self.refs, self.rows(b)
        self.free(l, b, H, NORM1, Q, K, V)

        @pl.when(l == 0)
        def _():
            r.h[at] = r.low[at].astype(jnp.float32)

        @pl.when(l == 1)
        def _():
            r.h[at] = r.h_mid[at] + (self.summed(1, b) + self.branch[0, 1:2])

    def first(self, l, b):
        r, at = self.refs, self.rows(b)
        low = self.norm(r.h[at], l, 0)
        r.norm1[at] = low
        r.q[at] = (dot(low, r.heads[l, 0], NN) + self.offsets[l, 0:1]).astype(jnp.bfloat16)
        r.k[at] = dot(low, r.heads[l, 1], NN).astype(jnp.bfloat16)
        r.v[at] = (dot(low, r.heads[l, 2], NN) + self.offsets[l, 1:2]).astype(jnp.bfloat16)

    def after_first(self, l, b):
        self.keep(l, b, H, NORM1, Q, K, V)

    def mix(self, l, b):
        r, at = self.refs, self.rows(b)
        self.free(l, b, ATT)
        for i in range(self.T // ROWS):
            @pl.when(b == i)
            def _():
                self.attend(l, i)

        r.part[0, at] = dot(r.att[at], r.merge[l], NN)
        self.core_copy(0, b).start()
        self.keep(l, b, ATT)

    def attend(self, l, b):
        r = self.refs
        rows, end = slice(b * ROWS, (b + 1) * ROWS), (b + 1) * ROWS

        @pl.when(l == 0)
        def _():
            query = b * ROWS + lax.broadcasted_iota(jnp.int32, (ROWS, 1), 0)
            spread = jnp.concatenate([self.positions[...].astype(jnp.float32)] * 16, axis=0).T
            column = jnp.concatenate([spread[:, j : j + 1] for j in range(2 * b, 2 * b + 2)], axis=0)
            lowest = query - column.astype(jnp.int32)
            key = lax.broadcasted_iota(jnp.int32, (ROWS, end), 1)
            r.bias[b, :, 0:end] = jnp.where((key <= query) & (key >= lowest), 0.0, -1e30)

        lane = lax.broadcasted_iota(jnp.int32, (1, 128), 1)
        logs = jnp.zeros((ROWS, 128), jnp.float32)
        for pair in range(self.W // 128):
            lanes = slice(pair * 128, (pair + 1) * 128)
            q, k, v = r.q[rows, lanes], r.k[0:end, lanes], r.v[0:end, lanes]
            total = jnp.zeros((ROWS, 128), jnp.float32)
            for side in range(2):
                mine = (lax.div(lane, 64) == side).astype(jnp.float32)
                scores = dot(q * (mine * 0.125).astype(jnp.bfloat16), k, NT) + r.bias[b, :, 0:end]
                highest = jnp.max(scores, axis=-1, keepdims=True)
                weights = jnp.exp(scores - highest)
                amount = jnp.sum(weights, axis=-1, keepdims=True)
                probs = (weights * (1.0 / amount)).astype(jnp.bfloat16)
                total = total + dot(probs, v * mine.astype(jnp.bfloat16), NN)
                logs = jnp.where(lane == pair * 2 + side, highest + jnp.log(amount), logs)
            r.att[rows, lanes] = total.astype(jnp.bfloat16)
        self.lse[l, :, rows] = logs.T[0:8]

    def before_second(self, l, b):
        self.free(l, b, H_MID, NORM2, PRE, ACT)
        copy = self.core_copy(0, b)
        copy.wait_send()
        copy.wait_recv()

    def second(self, l, b):
        r, at = self.refs, self.rows(b)
        middle = r.h[at] + (r.part[0, at] + r.came[0, at] + self.branch[l, 0:1])
        r.h_mid[at] = middle
        low = self.norm(middle, l, 1)
        r.norm2[at] = low
        for c in range(0, self.F, 512):
            pre = dot(low, r.expand[l, :, c : c + 512], NN) + self.hidden[pl.ds(l, 1), c : c + 512]
            r.pre[at, c : c + 512] = pre
            r.act[at, c : c + 512] = gelu(pre).astype(jnp.bfloat16)
        r.part[1, at] = dot(r.act[at], r.shrink[l], NN)

    def after_second(self, l, b):
        self.core_copy(1, b).start()
        self.keep(l, b, H_MID, NORM2, PRE, ACT)

    def finish(self, b):
        r, at = self.refs, self.rows(b)
        r.low[at] = (r.h_mid[at] + (self.summed(1, b) + self.branch[1, 1:2])).astype(jnp.bfloat16)
        pltpu.make_async_copy(r.low.at[at], self.output.at[at], r.out_s.at[b]).start()

    def run(self):
        r = self.refs
        n = self.T // ROWS
        load = pltpu.make_async_copy(self.tokens, r.low, r.token_s)
        load.start()
        for name in self.WEIGHTS:
            self.weight_copy(name, 0).start()
        other = (lax.axis_index("dp"), 1 - lax.axis_index("tensor"))
        bar = pltpu.get_barrier_semaphore()
        pl.semaphore_signal(bar, inc=1, device_id=other, device_id_type=MESH)
        pl.semaphore_wait(bar, 1)
        load.wait()

        self.weight_copy(HEADS, 0).wait()
        self.before_first(0, 0)
        self.first(0, 0)
        self.after_first(0, 0)

        def turn(t, carry):
            for l in range(2):
                @pl.when(t == l * n)
                def _():
                    self.weight_copy(MERGE, l).wait()

            @pl.when(t < 2 * n)
            def _():
                self.mix(lax.div(t, n), lax.rem(t, n))

            for l in range(2):
                @pl.when(t == l * n + 1)
                def _():
                    self.weight_copy(EXPAND, l).wait()
                    self.weight_copy(SHRINK, l).wait()

            @pl.when(t == 1)
            def _():
                for name in self.WEIGHTS:
                    self.weight_copy(name, 1).start()

            @pl.when(t == n - 1)
            def _():
                self.weight_copy(HEADS, 1).wait()

            old, new = t - 1, t + 1
            goes = (new < 2 * n, lax.div(new, n), lax.rem(new, n))
            comes = ((old >= 0) & (old < 2 * n), lax.div(old, n), lax.rem(old, n))

            @pl.when(comes[0])
            def _():
                self.before_second(*comes[1:])

            @pl.when(goes[0])
            def _():
                self.before_first(*goes[1:])

            @pl.when(comes[0] & goes[0])
            def _():
                self.second(*comes[1:])
                self.first(*goes[1:])

            @pl.when(comes[0] & jnp.logical_not(goes[0]))
            def _():
                self.second(*comes[1:])

            @pl.when(goes[0] & jnp.logical_not(comes[0]))
            def _():
                self.first(*goes[1:])

            @pl.when(comes[0])
            def _():
                self.after_second(*comes[1:])

            @pl.when(goes[0])
            def _():
                self.after_first(*goes[1:])

            @pl.when(t >= n + 2)
            def _():
                self.finish(t - n - 2)

            return carry

        lax.fori_loop(0, 2 * n + 2, turn, 0)
        for b in range(n):
            for name in self.KEPT:
                self.keep_copy(name, 1, b).wait()
            pltpu.make_async_copy(r.low.at[self.rows(b)], self.output.at[self.rows(b)], r.out_s.at[b]).wait()


def forward(tokens, positions, weights, rows):
    plan = Forward()
    T, D = tokens.shape
    plan.T, plan.D, plan.W, plan.F = T, D, weights[0].shape[3], weights[2].shape[2]
    scratch = plan.scratch()
    kinds = plan.KEPT

    def kernel(tokens, heads, merge, expand, shrink, positions, gain, shift, offsets, branch, hidden, output, lse, *refs):
        plan.tokens, plan.positions, plan.output, plan.lse = tokens, positions, output, lse
        plan.weights = dict(zip(plan.WEIGHTS, (heads, merge, expand, shrink)))
        plan.gain, plan.shift, plan.offsets, plan.branch, plan.hidden = gain, shift, offsets, branch, hidden
        plan.kept = dict(zip(kinds, refs))
        plan.refs = SimpleNamespace(**dict(zip(scratch, refs[len(kinds) :])))
        plan.run()

    hbm = pl.BlockSpec(memory_space=pl.ANY)
    vmem = pl.BlockSpec(memory_space=pltpu.VMEM)
    kept_shapes = [jax.ShapeDtypeStruct((2,) + scratch[name].shape, scratch[name].dtype) for name in kinds]
    out = pl.pallas_call(
        kernel,
        out_shape=[jax.ShapeDtypeStruct((T, D), jnp.bfloat16), jax.ShapeDtypeStruct((2, 8, T), jnp.float32)] + kept_shapes,
        in_specs=[hbm] * 5 + [vmem] * 6,
        out_specs=[hbm, vmem] + [hbm] * len(kept_shapes),
        scratch_shapes=list(scratch.values()),
        compiler_params=pltpu.CompilerParams(
            collective_id=1, has_side_effects=True, vmem_limit_bytes=61 * 2**20
        ),
    )(tokens, *weights, positions, *rows)
    return out[0], out[1], out[2:]


def spread(flat, small, shapes, dtype=jnp.float32):
    half = flat.shape[0] // 2
    width = small.shape[1]

    def kernel(source, sums, gain, shift, heads, offsets, merge, branch, expand, hidden, shrink, held, into, out):
        loads, copies = [], []

        def put(g, u, target):
            i = len(copies)
            loads.append(pltpu.make_async_copy(source.at[g, u], held.at[i], into.at[i]))
            copies.append(pltpu.make_async_copy(held.at[i], target, out.at[i]))
            loads[-1].start()

        for l in range(2):
            base = (1 - l) * half
            for u in range(2):
                rows = pl.ds(u * UNIT, UNIT)
                for i in range(4):
                    at = pl.ds((i // 2) * 2 * UNIT + u * UNIT, UNIT)
                    put(base + i, u, shrink.at[l, at, pl.ds((i % 2) * UNIT, UNIT)])
                    put(base + 4 + i, u, expand.at[l, rows, pl.ds(i * UNIT, UNIT)])
                put(base + 8, u, merge.at[l, :, rows])
                for c in range(3):
                    put(base + 9 + c, u, heads.at[l, c, rows])
            for target, at in ((gain, GAIN), (shift, SHIFT), (branch, BRANCH)):
                target[l] = sums[l * SMALL + at : l * SMALL + at + 2]
            for i in range(2):
                at = l * SMALL + HIDDEN + i
                hidden[l : l + 1, i * width : (i + 1) * width] = sums[at : at + 1]
                at = l * SMALL + OFFSETS
                offsets[l, i : i + 1] = sums[at : at + 1, i * UNIT : (i + 1) * UNIT]
        for load, copy in zip(loads, copies):
            load.wait()
            copy.start()
        for copy in copies:
            copy.wait()

    hbm = pl.BlockSpec(memory_space=pl.ANY)
    vmem = pl.BlockSpec(memory_space=pltpu.VMEM)
    return pl.pallas_call(
        kernel,
        out_shape=[jax.ShapeDtypeStruct(s, dtype) for s in shapes],
        in_specs=[hbm, vmem],
        out_specs=[vmem, vmem, hbm, vmem, hbm, vmem, hbm, vmem, hbm],
        scratch_shapes=[
            pltpu.VMEM((2 * flat.shape[0], UNIT, UNIT), dtype),
            pltpu.SemaphoreType.DMA((2 * flat.shape[0],)),
            pltpu.SemaphoreType.DMA((2 * flat.shape[0],)),
        ],
        compiler_params=pltpu.CompilerParams(has_side_effects=True, vmem_limit_bytes=48 * 2**20),
    )(flat, small)


def on_device(
    tokens,
    positions,
    norm_gain,
    norm_shift,
    heads_weight,
    offsets,
    merge_weight,
    branch_bias,
    expand_weight,
    hidden_bias,
    shrink_weight,
    cotangent,
):
    rows = (norm_gain, norm_shift, offsets, branch_bias, hidden_bias)
    places = positions.reshape(-1, 128)
    output, lse, kept = forward(
        tokens, places, (heads_weight, merge_weight, expand_weight, shrink_weight), rows
    )
    flat, grad_tokens, small = backward(
        kept, (shrink_weight, expand_weight, merge_weight, heads_weight), norm_gain, lse, places, cotangent
    )
    ranks = lax.axis_size("dp")
    if ranks > BLOCK:
        groups = [[j * BLOCK + i for j in range(ranks // BLOCK)] for i in range(BLOCK)]
        flat, small = lax.psum((flat, small), "dp", axis_index_groups=groups)
    shapes = [norm_gain, norm_shift, heads_weight, offsets, merge_weight, branch_bias, expand_weight, hidden_bias, shrink_weight]
    return (output, grad_tokens, *spread(flat, small, [like.shape for like in shapes]))


def solution(mesh):
    placed = (
        P("dp", None),
        P("dp"),
        P(),
        P(),
        P(None, None, None, "tensor"),
        P(None, None, "tensor"),
        P(None, "tensor", None),
        P(),
        P(None, None, "tensor"),
        P(None, "tensor"),
        P(None, "tensor", None),
        P("dp", None),
    )
    return jax.shard_map(
        on_device,
        mesh=mesh,
        in_specs=placed,
        out_specs=(
            P("dp", None),
            P("dp", None),
            P(),
            P(),
            P(None, None, None, "tensor"),
            P(None, None, "tensor"),
            P(None, "tensor", None),
            P(),
            P(None, None, "tensor"),
            P(None, "tensor"),
            P(None, "tensor", None),
        ),
        check_vma=False,
    )
```
